128 devices in a mesh: tok: 16 (over y, x_hi, core), hid: 8 (over z, x_lo).
Axes of the slice: x: 4 (x_hi: 2, x_lo: 2; x = x_hi * 2 + x_lo), y: 4, z: 4, core: 2. Of those that a mesh axis runs over, the one named last changes fastest.
Arguments:
- tokens: bfloat16 [24576, 1024], P(('tok', 'hid')), may hold values from -6 to 6
- memory: bfloat16 [49152, 1024], P(('tok', 'hid')), may hold values from -6 to 6
- cotangent: bfloat16 [24576, 1024], P(('tok', 'hid'))
- norm1: bfloat16 [1024], P('tok'), may hold values from 0.25 to 1.75
- w_query: bfloat16 [1024, 1024], P('tok', 'hid'), may hold values from -0.046875 to 0.046875
- w_key: bfloat16 [1024, 512], P('tok', 'hid'), may hold values from -0.1875 to 0.1875
- w_value: bfloat16 [1024, 512], P('tok', 'hid'), may hold values from -0.1875 to 0.1875
- w_out: bfloat16 [1024, 1024], P('hid', 'tok'), may hold values from -0.75 to 0.75
- rel_bias: bfloat16 [32, 16], P('tok', 'hid'), may hold values from -4 to 4
- norm2: bfloat16 [1024], P('tok'), may hold values from 0.25 to 1.75
- cross_query: bfloat16 [1024, 1024], P('tok', 'hid'), may hold values from -0.046875 to 0.046875
- cross_key: bfloat16 [1024, 512], P('tok', 'hid'), may hold values from -0.1875 to 0.1875
- cross_value: bfloat16 [1024, 512], P('tok', 'hid'), may hold values from -0.1875 to 0.1875
- cross_out: bfloat16 [1024, 1024], P('hid', 'tok'), may hold values from -0.75 to 0.75
- norm3: bfloat16 [1024], P('tok'), may hold values from 0.25 to 1.75
- w_gate: bfloat16 [1024, 2816], P('tok', 'hid'), may hold values from -0.1875 to 0.1875
- w_up: bfloat16 [1024, 2816], P('tok', 'hid'), may hold values from -0.1875 to 0.1875
- w_down: bfloat16 [2816, 1024], P('hid', 'tok'), may hold values from -0.109375 to 0.109375
- doc_lengths: int32 [16, 3], P('tok'), may hold values from 1 to 1024, 1536 in all within a row
- memory_slot: int32 [16, 3], P('tok'), may hold values from 0 to 2, each once within a row
- enc_lengths: int32 [16, 3], P('tok'), may hold values from 512 to 1024
- rel_bucket: int32 [1536], replicated, may hold values from 0 to 31
Outputs:
- mixed: bfloat16 [24576, 1024], P(('tok', 'hid'))
- d_tokens: float32 [24576, 1024], P(('tok', 'hid'))
- d_memory: float32 [49152, 1024], P(('tok', 'hid'))
- d_norm1: float32 [1024], P('tok')
- d_w_query: float32 [1024, 1024], P('tok', 'hid')
- d_w_key: float32 [1024, 512], P('tok', 'hid')
- d_w_value: float32 [1024, 512], P('tok', 'hid')
- d_w_out: float32 [1024, 1024], P('hid', 'tok')
- d_rel_bias: float32 [32, 16], P('tok', 'hid')
- d_norm2: float32 [1024], P('tok')
- d_cross_query: float32 [1024, 1024], P('tok', 'hid')
- d_cross_key: float32 [1024, 512], P('tok', 'hid')
- d_cross_value: float32 [1024, 512], P('tok', 'hid')
- d_cross_out: float32 [1024, 1024], P('hid', 'tok')
- d_norm3: float32 [1024], P('tok')
- d_w_gate: float32 [1024, 2816], P('tok', 'hid')
- d_w_up: float32 [1024, 2816], P('tok', 'hid')
- d_w_down: float32 [2816, 1024], P('hid', 'tok')
The draws below stay inside these ranges and needn't reach their ends.
Inputs may be any that keep to these rules, and one draw needn't show every extreme that they name: `doc_lengths`: each row holds 3 document lengths that sum to 1536; the longest is exactly 1024. `memory_slot`: each row is a permutation of the group's 3 memories.
All inputs are finite; a program needn't handle non-finite values.
Results may differ from the reference program's by a relative error of at most 0.04.
Values may be sent and summed in bfloat16 or wider, within the bound.
A program may use at most 192 MiB of HBM per device.

```python
import math
import jax
import jax.numpy as jnp
import numpy as np
from jax import lax

D = 1024
HEADS = 16
HDIM = 64
GROUPS = 8
FF = 2816
NB = 32
TOK_G = 1536
LONG = 1024
ENC = 1024
DOCS = 3
MEMORY = 3072
TOKENS = 24576
N_TOK = 16


def draw_cotangent(key, part):
    key = jax.random.fold_in(key, 7)
    row_pos = jnp.arange(TOKENS, dtype=jnp.float32)[:, None] / max(TOKENS - 1, 1)
    scale = 3.0 ** row_pos
    base = jax.random.normal(key, (TOKENS, D), jnp.float32)
    return (base * scale).astype(jnp.bfloat16)


def touch_ends(values, key, low, top_value):
    spot = [jax.random.randint(jax.random.fold_in(key, axis), (), 0, length) for axis, length in enumerate(values.shape)]
    main_axis = values.shape.index(max(values.shape))
    neighbour = spot[:main_axis] + [(spot[main_axis] + 1) % values.shape[main_axis]] + spot[main_axis + 1:]
    return values.at[tuple(spot)].set(low).at[tuple(neighbour)].set(top_value)


def levels(own_key, dims, cuts, smallest, high):
    def one(axis_at, blocks):
        steps = jax.random.uniform(jax.random.fold_in(jax.random.fold_in(own_key, 6), axis_at), (blocks,), jnp.float32, smallest / len(cuts), high / len(cuts))
        return jnp.repeat(jnp.exp(steps), dims[axis_at] // blocks).reshape((-1,) + (1,) * (len(dims) - axis_at - 1))

    loudness = one(*cuts[0])
    for cut in cuts[1:]:
        loudness = loudness * one(*cut)
    return loudness


def length_profile(amount, total, bound, lean):
    portions = [(1 << 20) // math.isqrt(grade ** lean) + 1 for grade in range(2, amount + 1)]
    surplus, given = total - bound - (amount - 1), [1] * (amount - 1)
    while surplus > 0:
        candidates = [i for i in range(amount - 1) if given[i] < bound]
        whole, remaining = sum([portions[i] for i in candidates]), surplus
        for i in candidates:
            extra = min(bound - given[i], max(1, remaining * portions[i] // whole), surplus)
            given[i] = given[i] + extra
            surplus = surplus - extra
    return np.array([bound] + given)


def ragged(rng, amount, total, limit, slope):
    if amount == 2:
        one = jax.random.randint(rng, (), max(1, total - limit), min(limit, total - 1) + 1)
        return jnp.stack([one, total - one])
    sizes = jnp.asarray(length_profile(amount, total, limit, slope), jnp.int32)
    pairs = (amount - 1) // 2
    giver, sink = sizes[1:1 + 2 * pairs:2], sizes[2:2 + 2 * pairs:2]
    margin = jnp.minimum(giver - 1, limit - sink)
    shifted = jax.random.randint(jax.random.fold_in(rng, 1), (pairs,), 0, 1 << 20) % (margin + 1)
    sizes = sizes.at[1:1 + 2 * pairs:2].set(giver - shifted).at[2:2 + 2 * pairs:2].set(sink + shifted)
    return sizes[jax.random.permutation(jax.random.fold_in(rng, 2), amount)]


def noise(key, dims, spread, most, pieces=(), kind=jnp.bfloat16):
    array = jax.random.normal(key, dims, jnp.float32) * spread
    if len(pieces) > 0:
        array = levels(key, dims, pieces, -0.22, 0.18) * array
    return jnp.clip(array, min=-most, max=most).astype(kind)


def setup_inputs(seed: int = 0) -> dict:
    streams_of = jax.random.split(jax.random.key(seed), 23)
    return {
        "tokens": noise(streams_of[0], (TOKENS, D), 1.0, 6.0, ((0, 128),)),
        "memory": noise(streams_of[1], (N_TOK * MEMORY, D), 1.0, 6.0, ((0, 128),)),
        "cotangent": draw_cotangent(jax.random.fold_in(streams_of[22], 71), 0),
        "norm1": jnp.clip(1.0 + 0.15 * jax.random.normal(streams_of[3], (D,), jnp.float32), 0.25, 1.75).astype(jnp.bfloat16),
        "w_query": noise(streams_of[4], (D, HEADS * HDIM), (16 * D) ** -0.5, 0.046875, ((0, 16), (1, 8))),
        "w_key": noise(streams_of[5], (D, GROUPS * HDIM), D ** -0.5, 0.1875, ((0, 16), (1, 8))),
        "w_value": noise(streams_of[6], (D, GROUPS * HDIM), D ** -0.5, 0.1875, ((0, 16), (1, 8))),
        "w_out": noise(streams_of[7], (HEADS * HDIM, D), (HEADS * HDIM // 16) ** -0.5, 0.75, ((0, 8), (1, 16))),
        "rel_bias": noise(streams_of[8], (NB, HEADS), 1.0, 4.0, ((0, 16), (1, 8))),
        "norm2": jnp.clip(1.0 + 0.15 * jax.random.normal(streams_of[9], (D,), jnp.float32), 0.25, 1.75).astype(jnp.bfloat16),
        "cross_query": noise(streams_of[10], (D, HEADS * HDIM), (16 * D) ** -0.5, 0.046875, ((0, 16), (1, 8))),
        "cross_key": noise(streams_of[11], (D, GROUPS * HDIM), D ** -0.5, 0.1875, ((0, 16), (1, 8))),
        "cross_value": noise(streams_of[12], (D, GROUPS * HDIM), D ** -0.5, 0.1875, ((0, 16), (1, 8))),
        "cross_out": noise(streams_of[13], (HEADS * HDIM, D), (HEADS * HDIM // 16) ** -0.5, 0.75, ((0, 8), (1, 16))),
        "norm3": jnp.clip(1.0 + 0.15 * jax.random.normal(streams_of[14], (D,), jnp.float32), 0.25, 1.75).astype(jnp.bfloat16),
        "w_gate": noise(streams_of[15], (D, FF), D ** -0.5, 0.1875, ((0, 16), (1, 8))),
        "w_up": noise(streams_of[16], (D, FF), D ** -0.5, 0.1875, ((0, 16), (1, 8))),
        "w_down": noise(streams_of[17], (FF, D), FF ** -0.5, 0.109375, ((0, 8), (1, 16))),
        "doc_lengths": jax.vmap(lambda own: ragged(own, DOCS, TOK_G, LONG, 2))(jax.random.split(streams_of[18], N_TOK)).reshape((N_TOK, DOCS)).astype(jnp.int32),
        "memory_slot": jax.vmap(lambda own: jax.random.permutation(own, DOCS))(jax.random.split(streams_of[19], N_TOK)).reshape((N_TOK, DOCS)).astype(jnp.int32),
        "enc_lengths": touch_ends(jax.random.randint(streams_of[20], (N_TOK, DOCS), ENC // 2, ENC + 1), jax.random.fold_in(streams_of[20], 1), ENC // 2, ENC).astype(jnp.int32),
        "rel_bucket": touch_ends(jax.random.randint(streams_of[21], (TOK_G,), 0, NB), jax.random.fold_in(streams_of[21], 1), 0, NB - 1).astype(jnp.int32),
    }


EPS = 1e-06
HIGH = lax.Precision.HIGHEST

@jax.custom_vjp
def low(v):
    return lax.optimization_barrier(v.astype(jnp.bfloat16)).astype(jnp.float32)

@jax.custom_vjp
def low_back(v):
    return v

def low_keep(v):
    return (low(v), None)

def low_pass(kept, grad):
    return (grad,)

def back_keep(v):
    return (v, None)

def back_low(kept, grad):
    return (low(grad),)
low.defvjp(low_keep, low_pass)
low_back.defvjp(back_keep, back_low)

def product(first_mat, second_mat):
    return jnp.dot(first_mat, second_mat, precision=HIGH, preferred_element_type=jnp.float32)

def rms_norm(row_vals, gain_vec):
    return row_vals * lax.rsqrt(lax.optimization_barrier(jnp.mean(row_vals * row_vals, axis=-1, keepdims=True)) + EPS) * gain_vec

def masked_softmax(scores, allowed):
    scores = jnp.where(allowed, scores, -1e+30)
    largest = lax.optimization_barrier(jnp.max(scores, axis=-1, keepdims=True))
    exponent = jnp.exp(scores - largest)
    return exponent / lax.optimization_barrier(jnp.sum(exponent, axis=-1, keepdims=True))

def doc_index(doc_lens, row_count):
    ends = jnp.cumsum(doc_lens)
    positions = jnp.arange(row_count, dtype=jnp.int32)
    return lax.optimization_barrier(jnp.sum((positions[:, None] >= ends[None, :]).astype(jnp.int32), axis=1))

def split_heads(flat_rows, head_count):
    return flat_rows.reshape(flat_rows.shape[0], head_count, HDIM).transpose(1, 0, 2)

def attention(queries, key_heads, value_heads, bias_of, mask_of):
    ratio = HEADS // GROUPS
    key_heads = jnp.repeat(key_heads, ratio, axis=0)
    value_heads = jnp.repeat(value_heads, ratio, axis=0)
    block_rows = min(512, TOK_G)

    def one_block(which_block):
        first_row = which_block * block_rows
        q_block = lax.dynamic_slice_in_dim(queries, first_row, block_rows, 1)
        scores = jnp.einsum('hqd,hkd->hqk', q_block, key_heads, precision=HIGH) + bias_of(first_row)
        weights_soft = low(masked_softmax(low_back(scores), mask_of(first_row)))
        return jnp.einsum('hqk,hkd->hqd', weights_soft, value_heads, precision=HIGH)
    outputs = lax.map(jax.checkpoint(one_block), jnp.arange(TOK_G // block_rows, dtype=jnp.int32))
    return outputs.transpose(0, 2, 1, 3).reshape(TOK_G, HEADS * HDIM)

def group_forward(residual, encoded, norm1, w_query, w_key, w_value, w_out, rel_bias, norm2, cross_query, cross_key, cross_value, cross_out, norm3, w_gate, w_up, w_down, doc_lens, slots, memory_lens, rel_bucket):
    block_rows = min(512, TOK_G)
    positions = jnp.arange(TOK_G, dtype=jnp.int32)
    doc_of = doc_index(doc_lens, TOK_G)
    key_slots = jnp.arange(MEMORY, dtype=jnp.int32)
    memory_id = key_slots // ENC
    key_valid = key_slots % ENC < memory_lens[memory_id]
    wanted = slots[doc_of]

    def self_bias(first_row):
        row_ids = first_row + jnp.arange(block_rows, dtype=jnp.int32)
        distance = jnp.clip(row_ids[:, None] - positions[None, :], 0, TOK_G - 1)
        return rel_bias[rel_bucket[distance]].transpose(2, 0, 1)

    def self_mask(first_row):
        row_ids = first_row + jnp.arange(block_rows, dtype=jnp.int32)
        own_doc = lax.dynamic_slice_in_dim(doc_of, first_row, block_rows)
        return ((row_ids[:, None] >= positions[None, :]) & (own_doc[:, None] == doc_of[None, :]))[None]

    def cross_mask(first_row):
        own_want = lax.dynamic_slice_in_dim(wanted, first_row, block_rows)
        return ((own_want[:, None] == memory_id[None, :]) & key_valid[None, :])[None]

    def no_bias(first_row):
        return jnp.zeros((), jnp.float32)
    h_one = low(rms_norm(residual, norm1))
    queries = split_heads(low_back(low(product(h_one, w_query))), HEADS)
    key_heads = split_heads(low_back(low(product(h_one, w_key))), GROUPS)
    value_heads = split_heads(low_back(low(product(h_one, w_value))), GROUPS)
    attended = low_back(low(attention(queries, key_heads, value_heads, self_bias, self_mask)))
    x_one = residual + low_back(product(attended, w_out))
    h_two = low(rms_norm(x_one, norm2))
    queries = split_heads(low_back(low(product(h_two, cross_query))), HEADS)
    key_heads = split_heads(low_back(low(product(encoded, cross_key))), GROUPS)
    value_heads = split_heads(low_back(low(product(encoded, cross_value))), GROUPS)
    attended = low_back(low(attention(queries, key_heads, value_heads, no_bias, cross_mask)))
    x_two = x_one + low_back(product(attended, cross_out))
    h_three = low(rms_norm(x_two, norm3))
    gate_vals = low_back(product(h_three, w_gate))
    up_vals = low_back(product(h_three, w_up))
    hidden = low(jax.nn.gelu(gate_vals, approximate=True) * up_vals)
    return x_two + low_back(product(hidden, w_down))

def reference(tokens, memory, cotangent, norm1, w_query, w_key, w_value, w_out, rel_bias, norm2, cross_query, cross_key, cross_value, cross_out, norm3, w_gate, w_up, w_down, doc_lengths, memory_slot, enc_lengths, rel_bucket):
    weights = tuple((w.astype(jnp.float32) for w in (norm1, w_query, w_key, w_value, w_out, rel_bias, norm2, cross_query, cross_key, cross_value, cross_out, norm3, w_gate, w_up, w_down)))
    rows_all = tokens.astype(jnp.float32).reshape(N_TOK, TOK_G, D)
    memory_all = memory.astype(jnp.float32).reshape(N_TOK, MEMORY, D)
    cot_all = cotangent.astype(jnp.float32).reshape(N_TOK, TOK_G, D)

    def step(totals, item):
        residual, encoded, cot_rows, doc_lens, slots, memory_lens = item

        def forward(res_in, enc_in, *params):
            return group_forward(res_in, enc_in, *params, doc_lens, slots, memory_lens, rel_bucket)
        output_rows, pullback = jax.vjp(forward, residual, encoded, *weights)
        grads = pullback(cot_rows)
        totals = tuple((t + g for t, g in zip(totals, grads[2:])))
        return (totals, (output_rows.astype(jnp.bfloat16), grads[0], grads[1]))
    start_totals = tuple((jnp.zeros(w.shape, jnp.float32) for w in weights))
    totals, (outputs, d_rows, d_enc) = lax.scan(step, start_totals, (rows_all, memory_all, cot_all, doc_lengths, memory_slot, enc_lengths))
    return (outputs.reshape(TOKENS, D), d_rows.reshape(TOKENS, D), d_enc.reshape(N_TOK * MEMORY, D), totals[0], totals[1], totals[2], totals[3], totals[4], totals[5], totals[6], totals[7], totals[8], totals[9], totals[10], totals[11], totals[12], totals[13], totals[14])
```

```python
import jax
import jax.numpy as jnp
from jax import lax
from jax.experimental import pallas as pl
from jax.experimental.pallas import tpu as pltpu
from jax.sharding import PartitionSpec as P

EPS = 1e-06
HIGH = lax.Precision.HIGHEST
MESH = pl.DeviceIdType.MESH

HDIM = 64
ENC = 1024
FLOAT = jnp.float32
HALF = jnp.bfloat16
TILE = 256
PAIR = 2 * TILE
NEG = -1e30
NT_DIMS = (((1,), (1,)), ((), ()))


def dot(first, second):
    return jnp.dot(first, second, preferred_element_type=FLOAT)


def dot_nt(first, second):
    return lax.dot_general(first, second, NT_DIMS, preferred_element_type=FLOAT)


def stack_heads(block):
    return jnp.concatenate([block[:, :HDIM], block[:, HDIM:]], axis=0)


def unstack_heads(columns):
    return jnp.concatenate(
        [columns[:, :TILE].T, columns[:, TILE:].T], axis=1
    )


def tile_rows(tile):
    return pl.ds(pl.multiple_of(tile * TILE, TILE), TILE)


def lane_positions(first):
    lane = lax.broadcasted_iota(jnp.int32, (1, PAIR), 1)
    return first + jnp.where(lane >= TILE, lane - TILE, lane)


def doc_ends(len_ref):
    first_end = len_ref[0, 0]
    return first_end, first_end + len_ref[0, 1]


def start_of(position, ends):
    return jnp.where(position >= ends[1], ends[1], jnp.where(position >= ends[0], ends[0], 0))


def build_bias(win_ref, bias, tiles):
    for diag in range(tiles):
        for head in range(2):
            row = win_ref[pl.ds(diag * 2 + head, 1), :]
            spread = jnp.broadcast_to(row, (TILE, PAIR))
            rolled = pltpu.roll(spread, 0, 1, stride=1, stride_axis=0)
            bias[diag, :, pl.ds(head * TILE, TILE)] = rolled[:, :TILE]


def online(state, scores, values_t):
    peak, total, acc = state
    new_peak = jnp.maximum(peak, jnp.max(scores, axis=0, keepdims=True))
    shrink = jnp.exp(peak - new_peak)
    weights = jnp.exp(scores - new_peak)
    total = total * shrink + jnp.sum(weights, axis=0, keepdims=True)
    acc = acc * shrink + dot(values_t, weights.astype(HALF))
    return new_peak, total, acc


def fresh_state():
    return (
        jnp.full((1, PAIR), NEG, FLOAT),
        jnp.zeros((1, PAIR), FLOAT),
        jnp.zeros((HDIM, PAIR), FLOAT),
    )


def finish(state, tile, out_ref, lse_ref):
    peak, total, acc = state
    out_ref[tile_rows(tile), :] = unstack_heads(acc / total).astype(HALF)
    lse_ref[pl.ds(tile, 1), :] = peak + jnp.log(total)


def self_forward_kernel(len_ref, qkv_ref, win_ref, out_ref, lse_ref, keys, values_t, bias):
    tiles = qkv_ref.shape[0] // TILE
    build_bias(win_ref, bias, tiles)
    for tile in range(tiles):
        block = qkv_ref[tile * TILE : (tile + 1) * TILE, 128:256]
        keys[tile] = block[:, :HDIM]
        values_t[tile] = block[:, HDIM:].astype(FLOAT).T.astype(HALF)
    ends = doc_ends(len_ref)

    @pl.loop(0, tiles)
    def row_tile(tile):
        first = tile * TILE
        queries = stack_heads(qkv_ref[tile_rows(tile), 0:128])
        row_pos = lane_positions(first)
        row_start = start_of(row_pos, ends)
        low = start_of(first, ends) // TILE

        def key_tile(other, state):
            scores = dot_nt(keys[other], queries) + bias[tile - other]
            key_pos = other * TILE + lax.broadcasted_iota(jnp.int32, (TILE, 1), 0)
            allowed = (key_pos <= row_pos) & (key_pos >= row_start)
            scores = jnp.where(allowed, scores, NEG)
            return online(state, scores, values_t[other])

        finish(lax.fori_loop(low, tile + 1, key_tile, fresh_state()), tile, out_ref, lse_ref)


def self_forward(doc_lens, qkv, windows):
    rows = qkv.shape[0]
    tiles = rows // TILE
    return pl.pallas_call(
        self_forward_kernel,
        out_shape=(
            jax.ShapeDtypeStruct((rows, 128), HALF),
            jax.ShapeDtypeStruct((8, PAIR), FLOAT),
        ),
        in_specs=[
            pl.BlockSpec(memory_space=pltpu.SMEM),
            pl.BlockSpec(memory_space=pltpu.VMEM),
            pl.BlockSpec(memory_space=pltpu.VMEM),
        ],
        out_specs=(pl.BlockSpec(memory_space=pltpu.VMEM),) * 2,
        scratch_shapes=[
            pltpu.VMEM((tiles, TILE, HDIM), HALF),
            pltpu.VMEM((tiles, HDIM, TILE), HALF),
            pltpu.VMEM((tiles, TILE, PAIR), FLOAT),
        ],
        compiler_params=pltpu.CompilerParams(vmem_limit_bytes=48 * 2**20),
    )(doc_lens, qkv, windows)


def row_prepare(tiles, q_of, do_ref, o_ref, queries, grads, deltas):
    for tile in range(tiles):
        rows = slice(tile * TILE, (tile + 1) * TILE)
        queries[tile] = stack_heads(q_of(rows))
        block = do_ref[rows, :]
        grads[tile] = stack_heads(block)
        product = (block.astype(FLOAT) * o_ref[rows, :].astype(FLOAT)).T
        deltas[tile] = jnp.concatenate(
            [
                jnp.sum(product[:HDIM], axis=0, keepdims=True),
                jnp.sum(product[HDIM:], axis=0, keepdims=True),
            ],
            axis=1,
        )


def fold_diagonals(block):
    half = TILE // 2
    while half >= 8:
        block = block[:half] + pltpu.roll(block[half:], PAIR - half, 1)
        half //= 2
    total = block[0:1]
    for row in range(1, 8):
        total = total + pltpu.roll(block[row : row + 1], PAIR - row, 1)
    return total


def self_backward_kernel(
    len_ref, qkv_ref, win_ref, do_ref, o_ref, lse_ref,
    dqkv_ref, diag_ref,
    keys, values, keys_t, queries, grads, deltas, bias, bias_grad, dq,
):
    tiles = qkv_ref.shape[0] // TILE
    build_bias(win_ref, bias, tiles)
    for tile in range(tiles):
        block = qkv_ref[tile * TILE : (tile + 1) * TILE, 128:256]
        keys[tile] = block[:, :HDIM]
        values[tile] = block[:, HDIM:]
        keys_t[tile] = block[:, :HDIM].astype(FLOAT).T.astype(HALF)
    row_prepare(tiles, lambda rows: qkv_ref[rows, 0:128], do_ref, o_ref, queries, grads, deltas)
    bias_grad[...] = jnp.zeros_like(bias_grad)
    dq[...] = jnp.zeros_like(dq)
    ends = doc_ends(len_ref)
    total_rows = qkv_ref.shape[0]

    @pl.loop(0, tiles)
    def key_tile(other):
        last = other * TILE + TILE - 1
        key_pos = other * TILE + lax.broadcasted_iota(jnp.int32, (TILE, 1), 0)
        stop = jnp.where(last < ends[0], ends[0], jnp.where(last < ends[1], ends[1], total_rows))

        def row_tile(tile, state):
            dk, dv = state
            row_pos = lane_positions(tile * TILE)
            row_start = start_of(row_pos, ends)
            scores = dot_nt(keys[other], queries[tile]) + bias[tile - other]
            allowed = (key_pos <= row_pos) & (key_pos >= row_start)
            scores = jnp.where(allowed, scores, NEG)
            weights = jnp.exp(scores - lse_ref[pl.ds(tile, 1), :])
            d_weights = dot_nt(values[other], grads[tile])
            d_scores = weights * (d_weights - deltas[tile])
            bias_grad[tile - other] += d_scores
            d_half = d_scores.astype(HALF)
            dv = dv + dot(weights.astype(HALF), grads[tile])
            dk = dk + dot(d_half, queries[tile])
            dq[tile] += dot(keys_t[other], d_half)
            return dk, dv

        zero = jnp.zeros((TILE, HDIM), FLOAT)
        dk, dv = lax.fori_loop(other, (stop - 1) // TILE + 1, row_tile, (zero, zero))
        dqkv_ref[tile_rows(other), 128:256] = jnp.concatenate([dk, dv], axis=1).astype(HALF)

    for tile in range(tiles):
        dqkv_ref[tile * TILE : (tile + 1) * TILE, 0:128] = unstack_heads(dq[tile]).astype(HALF)
        for head in range(2):
            part = bias_grad[tile, :, head * TILE : (head + 1) * TILE]
            part = jnp.concatenate([part, jnp.zeros_like(part)], axis=1)
            diag_ref[pl.ds(tile * 2 + head, 1), :] = fold_diagonals(part)


def self_backward(doc_lens, qkv, windows, d_out, out, lse):
    rows = qkv.shape[0]
    tiles = rows // TILE
    vmem = pl.BlockSpec(memory_space=pltpu.VMEM)
    return pl.pallas_call(
        self_backward_kernel,
        out_shape=(
            jax.ShapeDtypeStruct((rows, 256), HALF),
            jax.ShapeDtypeStruct((2 * tiles, PAIR), FLOAT),
        ),
        in_specs=[pl.BlockSpec(memory_space=pltpu.SMEM)] + [vmem] * 5,
        out_specs=(vmem, vmem),
        scratch_shapes=[
            pltpu.VMEM((tiles, TILE, HDIM), HALF),
            pltpu.VMEM((tiles, TILE, HDIM), HALF),
            pltpu.VMEM((tiles, HDIM, TILE), HALF),
            pltpu.VMEM((tiles, PAIR, HDIM), HALF),
            pltpu.VMEM((tiles, PAIR, HDIM), HALF),
            pltpu.VMEM((tiles, 1, PAIR), FLOAT),
            pltpu.VMEM((tiles, TILE, PAIR), FLOAT),
            pltpu.VMEM((tiles, TILE, PAIR), FLOAT),
            pltpu.VMEM((tiles, HDIM, PAIR), FLOAT),
        ],
        compiler_params=pltpu.CompilerParams(vmem_limit_bytes=48 * 2**20),
    )(doc_lens, qkv, windows, d_out, out, lse)


def cross_forward_kernel(
    len_ref, slot_ref, enc_ref, q_ref, kv_ref, out_ref, lse_ref, keys, values_t
):
    tiles = q_ref.shape[0] // TILE
    key_tiles = kv_ref.shape[0] // TILE
    for tile in range(key_tiles):
        block = kv_ref[tile * TILE : (tile + 1) * TILE, :]
        keys[tile] = block[:, :HDIM]
        values_t[tile] = block[:, HDIM:].astype(FLOAT).T.astype(HALF)
    ends = doc_ends(len_ref)

    def doc_at(position):
        return (position >= ends[0]).astype(jnp.int32) + (position >= ends[1]).astype(jnp.int32)

    @pl.loop(0, tiles)
    def row_tile(tile):
        first = tile * TILE
        queries = stack_heads(q_ref[tile_rows(tile), :])
        row_doc = doc_at(lane_positions(first))

        def one_doc(doc, state):
            slot = slot_ref[0, doc]
            valid = enc_ref[0, slot]
            mine = row_doc == doc
            base = slot * (ENC // TILE)

            def key_tile(other, inner):
                scores = dot_nt(keys[base + other], queries)
                key_pos = other * TILE + lax.broadcasted_iota(jnp.int32, (TILE, 1), 0)
                scores = jnp.where(mine & (key_pos < valid), scores, NEG)
                return online(inner, scores, values_t[base + other])

            return lax.fori_loop(0, (valid + TILE - 1) // TILE, key_tile, state)

        state = lax.fori_loop(doc_at(first), doc_at(first + TILE - 1) + 1, one_doc, fresh_state())
        finish(state, tile, out_ref, lse_ref)


def cross_forward(doc_lens, slots, enc_lens, queries, kv):
    rows = queries.shape[0]
    key_tiles = kv.shape[0] // TILE
    vmem = pl.BlockSpec(memory_space=pltpu.VMEM)
    return pl.pallas_call(
        cross_forward_kernel,
        out_shape=(
            jax.ShapeDtypeStruct((rows, 128), HALF),
            jax.ShapeDtypeStruct((8, PAIR), FLOAT),
        ),
        in_specs=[pl.BlockSpec(memory_space=pltpu.SMEM)] * 3 + [vmem] * 2,
        out_specs=(vmem, vmem),
        scratch_shapes=[
            pltpu.VMEM((key_tiles, TILE, HDIM), HALF),
            pltpu.VMEM((key_tiles, HDIM, TILE), HALF),
        ],
        compiler_params=pltpu.CompilerParams(vmem_limit_bytes=48 * 2**20),
    )(doc_lens, slots, enc_lens, queries, kv)


def cross_backward_kernel(
    len_ref, slot_ref, enc_ref, q_ref, kv_ref, do_ref, o_ref, lse_ref,
    dq_ref, dkv_ref,
    keys, values, keys_t, queries, grads, deltas, dq,
):
    tiles = q_ref.shape[0] // TILE
    key_tiles = kv_ref.shape[0] // TILE
    for tile in range(key_tiles):
        block = kv_ref[tile * TILE : (tile + 1) * TILE, :]
        keys[tile] = block[:, :HDIM]
        values[tile] = block[:, HDIM:]
        keys_t[tile] = block[:, :HDIM].astype(FLOAT).T.astype(HALF)
    row_prepare(tiles, lambda rows: q_ref[rows, :], do_ref, o_ref, queries, grads, deltas)
    dq[...] = jnp.zeros_like(dq)
    dkv_ref[...] = jnp.zeros_like(dkv_ref)
    ends = doc_ends(len_ref)
    total_rows = q_ref.shape[0]

    @pl.loop(0, 3)
    def one_doc(doc):
        start = jnp.where(doc == 0, 0, jnp.where(doc == 1, ends[0], ends[1]))
        stop = jnp.where(doc == 0, ends[0], jnp.where(doc == 1, ends[1], total_rows))
        slot = slot_ref[0, doc]
        valid = enc_ref[0, slot]
        base = slot * (ENC // TILE)

        @pl.loop(0, (valid + TILE - 1) // TILE)
        def key_tile(other):
            key_pos = other * TILE + lax.broadcasted_iota(jnp.int32, (TILE, 1), 0)
            place = base + other

            def row_tile(tile, state):
                dk, dv = state
                row_pos = lane_positions(tile * TILE)
                scores = dot_nt(keys[place], queries[tile])
                allowed = (row_pos >= start) & (row_pos < stop) & (key_pos < valid)
                scores = jnp.where(allowed, scores, NEG)
                weights = jnp.exp(scores - lse_ref[pl.ds(tile, 1), :])
                d_weights = dot_nt(values[place], grads[tile])
                d_half = (weights * (d_weights - deltas[tile])).astype(HALF)
                dv = dv + dot(weights.astype(HALF), grads[tile])
                dk = dk + dot(d_half, queries[tile])
                dq[tile] += dot(keys_t[place], d_half)
                return dk, dv

            zero = jnp.zeros((TILE, HDIM), FLOAT)
            dk, dv = lax.fori_loop(
                start // TILE, (stop - 1) // TILE + 1, row_tile, (zero, zero)
            )
            dkv_ref[tile_rows(place), :] = jnp.concatenate([dk, dv], axis=1).astype(HALF)

    for tile in range(tiles):
        dq_ref[tile * TILE : (tile + 1) * TILE, :] = unstack_heads(dq[tile]).astype(HALF)


def cross_backward(doc_lens, slots, enc_lens, queries, kv, d_out, out, lse):
    rows = queries.shape[0]
    tiles = rows // TILE
    key_tiles = kv.shape[0] // TILE
    vmem = pl.BlockSpec(memory_space=pltpu.VMEM)
    return pl.pallas_call(
        cross_backward_kernel,
        out_shape=(
            jax.ShapeDtypeStruct((rows, 128), HALF),
            jax.ShapeDtypeStruct((kv.shape[0], 128), HALF),
        ),
        in_specs=[pl.BlockSpec(memory_space=pltpu.SMEM)] * 3 + [vmem] * 5,
        out_specs=(vmem, vmem),
        scratch_shapes=[
            pltpu.VMEM((key_tiles, TILE, HDIM), HALF),
            pltpu.VMEM((key_tiles, TILE, HDIM), HALF),
            pltpu.VMEM((key_tiles, HDIM, TILE), HALF),
            pltpu.VMEM((tiles, PAIR, HDIM), HALF),
            pltpu.VMEM((tiles, PAIR, HDIM), HALF),
            pltpu.VMEM((tiles, 1, PAIR), FLOAT),
            pltpu.VMEM((tiles, HDIM, PAIR), FLOAT),
        ],
        compiler_params=pltpu.CompilerParams(vmem_limit_bytes=48 * 2**20),
    )(doc_lens, slots, enc_lens, queries, kv, d_out, out, lse)


WIDTH = 1920
SHARD = 64
FF_PAD = 384
PAD_AT = 1536 + 352
CUTS = ((0, 640), (640, 640), (1280, 640))
ORDERS = ("zyx", "yxz", "xzy")


class Torus:
    def __init__(self):
        tok, hid = lax.axis_index("tok"), lax.axis_index("hid")
        self.core = lax.rem(tok, 2)
        self.pos = {
            "x": lax.rem(tok // 2, 2) * 2 + lax.rem(hid, 2),
            "y": tok // 4,
            "z": hid // 2,
        }

    def moved(self, axis, step):
        place = dict(self.pos)
        place[axis] = lax.rem(place[axis] + step + 4, 4)
        return place

    def device(self, place, core=None):
        core = self.core if core is None else core
        return (
            (place["y"] * 2 + place["x"] // 2) * 2 + core,
            place["z"] * 2 + lax.rem(place["x"], 2),
        )

    def neighbour(self, axis, step):
        return self.device(self.moved(axis, step))

    def sibling(self):
        return self.device(self.pos, 1 - self.core)

    def greet(self):
        barrier = pltpu.get_barrier_semaphore()
        peers = [self.neighbour(axis, step) for axis in "xyz" for step in (1, -1)]
        for peer in peers + [self.sibling()]:
            pl.semaphore_signal(barrier, inc=1, device_id=peer, device_id_type=MESH)
        return barrier


def block_index(place, whole):
    return (
        slice(None) if "z" in whole else place["z"],
        slice(None) if "x" in whole else lax.rem(place["x"], 2),
        slice(None) if "y" in whole else place["y"],
        slice(None) if "x" in whole else place["x"] // 2,
    )


def whole_dims(whole):
    dims = (4,) if "z" in whole else ()
    dims += (2,) if "x" in whole else ()
    dims += (4,) if "y" in whole else ()
    return dims + ((2,) if "x" in whole else ())


def gather_kernel(w_ref, out_ref, send_sem, recv_sem, core_send, core_recv, own_sem):
    torus = Torus()
    barrier = torus.greet()

    def view(place, whole, cut, rows=(0, SHARD)):
        return out_ref.at[
            block_index(place, whole) + (torus.core, pl.ds(*rows), pl.ds(*cut))
        ]

    own = pltpu.make_async_copy(
        w_ref, out_ref.at[block_index(torus.pos, "") + (torus.core,)], own_sem
    )
    own.start()
    own.wait()
    pl.semaphore_wait(barrier, 7)
    siblings, sends = [], []

    def to_sibling(ref):
        at = len(siblings)
        copy = pltpu.make_async_remote_copy(
            src_ref=ref, dst_ref=ref, send_sem=core_send.at[at], recv_sem=core_recv.at[at],
            device_id=torus.sibling(), device_id_type=MESH,
        )
        copy.start()
        siblings.append(copy)

    def send(ref, target):
        at = len(sends)
        copy = pltpu.make_async_remote_copy(
            src_ref=ref, dst_ref=ref, send_sem=send_sem.at[at], recv_sem=recv_sem.at[at],
            device_id=target, device_id_type=MESH,
        )
        copy.start()
        sends.append(copy)
        return copy

    for cut in CUTS:
        to_sibling(view(torus.pos, "", cut))
    for stage in range(3):
        near, far = [], []
        for part, cut in enumerate(CUTS):
            axis, whole = ORDERS[part][stage], ORDERS[part][:stage]
            ref = view(torus.pos, whole, cut)
            near.append(
                (send(ref, torus.neighbour(axis, 1)), send(ref, torus.neighbour(axis, -1)))
            )
        for part, cut in enumerate(CUTS):
            axis, whole = ORDERS[part][stage], ORDERS[part][:stage]
            before, after = torus.moved(axis, -1), torus.moved(axis, 1)
            near[part][0].wait_recv()
            one = send(view(before, whole, cut, (0, 32)), torus.neighbour(axis, 1))
            to_sibling(view(before, whole, cut))
            near[part][1].wait_recv()
            two = send(view(after, whole, cut, (32, 32)), torus.neighbour(axis, -1))
            to_sibling(view(after, whole, cut))
            far.append((one, two))
        for part, cut in enumerate(CUTS):
            axis, whole = ORDERS[part][stage], ORDERS[part][:stage]
            far[part][0].wait_recv()
            far[part][1].wait_recv()
            to_sibling(view(torus.moved(axis, 2), whole, cut))
    for copy in sends:
        copy.wait_send()
    for copy in siblings:
        copy.wait()


def gather_weights(packed):
    gathered = pl.pallas_call(
        gather_kernel,
        out_shape=jax.ShapeDtypeStruct((4, 2, 4, 2, 2, SHARD, WIDTH), HALF),
        in_specs=[pl.BlockSpec(memory_space=pl.ANY)],
        out_specs=pl.BlockSpec(memory_space=pl.ANY),
        scratch_shapes=[
            pltpu.SemaphoreType.DMA((36,)),
            pltpu.SemaphoreType.DMA((36,)),
            pltpu.SemaphoreType.DMA((30,)),
            pltpu.SemaphoreType.DMA((30,)),
            pltpu.SemaphoreType.DMA,
        ],
        compiler_params=pltpu.CompilerParams(collective_id=0, has_side_effects=True),
    )(packed)
    return gathered.reshape(8, 16 * SHARD, WIDTH)


def scatter_kernel(
    g_ref, out_ref, acc, core_in, *rest
):
    buffers = rest[:18]
    core_send, core_recv, load_sem, send_sem, recv_sem = rest[18:]
    torus = Torus()
    barrier = torus.greet()
    pl.semaphore_wait(barrier, 7)

    def add_blocks(place, whole, rows, cut, sources):
        dims = whole_dims(whole)
        count = 1
        for dim in dims:
            count *= dim

        def one(step):
            index, rest_of = [], step
            for dim in reversed(dims):
                index.append(lax.rem(rest_of, dim))
                rest_of = rest_of // dim
            index = index[::-1]
            left = iter(index)
            at = tuple(
                next(left) if isinstance(entry, slice) else entry
                for entry in block_index(place, whole)
            )
            where = at + (pl.ds(*rows), pl.ds(*cut))
            total = acc[where].astype(FLOAT)
            for source in sources:
                total = total + source(at, tuple(index)).astype(FLOAT)
            acc[where] = total.astype(acc.dtype)

        if count == 1:
            one(jnp.int32(0))
        else:
            pl.loop(0, count)(one)

    core_copies = {}
    for step in (2, 1, -1, 0):
        for part, cut in enumerate(CUTS):
            axis, whole = ORDERS[part][2], ORDERS[part][:2]
            at = block_index(torus.moved(axis, step), whole)
            cols = (slice(None), pl.ds(*cut))
            number = len(core_copies)
            remote = pltpu.make_async_remote_copy(
                src_ref=g_ref.at[at + (1 - torus.core,) + cols],
                dst_ref=core_in.at[at + cols],
                send_sem=core_send.at[number],
                recv_sem=core_recv.at[number],
                device_id=torus.sibling(),
                device_id_type=MESH,
            )
            remote.start()
            here = pltpu.make_async_copy(
                g_ref.at[at + (torus.core,) + cols], acc.at[at + cols], load_sem.at[number]
            )
            here.start()
            core_copies[step, part] = (remote, here)

    def core_sum(step, part):
        remote, here = core_copies[step, part]
        remote.wait_recv()
        here.wait()
        axis, whole, cut = ORDERS[part][2], ORDERS[part][:2], CUTS[part]
        add_blocks(
            torus.moved(axis, step), whole, (0, SHARD), cut,
            [lambda at, index: core_in[at + (slice(None), pl.ds(*cut))]],
        )

    sends = []

    def send(src, dst, target):
        at = len(sends)
        copy = pltpu.make_async_remote_copy(
            src_ref=src, dst_ref=dst, send_sem=send_sem.at[at], recv_sem=recv_sem.at[at],
            device_id=target, device_id_type=MESH,
        )
        copy.start()
        sends.append(copy)
        return copy

    def view(place, whole, rows, cut):
        return acc.at[block_index(place, whole) + (pl.ds(*rows), pl.ds(*cut))]

    def landed(buffer, slot):
        return lambda at, index: buffer[(slot,) + index]

    for stage in (2, 1, 0):
        far, near = [], []
        for part, cut in enumerate(CUTS):
            if stage == 2:
                core_sum(2, part)
            axis, whole = ORDERS[part][stage], ORDERS[part][:stage]
            buffer = buffers[(stage * 3 + part) * 2]
            across = torus.moved(axis, 2)
            far.append((
                send(view(across, whole, (0, 32), cut), buffer.at[0], torus.neighbour(axis, 1)),
                send(view(across, whole, (32, 32), cut), buffer.at[1], torus.neighbour(axis, -1)),
            ))
        for part, cut in enumerate(CUTS):
            if stage == 2:
                core_sum(1, part)
                core_sum(-1, part)
            axis, whole = ORDERS[part][stage], ORDERS[part][:stage]
            got, last = buffers[(stage * 3 + part) * 2 : (stage * 3 + part) * 2 + 2]
            pair = []
            for slot, step, rows in ((0, 1, (0, 32)), (1, -1, (32, 32))):
                place = torus.moved(axis, step)
                far[part][slot].wait_recv()
                add_blocks(place, whole, rows, cut, [landed(got, slot)])
                pair.append(
                    send(view(place, whole, (0, SHARD), cut), last.at[slot], torus.neighbour(axis, step))
                )
            near.append(pair)
        for part, cut in enumerate(CUTS):
            if stage == 2:
                core_sum(0, part)
            whole = ORDERS[part][:stage]
            last = buffers[(stage * 3 + part) * 2 + 1]
            near[part][0].wait_recv()
            near[part][1].wait_recv()
            if stage > 0:
                add_blocks(torus.pos, whole, (0, SHARD), cut, [landed(last, 0), landed(last, 1)])
            else:
                mine = acc[block_index(torus.pos, "") + (slice(None), pl.ds(*cut))]
                out_ref[:, pl.ds(*cut)] = (
                    mine.astype(FLOAT) + last[0].astype(FLOAT) + last[1].astype(FLOAT)
                )
    for copy in sends:
        copy.wait_send()
    for remote, _ in core_copies.values():
        remote.wait_send()


def scatter_grads(grads):
    scratch = [pltpu.VMEM((4, 2, 4, 2, SHARD, WIDTH), HALF)] * 2
    for stage in range(3):
        for part, cut in enumerate(CUTS):
            dims = whole_dims(ORDERS[part][:stage])
            scratch.append(pltpu.VMEM((2,) + dims + (32, cut[1]), HALF))
            scratch.append(pltpu.VMEM((2,) + dims + (SHARD, cut[1]), HALF))
    scratch += [pltpu.SemaphoreType.DMA((12,))] * 3 + [pltpu.SemaphoreType.DMA((36,))] * 2
    return pl.pallas_call(
        scatter_kernel,
        out_shape=jax.ShapeDtypeStruct((SHARD, WIDTH), FLOAT),
        in_specs=[pl.BlockSpec(memory_space=pl.ANY)],
        out_specs=pl.BlockSpec(memory_space=pltpu.VMEM),
        scratch_shapes=scratch,
        compiler_params=pltpu.CompilerParams(
            collective_id=1, has_side_effects=True, vmem_limit_bytes=60 * 2**20
        ),
    )(grads.reshape(4, 2, 4, 2, 2, SHARD, WIDTH))


def exchange_kernel(src_ref, dst_ref, send_sem, recv_sem, own_sem):
    me = lax.axis_index("hid")
    tok = lax.axis_index("tok")
    barrier = pltpu.get_barrier_semaphore()
    for step in range(1, 8):
        pl.semaphore_signal(
            barrier, inc=1, device_id=(tok, lax.rem(me + step, 8)), device_id_type=MESH
        )
    own = pltpu.make_async_copy(src_ref.at[me], dst_ref.at[me], own_sem)
    own.start()
    pl.semaphore_wait(barrier, 7)
    copies = []
    for step in range(1, 8):
        target = lax.rem(me + step, 8)
        copy = pltpu.make_async_remote_copy(
            src_ref=src_ref.at[target], dst_ref=dst_ref.at[me],
            send_sem=send_sem.at[step - 1], recv_sem=recv_sem.at[step - 1],
            device_id=(tok, target), device_id_type=MESH,
        )
        copy.start()
        copies.append(copy)
    own.wait()
    for copy in copies:
        copy.wait()


def exchange(blocks, number):
    return pl.pallas_call(
        exchange_kernel,
        out_shape=jax.ShapeDtypeStruct(blocks.shape, blocks.dtype),
        in_specs=[pl.BlockSpec(memory_space=pl.ANY)],
        out_specs=pl.BlockSpec(memory_space=pl.ANY),
        scratch_shapes=[
            pltpu.SemaphoreType.DMA((7,)),
            pltpu.SemaphoreType.DMA((7,)),
            pltpu.SemaphoreType.DMA,
        ],
        compiler_params=pltpu.CompilerParams(collective_id=number, has_side_effects=True),
    )(blocks)


def weight_grad_kernel(
    h1_ref, g1_ref, h2_ref, mem_ref, g2_ref, h3_ref, cot_ref,
    dqkv_ref, o1_ref, dq2_ref, dkv2_ref, o2_ref, dgu_ref, hid_ref, pad_ref,
    out_ref,
):
    def put(at, left, right):
        value = dot(left[...], right[0])
        out_ref[0, :, at : at + value.shape[1]] = value.astype(HALF)

    put(0, h1_ref, dqkv_ref)
    put(256, g1_ref, o1_ref)
    put(384, h2_ref, dq2_ref)
    put(512, mem_ref, dkv2_ref)
    put(640, g2_ref, o2_ref)
    put(768, h3_ref, dgu_ref)
    value = dot(cot_ref[...], hid_ref[0])
    out_ref[0, :, 1536:1792] = value[:, :256].astype(HALF)
    out_ref[0, :, 1792:1920] = (value[:, 256:] + pad_ref[0]).astype(HALF)


def weight_grads(lefts, rights, pads):
    return pl.pallas_call(
        weight_grad_kernel,
        grid=(8,),
        out_shape=jax.ShapeDtypeStruct((8, 1024, WIDTH), HALF),
        in_specs=[pl.BlockSpec(left.shape, lambda j: (0, 0)) for left in lefts]
        + [
            pl.BlockSpec((1,) + right.shape[1:], lambda j: (j, 0, 0))
            for right in rights + [pads]
        ],
        out_specs=pl.BlockSpec((1, 1024, WIDTH), lambda j: (j, 0, 0)),
        compiler_params=pltpu.CompilerParams(vmem_limit_bytes=56 * 2**20),
    )(*lefts, *rights, pads)


def rms_norm(row_vals, gain_vec):
    return (
        row_vals * lax.rsqrt(jnp.mean(row_vals * row_vals, axis=-1, keepdims=True) + EPS) * gain_vec
    )


def norm_back(row_vals, gain_vec, gradient):
    _, pullback = jax.vjp(rms_norm, row_vals, gain_vec)
    return pullback(gradient)


def gelu_product(gate_vals, up_vals):
    return jax.nn.gelu(gate_vals, approximate=True) * up_vals


def spread_cols(rows, weights):
    return jnp.einsum("rd,jdc->jrc", rows, weights, preferred_element_type=FLOAT)


def join_cols(blocks, weights):
    return jnp.einsum("jrc,jdc->rd", blocks, weights, preferred_element_type=FLOAT)


def bias_windows(by_distance):
    heads, rows = by_distance.shape
    tiles = by_distance.reshape(heads, rows // TILE, TILE)
    before = jnp.concatenate([jnp.zeros((heads, 1, TILE), FLOAT), tiles[:, :-1]], axis=1)
    windows = jnp.concatenate([tiles, before], axis=-1)
    return windows.transpose(1, 0, 2).reshape(-1, PAIR)


def from_windows(sums):
    sums = sums.reshape(-1, 2, PAIR)
    tail = jnp.concatenate([sums[1:, :, TILE:], jnp.zeros((1, 2, TILE), FLOAT)], axis=0)
    return (sums[:, :, :TILE] + tail).transpose(1, 0, 2).reshape(2, -1)


def local(
    tokens, memory, cotangent, norm1, w_query, w_key, w_value, w_out, rel_bias, norm2,
    cross_query, cross_key, cross_value, cross_out, norm3, w_gate, w_up, w_down,
    doc_lengths, memory_slot, enc_lengths, rel_bucket,
):
    widen = ((0, 0), (0, FF_PAD - w_gate.shape[1]))
    extras = jnp.concatenate(
        [
            jnp.stack([norm1, norm2, norm3], axis=1),
            jnp.pad(rel_bias, ((0, SHARD - rel_bias.shape[0]), (0, 0))),
            jnp.zeros((SHARD, 27), HALF),
        ],
        axis=1,
    )
    packed = jnp.concatenate(
        [
            w_query, w_key, w_value, w_out.T, cross_query, cross_key, cross_value, cross_out.T,
            jnp.pad(w_gate, widen), jnp.pad(w_up, widen), w_down.T, extras,
        ],
        axis=1,
    )
    weights = gather_weights(packed)
    gains = weights[0, :, PAD_AT : PAD_AT + 3].astype(FLOAT)
    gain_one, gain_two, gain_three = gains[:, 0], gains[:, 1], gains[:, 2]
    hid = lax.axis_index("hid")
    table = lax.dynamic_index_in_dim(weights, hid, 0, keepdims=False)
    table = table[:, PAD_AT + 3 : PAD_AT + 5].reshape(16, SHARD, 2)[:, :2].reshape(32, 2)
    onehot = (
        rel_bucket[:, None] == jnp.arange(32, dtype=jnp.int32)[None, :]
    ).astype(FLOAT)
    windows = bias_windows(jnp.dot(onehot, table.astype(FLOAT), precision=HIGH).T)
    w_qkv, w_o1, w_q2, w_kv2, w_o2 = (
        weights[:, :, 0:256], weights[:, :, 256:384], weights[:, :, 384:512],
        weights[:, :, 512:640], weights[:, :, 640:768],
    )
    w_g, w_u, w_d = weights[:, :, 768:1152], weights[:, :, 1152:1536], weights[:, :, 1536:1920]

    rows = tokens.shape[0]
    group_rows = rows * 8
    residual = tokens.astype(FLOAT)
    h_one = rms_norm(residual, gain_one).astype(HALF)
    qkv = exchange(spread_cols(h_one, w_qkv).astype(HALF), 2).reshape(group_rows, 256)
    kv_two = exchange(spread_cols(memory, w_kv2).astype(HALF), 3).reshape(-1, 128)
    o_one, lse_one = self_forward(doc_lengths, qkv, windows)
    o_one_rows = exchange(o_one.reshape(8, rows, 128), 4)
    x_one = residual + join_cols(o_one_rows, w_o1)
    h_two = rms_norm(x_one, gain_two).astype(HALF)
    q_two = exchange(spread_cols(h_two, w_q2).astype(HALF), 5).reshape(group_rows, 128)
    o_two, lse_two = cross_forward(doc_lengths, memory_slot, enc_lengths, q_two, kv_two)
    o_two_rows = exchange(o_two.reshape(8, rows, 128), 6)
    x_two = x_one + join_cols(o_two_rows, w_o2)
    h_three = rms_norm(x_two, gain_three).astype(HALF)
    gate, up = spread_cols(h_three, w_g), spread_cols(h_three, w_u)
    d_hidden = spread_cols(cotangent, w_d)
    hidden, pullback = jax.vjp(gelu_product, gate, up)
    hidden = hidden.astype(HALF)
    mixed = (x_two + join_cols(hidden, w_d)).astype(HALF)
    d_gate, d_up = pullback(d_hidden)
    d_gate, d_up = d_gate.astype(HALF), d_up.astype(HALF)
    d_h = join_cols(d_gate, w_g) + join_cols(d_up, w_u)
    d_inner, d_norm3 = norm_back(x_two, gain_three, d_h)
    d_rows = cotangent.astype(FLOAT) + d_inner
    g_two = d_rows.astype(HALF)
    d_out = exchange(spread_cols(g_two, w_o2).astype(HALF), 7).reshape(group_rows, 128)
    dq_two, dkv_two = cross_backward(
        doc_lengths, memory_slot, enc_lengths, q_two, kv_two, d_out, o_two, lse_two
    )
    dq_two = exchange(dq_two.reshape(8, rows, 128), 8)
    dkv_two = exchange(dkv_two.reshape(8, -1, 128), 9)
    d_memory = join_cols(dkv_two, w_kv2)
    d_inner, d_norm2 = norm_back(x_one, gain_two, join_cols(dq_two, w_q2))
    d_rows = d_rows + d_inner
    g_one = d_rows.astype(HALF)
    d_out = exchange(spread_cols(g_one, w_o1).astype(HALF), 10).reshape(group_rows, 128)
    dqkv, diagonals = self_backward(doc_lengths, qkv, windows, d_out, o_one, lse_one)
    dqkv = exchange(dqkv.reshape(8, rows, 256), 11)
    d_inner, d_norm1 = norm_back(residual, gain_one, join_cols(dqkv, w_qkv))
    d_tokens = d_rows + d_inner

    d_table = jnp.dot(onehot.T, from_windows(diagonals).T, precision=HIGH)
    d_table = jnp.pad(d_table.reshape(16, 2, 2), ((0, 0), (0, SHARD - 2), (0, 0)))
    d_table = d_table.reshape(1, 16 * SHARD, 2)
    owned = (jnp.arange(8, dtype=jnp.int32) == hid)[:, None, None]
    norms = jnp.stack([d_norm1, d_norm2, d_norm3], axis=1)
    pads = jnp.concatenate(
        [
            jnp.broadcast_to(norms[None], (8,) + norms.shape),
            jnp.where(owned, d_table, 0.0),
        ],
        axis=2,
    )
    pads = jnp.pad(pads, ((0, 0), (0, 0), (96, 27)))
    grads = weight_grads(
        [
            left.T for left in (h_one, g_one, h_two, memory, g_two, h_three, cotangent)
        ],
        [
            dqkv, o_one_rows, dq_two, dkv_two, o_two_rows,
            jnp.concatenate([d_gate, d_up], axis=2), hidden,
        ],
        pads,
    )
    shard = scatter_grads(grads)
    return (
        mixed,
        d_tokens,
        d_memory,
        shard[:, PAD_AT],
        shard[:, 0:128],
        shard[:, 128:192],
        shard[:, 192:256],
        shard[:, 256:384].T,
        shard[:2, PAD_AT + 3 : PAD_AT + 5],
        shard[:, PAD_AT + 1],
        shard[:, 384:512],
        shard[:, 512:576],
        shard[:, 576:640],
        shard[:, 640:768].T,
        shard[:, PAD_AT + 2],
        shard[:, 768:1120],
        shard[:, 1152:1504],
        shard[:, 1536:1888].T,
    )


def solution(mesh):
    return jax.shard_map(
        local,
        mesh=mesh,
        in_specs=(
            P(("tok", "hid"), None),
            P(("tok", "hid"), None),
            P(("tok", "hid"), None),
            P("tok"),
            P("tok", "hid"),
            P("tok", "hid"),
            P("tok", "hid"),
            P("hid", "tok"),
            P("tok", "hid"),
            P("tok"),
            P("tok", "hid"),
            P("tok", "hid"),
            P("tok", "hid"),
            P("hid", "tok"),
            P("tok"),
            P("tok", "hid"),
            P("tok", "hid"),
            P("hid", "tok"),
            P("tok", None),
            P("tok", None),
            P("tok", None),
            P(),
        ),
        out_specs=(
            P(("tok", "hid"), None),
            P(("tok", "hid"), None),
            P(("tok", "hid"), None),
            P("tok"),
            P("tok", "hid"),
            P("tok", "hid"),
            P("tok", "hid"),
            P("hid", "tok"),
            P("tok", "hid"),
            P("tok"),
            P("tok", "hid"),
            P("tok", "hid"),
            P("tok", "hid"),
            P("hid", "tok"),
            P("tok"),
            P("tok", "hid"),
            P("tok", "hid"),
            P("hid", "tok"),
        ),
        check_vma=False,
    )
```

```python
import jax
import jax.numpy as jnp
from jax import lax
from jax.experimental import pallas as pl
from jax.experimental.pallas import tpu as pltpu
from jax.sharding import PartitionSpec as P

EPS = 1e-06
HIGH = lax.Precision.HIGHEST
MESH = pl.DeviceIdType.MESH

HDIM = 64
ENC = 1024
FLOAT = jnp.float32
HALF = jnp.bfloat16
TILE = 256
PAIR = 2 * TILE
NEG = -1e30
NT_DIMS = (((1,), (1,)), ((), ()))


def dot(first, second):
    return jnp.dot(first, second, preferred_element_type=FLOAT)


def dot_nt(first, second):
    return lax.dot_general(first, second, NT_DIMS, preferred_element_type=FLOAT)


def stack_heads(block):
    return jnp.concatenate([block[:, :HDIM], block[:, HDIM:]], axis=0)


def unstack_heads(columns):
    return jnp.concatenate(
        [columns[:, :TILE].T, columns[:, TILE:].T], axis=1
    )


def tile_rows(tile):
    return pl.ds(pl.multiple_of(tile * TILE, TILE), TILE)


def lane_positions(first):
    lane = lax.broadcasted_iota(jnp.int32, (1, PAIR), 1)
    return first + jnp.where(lane >= TILE, lane - TILE, lane)


def doc_ends(len_ref):
    first_end = len_ref[0, 0]
    return first_end, first_end + len_ref[0, 1]


def start_of(position, ends):
    return jnp.where(position >= ends[1], ends[1], jnp.where(position >= ends[0], ends[0], 0))


def build_bias(win_ref, bias, tiles):
    for diag in range(tiles):
        for head in range(2):
            row = win_ref[pl.ds(head * 8 + diag, 1), :]
            spread = jnp.broadcast_to(row, (TILE, PAIR))
            rolled = pltpu.roll(spread, 0, 1, stride=1, stride_axis=0)
            bias[diag, :, pl.ds(head * TILE, TILE)] = rolled[:, :TILE]


def online(state, scores, values_t):
    peak, total, acc = state
    new_peak = jnp.maximum(peak, jnp.max(scores, axis=0, keepdims=True))
    shrink = jnp.exp(peak - new_peak)
    weights = jnp.exp(scores - new_peak)
    total = total * shrink + jnp.sum(weights, axis=0, keepdims=True)
    acc = acc * shrink + dot(values_t, weights.astype(HALF))
    return new_peak, total, acc


def fresh_state():
    return (
        jnp.full((1, PAIR), NEG, FLOAT),
        jnp.zeros((1, PAIR), FLOAT),
        jnp.zeros((HDIM, PAIR), FLOAT),
    )


def finish(state, tile, out_ref, lse_ref):
    peak, total, acc = state
    out_ref[tile_rows(tile), :] = unstack_heads(acc / total).astype(HALF)
    lse_ref[pl.ds(tile, 1), :] = peak + jnp.log(total)


def row_prepare(tiles, q_of, do_ref, o_ref, queries, grads, deltas):
    for tile in range(tiles):
        rows = slice(tile * TILE, (tile + 1) * TILE)
        queries[tile] = stack_heads(q_of(rows))
        block = do_ref[rows, :]
        grads[tile] = stack_heads(block)
        product = (block.astype(FLOAT) * o_ref[rows, :].astype(FLOAT)).T
        deltas[tile] = jnp.concatenate(
            [
                jnp.sum(product[:HDIM], axis=0, keepdims=True),
                jnp.sum(product[HDIM:], axis=0, keepdims=True),
            ],
            axis=1,
        )


def fold_diagonals(block):
    half = TILE // 2
    while half >= 8:
        block = block[:half] + pltpu.roll(block[half:], PAIR - half, 1)
        half //= 2
    total = block[0:1]
    for row in range(1, 8):
        total = total + pltpu.roll(block[row : row + 1], PAIR - row, 1)
    return total


def self_backward_kernel(
    len_ref, qkv_ref, win_ref, do_ref, o_ref, lse_ref,
    dqkv_ref, diag_ref,
    keys, values, keys_t, queries, grads, deltas, bias, bias_grad, dq,
):
    tiles = qkv_ref.shape[0] // TILE
    build_bias(win_ref, bias, tiles)
    for tile in range(tiles):
        block = qkv_ref[tile * TILE : (tile + 1) * TILE, 128:256]
        keys[tile] = block[:, :HDIM]
        values[tile] = block[:, HDIM:]
        keys_t[tile] = block[:, :HDIM].astype(FLOAT).T.astype(HALF)
    row_prepare(tiles, lambda rows: qkv_ref[rows, 0:128], do_ref, o_ref, queries, grads, deltas)
    bias_grad[...] = jnp.zeros_like(bias_grad)
    dq[...] = jnp.zeros_like(dq)
    ends = doc_ends(len_ref)
    total_rows = qkv_ref.shape[0]

    @pl.loop(0, tiles)
    def key_tile(other):
        last = other * TILE + TILE - 1
        key_pos = other * TILE + lax.broadcasted_iota(jnp.int32, (TILE, 1), 0)
        stop = jnp.where(last < ends[0], ends[0], jnp.where(last < ends[1], ends[1], total_rows))

        def row_tile(tile, state):
            dk, dv = state
            row_pos = lane_positions(tile * TILE)
            row_start = start_of(row_pos, ends)
            scores = dot_nt(keys[other], queries[tile]) + bias[tile - other]
            allowed = (key_pos <= row_pos) & (key_pos >= row_start)
            scores = jnp.where(allowed, scores, NEG)
            weights = jnp.exp(scores - lse_ref[pl.ds(tile, 1), :])
            d_weights = dot_nt(values[other], grads[tile])
            d_scores = weights * (d_weights - deltas[tile])
            bias_grad[tile - other] += d_scores
            d_half = d_scores.astype(HALF)
            dv = dv + dot(weights.astype(HALF), grads[tile])
            dk = dk + dot(d_half, queries[tile])
            dq[tile] += dot(keys_t[other], d_half)
            return dk, dv

        zero = jnp.zeros((TILE, HDIM), FLOAT)
        dk, dv = lax.fori_loop(other, (stop - 1) // TILE + 1, row_tile, (zero, zero))
        dqkv_ref[tile_rows(other), 128:256] = jnp.concatenate([dk, dv], axis=1).astype(HALF)

    for tile in range(tiles):
        dqkv_ref[tile * TILE : (tile + 1) * TILE, 0:128] = unstack_heads(dq[tile]).astype(HALF)
        for head in range(2):
            part = bias_grad[tile, :, head * TILE : (head + 1) * TILE]
            part = jnp.concatenate([part, jnp.zeros_like(part)], axis=1)
            diag_ref[pl.ds(tile * 2 + head, 1), :] = fold_diagonals(part)


def self_backward(doc_lens, qkv, windows, d_out, out, lse):
    rows = qkv.shape[0]
    tiles = rows // TILE
    vmem = pl.BlockSpec(memory_space=pltpu.VMEM)
    return pl.pallas_call(
        self_backward_kernel,
        out_shape=(
            jax.ShapeDtypeStruct((rows, 256), HALF),
            jax.ShapeDtypeStruct((2 * tiles, PAIR), FLOAT),
        ),
        in_specs=[pl.BlockSpec(memory_space=pltpu.SMEM)] + [vmem] * 5,
        out_specs=(vmem, vmem),
        scratch_shapes=[
            pltpu.VMEM((tiles, TILE, HDIM), HALF),
            pltpu.VMEM((tiles, TILE, HDIM), HALF),
            pltpu.VMEM((tiles, HDIM, TILE), HALF),
            pltpu.VMEM((tiles, PAIR, HDIM), HALF),
            pltpu.VMEM((tiles, PAIR, HDIM), HALF),
            pltpu.VMEM((tiles, 1, PAIR), FLOAT),
            pltpu.VMEM((tiles, TILE, PAIR), FLOAT),
            pltpu.VMEM((tiles, TILE, PAIR), FLOAT),
            pltpu.VMEM((tiles, HDIM, PAIR), FLOAT),
        ],
        compiler_params=pltpu.CompilerParams(vmem_limit_bytes=48 * 2**20),
    )(doc_lens, qkv, windows, d_out, out, lse)


def cross_forward_kernel(
    len_ref, slot_ref, enc_ref, q_ref, kv_ref, out_ref, lse_ref, keys, values_t
):
    tiles = q_ref.shape[0] // TILE
    key_tiles = kv_ref.shape[0] // TILE
    for tile in range(key_tiles):
        block = kv_ref[tile * TILE : (tile + 1) * TILE, :]
        keys[tile] = block[:, :HDIM]
        values_t[tile] = block[:, HDIM:].astype(FLOAT).T.astype(HALF)
    ends = doc_ends(len_ref)

    def doc_at(position):
        return (position >= ends[0]).astype(jnp.int32) + (position >= ends[1]).astype(jnp.int32)

    @pl.loop(0, tiles)
    def row_tile(tile):
        first = tile * TILE
        queries = stack_heads(q_ref[tile_rows(tile), :])
        row_doc = doc_at(lane_positions(first))

        def one_doc(doc, state):
            slot = slot_ref[0, doc]
            valid = enc_ref[0, slot]
            mine = row_doc == doc
            base = slot * (ENC // TILE)

            def key_tile(other, inner):
                scores = dot_nt(keys[base + other], queries)
                key_pos = other * TILE + lax.broadcasted_iota(jnp.int32, (TILE, 1), 0)
                scores = jnp.where(mine & (key_pos < valid), scores, NEG)
                return online(inner, scores, values_t[base + other])

            return lax.fori_loop(0, (valid + TILE - 1) // TILE, key_tile, state)

        state = lax.fori_loop(doc_at(first), doc_at(first + TILE - 1) + 1, one_doc, fresh_state())
        finish(state, tile, out_ref, lse_ref)


def cross_forward(doc_lens, slots, enc_lens, queries, kv):
    rows = queries.shape[0]
    key_tiles = kv.shape[0] // TILE
    vmem = pl.BlockSpec(memory_space=pltpu.VMEM)
    return pl.pallas_call(
        cross_forward_kernel,
        out_shape=(
            jax.ShapeDtypeStruct((rows, 128), HALF),
            jax.ShapeDtypeStruct((8, PAIR), FLOAT),
        ),
        in_specs=[pl.BlockSpec(memory_space=pltpu.SMEM)] * 3 + [vmem] * 2,
        out_specs=(vmem, vmem),
        scratch_shapes=[
            pltpu.VMEM((key_tiles, TILE, HDIM), HALF),
            pltpu.VMEM((key_tiles, HDIM, TILE), HALF),
        ],
        compiler_params=pltpu.CompilerParams(vmem_limit_bytes=48 * 2**20),
    )(doc_lens, slots, enc_lens, queries, kv)


def cross_backward_kernel(
    len_ref, slot_ref, enc_ref, q_ref, kv_ref, do_ref, o_ref, lse_ref,
    dq_ref, dkv_ref,
    keys, values, keys_t, queries, grads, deltas, dq,
):
    tiles = q_ref.shape[0] // TILE
    key_tiles = kv_ref.shape[0] // TILE
    for tile in range(key_tiles):
        block = kv_ref[tile * TILE : (tile + 1) * TILE, :]
        keys[tile] = block[:, :HDIM]
        values[tile] = block[:, HDIM:]
        keys_t[tile] = block[:, :HDIM].astype(FLOAT).T.astype(HALF)
    row_prepare(tiles, lambda rows: q_ref[rows, :], do_ref, o_ref, queries, grads, deltas)
    dq[...] = jnp.zeros_like(dq)
    dkv_ref[...] = jnp.zeros_like(dkv_ref)
    ends = doc_ends(len_ref)
    total_rows = q_ref.shape[0]

    @pl.loop(0, 3)
    def one_doc(doc):
        start = jnp.where(doc == 0, 0, jnp.where(doc == 1, ends[0], ends[1]))
        stop = jnp.where(doc == 0, ends[0], jnp.where(doc == 1, ends[1], total_rows))
        slot = slot_ref[0, doc]
        valid = enc_ref[0, slot]
        base = slot * (ENC // TILE)

        @pl.loop(0, (valid + TILE - 1) // TILE)
        def key_tile(other):
            key_pos = other * TILE + lax.broadcasted_iota(jnp.int32, (TILE, 1), 0)
            place = base + other

            def row_tile(tile, state):
                dk, dv = state
                row_pos = lane_positions(tile * TILE)
                scores = dot_nt(keys[place], queries[tile])
                allowed = (row_pos >= start) & (row_pos < stop) & (key_pos < valid)
                scores = jnp.where(allowed, scores, NEG)
                weights = jnp.exp(scores - lse_ref[pl.ds(tile, 1), :])
                d_weights = dot_nt(values[place], grads[tile])
                d_half = (weights * (d_weights - deltas[tile])).astype(HALF)
                dv = dv + dot(weights.astype(HALF), grads[tile])
                dk = dk + dot(d_half, queries[tile])
                dq[tile] += dot(keys_t[place], d_half)
                return dk, dv

            zero = jnp.zeros((TILE, HDIM), FLOAT)
            dk, dv = lax.fori_loop(
                start // TILE, (stop - 1) // TILE + 1, row_tile, (zero, zero)
            )
            dkv_ref[tile_rows(place), :] = jnp.concatenate([dk, dv], axis=1).astype(HALF)

    for tile in range(tiles):
        dq_ref[tile * TILE : (tile + 1) * TILE, :] = unstack_heads(dq[tile]).astype(HALF)


def cross_backward(doc_lens, slots, enc_lens, queries, kv, d_out, out, lse):
    rows = queries.shape[0]
    tiles = rows // TILE
    key_tiles = kv.shape[0] // TILE
    vmem = pl.BlockSpec(memory_space=pltpu.VMEM)
    return pl.pallas_call(
        cross_backward_kernel,
        out_shape=(
            jax.ShapeDtypeStruct((rows, 128), HALF),
            jax.ShapeDtypeStruct((kv.shape[0], 128), HALF),
        ),
        in_specs=[pl.BlockSpec(memory_space=pltpu.SMEM)] * 3 + [vmem] * 5,
        out_specs=(vmem, vmem),
        scratch_shapes=[
            pltpu.VMEM((key_tiles, TILE, HDIM), HALF),
            pltpu.VMEM((key_tiles, TILE, HDIM), HALF),
            pltpu.VMEM((key_tiles, HDIM, TILE), HALF),
            pltpu.VMEM((tiles, PAIR, HDIM), HALF),
            pltpu.VMEM((tiles, PAIR, HDIM), HALF),
            pltpu.VMEM((tiles, 1, PAIR), FLOAT),
            pltpu.VMEM((tiles, HDIM, PAIR), FLOAT),
        ],
        compiler_params=pltpu.CompilerParams(vmem_limit_bytes=48 * 2**20),
    )(doc_lens, slots, enc_lens, queries, kv, d_out, out, lse)


WIDTH = 1920
SHARD = 64
FF_PAD = 384
PAD_AT = 1536 + 352
CUTS = ((0, 640), (640, 640), (1280, 640))
ORDERS = ("zyx", "yxz", "xzy")


class Torus:
    def __init__(self):
        tok, hid = lax.axis_index("tok"), lax.axis_index("hid")
        self.core = lax.rem(tok, 2)
        self.pos = {
            "x": lax.rem(tok // 2, 2) * 2 + lax.rem(hid, 2),
            "y": tok // 4,
            "z": hid // 2,
        }

    def moved(self, axis, step):
        place = dict(self.pos)
        place[axis] = lax.rem(place[axis] + step + 4, 4)
        return place

    def device(self, place, core=None):
        core = self.core if core is None else core
        return (
            (place["y"] * 2 + place["x"] // 2) * 2 + core,
            place["z"] * 2 + lax.rem(place["x"], 2),
        )

    def neighbour(self, axis, step):
        return self.device(self.moved(axis, step))

    def sibling(self):
        return self.device(self.pos, 1 - self.core)

    def greet(self):
        barrier = pltpu.get_barrier_semaphore()
        peers = [self.neighbour(axis, step) for axis in "xyz" for step in (1, -1)]
        for peer in peers + [self.sibling()]:
            pl.semaphore_signal(barrier, inc=1, device_id=peer, device_id_type=MESH)
        return barrier


def block_index(place, whole):
    return (
        slice(None) if "z" in whole else place["z"],
        slice(None) if "x" in whole else lax.rem(place["x"], 2),
        slice(None) if "y" in whole else place["y"],
        slice(None) if "x" in whole else place["x"] // 2,
    )


def whole_dims(whole):
    dims = (4,) if "z" in whole else ()
    dims += (2,) if "x" in whole else ()
    dims += (4,) if "y" in whole else ()
    return dims + ((2,) if "x" in whole else ())


class Flow:
    def __init__(self, torus, out_ref, cuts, orders, sems):
        self.torus, self.out_ref, self.cuts, self.orders = torus, out_ref, cuts, orders
        self.sems = sems
        self.rows = out_ref.shape[5]
        self.sends, self.siblings = [], []
        self.last = {}

    def view(self, place, whole, cut, rows=None):
        rows = (0, self.rows) if rows is None else rows
        return self.out_ref.at[
            block_index(place, whole) + (self.torus.core, pl.ds(*rows), pl.ds(*cut))
        ]

    def copy(self, ref, target, first, log):
        at = len(log)
        copy = pltpu.make_async_remote_copy(
            src_ref=ref, dst_ref=ref,
            send_sem=self.sems[first].at[at], recv_sem=self.sems[first + 1].at[at],
            device_id=target, device_id_type=MESH,
        )
        copy.start()
        log.append(copy)
        return copy

    def to_sibling(self, place, whole, cut):
        self.copy(self.view(place, whole, cut), self.torus.sibling(), 2, self.siblings)

    def plan(self, stage):
        for part, cut in enumerate(self.cuts):
            yield part, cut, self.orders[part][stage], self.orders[part][:stage]

    def near(self, stage):
        torus = self.torus
        for part, cut, axis, whole in self.plan(stage):
            if stage == 0:
                self.to_sibling(torus.pos, "", cut)
            ref = self.view(torus.pos, whole, cut)
            self.last[part] = [
                self.copy(ref, torus.neighbour(axis, step), 0, self.sends) for step in (1, -1)
            ]

    def far(self, stage):
        torus, half = self.torus, self.rows // 2
        for part, cut, axis, whole in self.plan(stage):
            copies = []
            for copy, step, first in zip(self.last[part], (1, -1), (0, half)):
                origin = torus.moved(axis, -step)
                copy.wait_recv()
                if half >= 16:
                    ref = self.view(origin, whole, cut, (first, half))
                    copies.append(self.copy(ref, torus.neighbour(axis, step), 0, self.sends))
                elif step == 1:
                    ref = self.view(origin, whole, cut)
                    copies.append(self.copy(ref, torus.neighbour(axis, step), 0, self.sends))
                self.to_sibling(origin, whole, cut)
            self.last[part] = copies

    def done(self, stage):
        for part, cut, axis, whole in self.plan(stage):
            for copy in self.last[part]:
                copy.wait_recv()
            self.to_sibling(self.torus.moved(axis, 2), whole, cut)

    def arrived(self):
        for copy in self.siblings:
            copy.wait_recv()

    def finish(self):
        for copy in self.sends + self.siblings:
            copy.wait_send()


def flow_sems(parts, split):
    sends = parts * 3 * (2 + split)
    return [pltpu.SemaphoreType.DMA((sends,))] * 2 + [pltpu.SemaphoreType.DMA((parts * 10,))] * 2


class Trade:
    def __init__(self, src, land, sems):
        self.src, self.land, self.sems = src, land, sems
        self.me = lax.axis_index("hid")
        self.tok = lax.axis_index("tok")

    def copy(self, step):
        target = lax.rem(self.me + step, 8)
        return pltpu.make_async_remote_copy(
            src_ref=self.src(target), dst_ref=self.land(self.me),
            send_sem=self.sems[0].at[step - 1], recv_sem=self.sems[1].at[step - 1],
            device_id=(self.tok, target), device_id_type=MESH,
        )

    def start(self, step):
        self.copy(step).start()

    def start_all(self):
        for step in range(1, 8):
            self.start(step)

    def arrived(self):
        for step in range(1, 8):
            self.copy(step).wait_recv()

    def finish(self):
        for step in range(1, 8):
            self.copy(step).wait_send()


def trade_sems():
    return [pltpu.SemaphoreType.DMA((7,))] * 2


def greet_all(torus):
    barrier = pltpu.get_barrier_semaphore()
    tok, me = lax.axis_index("tok"), lax.axis_index("hid")
    outside = 2 * lax.rem(me, 2) - 1
    peers = [(tok, lax.rem(me + step, 8)) for step in range(1, 8)]
    peers += [torus.neighbour("y", 1), torus.neighbour("y", -1), torus.neighbour("x", outside)]
    peers += [torus.sibling()]
    for peer in peers:
        pl.semaphore_signal(barrier, inc=1, device_id=peer, device_id_type=MESH)
    return barrier, len(peers)


def greet_hid():
    barrier = pltpu.get_barrier_semaphore()
    tok, me = lax.axis_index("tok"), lax.axis_index("hid")
    for step in range(1, 8):
        pl.semaphore_signal(
            barrier, inc=1, device_id=(tok, lax.rem(me + step, 8)), device_id_type=MESH
        )
    return barrier


def rows_at(index, rows):
    return pl.ds(pl.multiple_of(index * rows, 64), rows)


def each_target(body):
    me = lax.axis_index("hid")

    @pl.loop(1, 9)
    def one(step):
        body(step, lax.rem(me + step, 8), step < 8)


def scale_of(row_vals):
    return lax.rsqrt(jnp.mean(row_vals * row_vals, axis=-1, keepdims=True) + EPS)


def norm_backward(row_vals, gain, gradient):
    scale = scale_of(row_vals)
    normal = row_vals * scale
    d_gain = jnp.sum(gradient * normal, axis=0, keepdims=True)
    weighted = gradient * gain
    inner = jnp.mean(weighted * normal, axis=-1, keepdims=True)
    return scale * (weighted - normal * inner), d_gain


def forward_kernel(
    packed_ref, small_ref, tok_ref, mem_ref, len_ref, bucket_ref,
    wf_ref, wa_ref, gain_ref, win_ref, h1_ref, h2_ref, qkv_ref, kv_ref,
    o1_ref, o1r_ref, lse_ref, x1_ref, q2_ref,
    wa, small, send_qkv, send_kv, send_q2, keys, values_t, bias, own_sem, *sems,
):
    torus = Torus()
    me = lax.axis_index("hid")
    rows, mem_rows = tok_ref.shape[0], mem_ref.shape[0]
    tiles = qkv_ref.shape[0] // TILE
    barrier, count = greet_all(torus)
    here = block_index(torus.pos, "") + (torus.core,)
    owns = [
        pltpu.make_async_copy(packed_ref.at[:, pl.ds(0, 768)], wa.at[here], own_sem.at[0]),
        pltpu.make_async_copy(packed_ref.at[:, pl.ds(768, 1152)], wf_ref.at[here], own_sem.at[1]),
        pltpu.make_async_copy(small_ref, small.at[here], own_sem.at[2]),
    ]
    for own in owns:
        own.start()
    for own in owns:
        own.wait()
    pl.semaphore_wait(barrier, count)

    cuts_a = tuple((at, 256) for at in (0, 256, 512))
    cuts_f = tuple((at, 384) for at in (0, 384, 768))
    flow_a = Flow(torus, wa, cuts_a, ORDERS, sems[0:4])
    flow_f = Flow(torus, wf_ref, cuts_f, ORDERS, sems[4:8])
    flow_s = Flow(torus, small, ((0, 128),), ORDERS, sems[8:12])
    flow_a.near(0)
    flow_s.near(0)
    flow_f.near(0)
    flow_a.far(0)
    flow_s.far(0)
    flow_f.far(0)
    for stage in (1, 2):
        flow_a.done(stage - 1)
        flow_s.done(stage - 1)
        flow_a.near(stage)
        flow_s.near(stage)
        if stage == 1:
            flow_f.done(0)
            flow_f.near(1)
        flow_a.far(stage)
        flow_s.far(stage)
        if stage == 1:
            flow_f.far(1)
    flow_s.done(2)
    flow_f.done(1)
    flow_s.arrived()
    z, xlo = torus.pos["z"], lax.rem(me, 2)
    gain_parts = []
    heads = [jnp.zeros((8, PAIR), FLOAT), jnp.zeros((8, PAIR), FLOAT)]
    buckets = bucket_ref[...]
    for pair in range(8):
        blocks = [small[z, xlo, pair // 2, pair % 2, core].astype(FLOAT) for core in range(2)]
        gain_parts.append((blocks[0] + blocks[1])[0:8])
        for core in range(2):
            for part in range(2):
                bucket = (pair * 2 + core) * 2 + part
                for head in range(2):
                    at = 3 + part * 2 + head
                    value = blocks[core][at : at + 1]
                    value = jnp.concatenate([value] * 4, axis=1)
                    heads[head] = jnp.where(buckets == bucket, value, heads[head])
    gain_ref[...] = jnp.concatenate(gain_parts, axis=1)
    win_ref[0:8] = heads[0]
    win_ref[8:16] = heads[1]
    residual = tok_ref[...].astype(FLOAT)
    h1_ref[...] = (residual * scale_of(residual) * gain_ref[0:1, :]).astype(HALF)
    build_bias(win_ref, bias, tiles)

    flow_a.done(2)
    flow_f.near(2)
    flow_a.arrived()
    keep = pltpu.make_async_copy(wa, wa_ref, own_sem.at[0])
    keep.start()

    def weights(j, first, width):
        block = wa[j // 2, lax.rem(j, 2), :, :, :, :, first : first + width]
        return block.reshape(16 * SHARD, width)

    qkv_trade = Trade(
        lambda j: send_qkv.at[j], lambda j: qkv_ref.at[rows_at(j, rows)], sems[12:14]
    )
    kv_trade = Trade(
        lambda j: send_kv.at[j], lambda j: kv_ref.at[rows_at(j, mem_rows)], sems[14:16]
    )
    o1_trade = Trade(
        lambda j: o1_ref.at[rows_at(j, rows)], lambda j: o1r_ref.at[j], sems[16:18]
    )
    q2_trade = Trade(
        lambda j: send_q2.at[j], lambda j: q2_ref.at[rows_at(j, rows)], sems[18:20]
    )

    def spread(trade, left_ref, first, width, send_ref, land_ref):
        def one(step, j, remote):
            value = dot(left_ref[...], weights(j, first, width)).astype(HALF)

            @pl.when(remote)
            def _():
                send_ref[j] = value
                trade.start(step)

            @pl.when(jnp.logical_not(remote))
            def _():
                land_ref[rows_at(me, left_ref.shape[0]), :] = value

        each_target(one)

    spread(qkv_trade, h1_ref, 0, 256, send_qkv, qkv_ref)
    spread(kv_trade, mem_ref, 512, 128, send_kv, kv_ref)
    qkv_trade.arrived()
    flow_f.far(2)

    for tile in range(tiles):
        block = qkv_ref[tile * TILE : (tile + 1) * TILE, 128:256]
        keys[tile] = block[:, :HDIM]
        values_t[tile] = block[:, HDIM:].astype(FLOAT).T.astype(HALF)
    ends = doc_ends(len_ref)

    @pl.loop(0, tiles)
    def row_tile(tile):
        queries = stack_heads(qkv_ref[tile_rows(tile), 0:128])
        row_pos = lane_positions(tile * TILE)
        row_start = start_of(row_pos, ends)

        def key_tile(other, state):
            scores = dot_nt(keys[other], queries) + bias[tile - other]
            key_pos = other * TILE + lax.broadcasted_iota(jnp.int32, (TILE, 1), 0)
            allowed = (key_pos <= row_pos) & (key_pos >= row_start)
            scores = jnp.where(allowed, scores, NEG)
            return online(state, scores, values_t[other])

        finish(lax.fori_loop(0, tile + 1, key_tile, fresh_state()), tile, o1_ref, lse_ref)

    o1_trade.start_all()
    o1r_ref[me] = o1_ref[rows_at(me, rows), :]
    o1_trade.arrived()
    total = tok_ref[...].astype(FLOAT)
    for pair in range(4):
        left = jnp.concatenate([o1r_ref[2 * pair], o1r_ref[2 * pair + 1]], axis=1)
        right = jnp.concatenate(
            [weights(2 * pair, 256, 128), weights(2 * pair + 1, 256, 128)], axis=1
        )
        total = total + dot_nt(left, right)
    x1_ref[...] = total
    h2_ref[...] = (total * scale_of(total) * gain_ref[1:2, :]).astype(HALF)
    spread(q2_trade, h2_ref, 384, 128, send_q2, q2_ref)
    flow_f.done(2)
    q2_trade.arrived()
    kv_trade.arrived()
    flow_f.arrived()
    for trade in (qkv_trade, kv_trade, o1_trade, q2_trade):
        trade.finish()
    for flow in (flow_a, flow_f, flow_s):
        flow.finish()
    keep.wait()


def forward(packed, small, tokens, memory, doc_lens, buckets):
    rows, mem_rows = tokens.shape[0], memory.shape[0]
    group, keys = rows * 8, mem_rows * 8
    tiles = group // TILE
    vmem = pl.BlockSpec(memory_space=pltpu.VMEM)
    anywhere = pl.BlockSpec(memory_space=pl.ANY)
    shape = jax.ShapeDtypeStruct
    places = (4, 2, 4, 2, 2)
    return pl.pallas_call(
        forward_kernel,
        out_shape=(
            shape(places + (SHARD, 1152), HALF),
            shape(places + (SHARD, 768), HALF),
            shape((8, 1024), FLOAT),
            shape((16, PAIR), FLOAT),
            shape((rows, 1024), HALF),
            shape((rows, 1024), HALF),
            shape((group, 256), HALF),
            shape((keys, 128), HALF),
            shape((group, 128), HALF),
            shape((8, rows, 128), HALF),
            shape((8, PAIR), FLOAT),
            shape((rows, 1024), FLOAT),
            shape((group, 128), HALF),
        ),
        in_specs=[anywhere, anywhere, vmem, vmem, pl.BlockSpec(memory_space=pltpu.SMEM), vmem],
        out_specs=(anywhere, anywhere) + (vmem,) * 11,
        scratch_shapes=[
            pltpu.VMEM(places + (SHARD, 768), HALF),
            pltpu.VMEM(places + (16, 128), HALF),
            pltpu.VMEM((8, rows, 256), HALF),
            pltpu.VMEM((8, mem_rows, 128), HALF),
            pltpu.VMEM((8, rows, 128), HALF),
            pltpu.VMEM((tiles, TILE, HDIM), HALF),
            pltpu.VMEM((tiles, HDIM, TILE), HALF),
            pltpu.VMEM((tiles, TILE, PAIR), FLOAT),
            pltpu.SemaphoreType.DMA((3,)),
        ]
        + flow_sems(3, 2) + flow_sems(3, 2) + flow_sems(1, 1)
        + trade_sems() * 4,
        compiler_params=pltpu.CompilerParams(
            collective_id=0, has_side_effects=True, vmem_limit_bytes=56 * 2**20
        ),
    )(packed, small, tokens, memory, doc_lens, buckets)


def middle_kernel(
    o2_ref, x1_ref, cot_ref, gain_ref, wa_ref, wf_ref,
    o2r_ref, mixed_ref, h3_ref, hid_ref, dgu_ref, g2_ref, do_ref, dnorm_ref,
    w_out, w_ff, send_do, out_acc, in_acc, load_sem, ff_sem, *sems,
):
    me = lax.axis_index("hid")
    rows = x1_ref.shape[0]
    barrier = greet_hid()
    load = pltpu.make_async_copy(wa_ref.at[:, :, pl.ds(640, 128)], w_out, load_sem)
    load.start()

    def fetch(j):
        slot = lax.rem(j, 2)
        return pltpu.make_async_copy(wf_ref.at[j], w_ff.at[slot], ff_sem.at[slot])

    fetch(0).start()
    o2_trade = Trade(
        lambda j: o2_ref.at[rows_at(j, rows)], lambda j: o2r_ref.at[j], sems[0:2]
    )
    do_trade = Trade(
        lambda j: send_do.at[j], lambda j: do_ref.at[rows_at(j, rows)], sems[2:4]
    )
    o2r_ref[me] = o2_ref[rows_at(me, rows), :]
    pl.semaphore_wait(barrier, 7)
    o2_trade.start_all()
    load.wait()
    o2_trade.arrived()
    x_two = x1_ref[...]
    for pair in range(4):
        left = jnp.concatenate([o2r_ref[2 * pair], o2r_ref[2 * pair + 1]], axis=1)
        right = jnp.concatenate([w_out[2 * pair], w_out[2 * pair + 1]], axis=1)
        x_two = x_two + dot_nt(left, right)
    out_acc[...] = x_two
    g2_ref[...] = x_two
    in_acc[...] = jnp.zeros_like(in_acc)
    h3_ref[...] = (x_two * scale_of(x_two) * gain_ref[2:3, :]).astype(HALF)

    @pl.loop(0, 8)
    def one_block(j):
        @pl.when(j < 7)
        def _():
            fetch(j + 1).start()

        fetch(j).wait()
        slot = lax.rem(j, 2)
        gate_up = dot(h3_ref[...], w_ff[slot, :, 0:768])
        gate, up = gate_up[:, :FF_PAD], gate_up[:, FF_PAD:]
        d_hidden = dot(cot_ref[...], w_ff[slot, :, 768:1152])
        curve = 0.7978845608028654 * (gate + 0.044715 * gate * gate * gate)
        bend = jnp.tanh(curve)
        gelu = 0.5 * gate * (1.0 + bend)
        slope = 0.5 * (1.0 + bend) + 0.5 * gate * (1.0 - bend * bend) * (
            0.7978845608028654 * (1.0 + 3.0 * 0.044715 * gate * gate)
        )
        hidden = (gelu * up).astype(HALF)
        hid_ref[j] = hidden
        d_both = jnp.concatenate([d_hidden * up * slope, d_hidden * gelu], axis=1).astype(HALF)
        dgu_ref[j] = d_both
        out_acc[...] += dot_nt(hidden, w_ff[slot, :, 768:1152])
        in_acc[...] += dot_nt(d_both, w_ff[slot, :, 0:768])

    mixed_ref[...] = out_acc[...].astype(HALF)
    d_inner, d_gain = norm_backward(g2_ref[...], gain_ref[2:3, :], in_acc[...])
    dnorm_ref[...] = d_gain
    g_two = cot_ref[...].astype(FLOAT) + d_inner
    g2_ref[...] = g_two
    in_acc[...] = g_two

    def one(step, j, remote):
        value = dot(in_acc[...].astype(HALF), w_out[j]).astype(HALF)

        @pl.when(remote)
        def _():
            send_do[j] = value
            do_trade.start(step)

        @pl.when(jnp.logical_not(remote))
        def _():
            do_ref[rows_at(me, rows), :] = value

    each_target(one)
    do_trade.arrived()
    o2_trade.finish()
    do_trade.finish()


def middle(o_two, x_one, cotangent, gains, wa, wf):
    rows = x_one.shape[0]
    vmem = pl.BlockSpec(memory_space=pltpu.VMEM)
    anywhere = pl.BlockSpec(memory_space=pl.ANY)
    shape = jax.ShapeDtypeStruct
    return pl.pallas_call(
        middle_kernel,
        out_shape=(
            shape((8, rows, 128), HALF),
            shape((rows, 1024), HALF),
            shape((rows, 1024), HALF),
            shape((8, rows, FF_PAD), HALF),
            shape((8, rows, 2 * FF_PAD), HALF),
            shape((rows, 1024), FLOAT),
            shape((rows * 8, 128), HALF),
            shape((1, 1024), FLOAT),
        ),
        in_specs=[vmem] * 4 + [anywhere] * 2,
        out_specs=(vmem,) * 8,
        scratch_shapes=[
            pltpu.VMEM((8, 1024, 128), HALF),
            pltpu.VMEM((2, 1024, 1152), HALF),
            pltpu.VMEM((8, rows, 128), HALF),
            pltpu.VMEM((rows, 1024), FLOAT),
            pltpu.VMEM((rows, 1024), FLOAT),
            pltpu.SemaphoreType.DMA,
            pltpu.SemaphoreType.DMA((2,)),
        ]
        + trade_sems() * 2,
        compiler_params=pltpu.CompilerParams(
            collective_id=2, has_side_effects=True, vmem_limit_bytes=56 * 2**20
        ),
    )(o_two, x_one, cotangent, gains, wa, wf)


def scatter_kernel(
    g_ref, out_ref, acc, core_in, *rest
):
    buffers = rest[:18]
    core_send, core_recv, load_sem, send_sem, recv_sem = rest[18:]
    torus = Torus()
    barrier = torus.greet()
    pl.semaphore_wait(barrier, 7)

    def add_blocks(place, whole, rows, cut, sources):
        dims = whole_dims(whole)
        count = 1
        for dim in dims:
            count *= dim

        def one(step):
            index, rest_of = [], step
            for dim in reversed(dims):
                index.append(lax.rem(rest_of, dim))
                rest_of = rest_of // dim
            index = index[::-1]
            left = iter(index)
            at = tuple(
                next(left) if isinstance(entry, slice) else entry
                for entry in block_index(place, whole)
            )
            where = at + (pl.ds(*rows), pl.ds(*cut))
            total = acc[where].astype(FLOAT)
            for source in sources:
                total = total + source(at, tuple(index)).astype(FLOAT)
            acc[where] = total.astype(acc.dtype)

        if count == 1:
            one(jnp.int32(0))
        else:
            pl.loop(0, count)(one)

    core_copies = {}
    for step in (2, 1, -1, 0):
        for part, cut in enumerate(CUTS):
            axis, whole = ORDERS[part][2], ORDERS[part][:2]
            at = block_index(torus.moved(axis, step), whole)
            cols = (slice(None), pl.ds(*cut))
            number = len(core_copies)
            remote = pltpu.make_async_remote_copy(
                src_ref=g_ref.at[at + (1 - torus.core,) + cols],
                dst_ref=core_in.at[at + cols],
                send_sem=core_send.at[number],
                recv_sem=core_recv.at[number],
                device_id=torus.sibling(),
                device_id_type=MESH,
            )
            remote.start()
            here = pltpu.make_async_copy(
                g_ref.at[at + (torus.core,) + cols], acc.at[at + cols], load_sem.at[number]
            )
            here.start()
            core_copies[step, part] = (remote, here)

    def core_sum(step, part):
        remote, here = core_copies[step, part]
        remote.wait_recv()
        here.wait()
        axis, whole, cut = ORDERS[part][2], ORDERS[part][:2], CUTS[part]
        add_blocks(
            torus.moved(axis, step), whole, (0, SHARD), cut,
            [lambda at, index: core_in[at + (slice(None), pl.ds(*cut))]],
        )

    sends = []

    def send(src, dst, target):
        at = len(sends)
        copy = pltpu.make_async_remote_copy(
            src_ref=src, dst_ref=dst, send_sem=send_sem.at[at], recv_sem=recv_sem.at[at],
            device_id=target, device_id_type=MESH,
        )
        copy.start()
        sends.append(copy)
        return copy

    def view(place, whole, rows, cut):
        return acc.at[block_index(place, whole) + (pl.ds(*rows), pl.ds(*cut))]

    def landed(buffer, slot):
        return lambda at, index: buffer[(slot,) + index]

    for stage in (2, 1, 0):
        far, near = [], []
        for part, cut in enumerate(CUTS):
            if stage == 2:
                core_sum(2, part)
            axis, whole = ORDERS[part][stage], ORDERS[part][:stage]
            buffer = buffers[(stage * 3 + part) * 2]
            across = torus.moved(axis, 2)
            far.append((
                send(view(across, whole, (0, 32), cut), buffer.at[0], torus.neighbour(axis, 1)),
                send(view(across, whole, (32, 32), cut), buffer.at[1], torus.neighbour(axis, -1)),
            ))
        for part, cut in enumerate(CUTS):
            if stage == 2:
                core_sum(1, part)
                core_sum(-1, part)
            axis, whole = ORDERS[part][stage], ORDERS[part][:stage]
            got, last = buffers[(stage * 3 + part) * 2 : (stage * 3 + part) * 2 + 2]
            pair = []
            for slot, step, rows in ((0, 1, (0, 32)), (1, -1, (32, 32))):
                place = torus.moved(axis, step)
                far[part][slot].wait_recv()
                add_blocks(place, whole, rows, cut, [landed(got, slot)])
                pair.append(
                    send(view(place, whole, (0, SHARD), cut), last.at[slot], torus.neighbour(axis, step))
                )
            near.append(pair)
        for part, cut in enumerate(CUTS):
            if stage == 2:
                core_sum(0, part)
            whole = ORDERS[part][:stage]
            last = buffers[(stage * 3 + part) * 2 + 1]
            near[part][0].wait_recv()
            near[part][1].wait_recv()
            if stage > 0:
                add_blocks(torus.pos, whole, (0, SHARD), cut, [landed(last, 0), landed(last, 1)])
            else:
                mine = acc[block_index(torus.pos, "") + (slice(None), pl.ds(*cut))]
                out_ref[:, pl.ds(*cut)] = (
                    mine.astype(FLOAT) + last[0].astype(FLOAT) + last[1].astype(FLOAT)
                )
    for copy in sends:
        copy.wait_send()
    for remote, _ in core_copies.values():
        remote.wait_send()


def scatter_grads(grads):
    scratch = [pltpu.VMEM((4, 2, 4, 2, SHARD, WIDTH), HALF)] * 2
    for stage in range(3):
        for part, cut in enumerate(CUTS):
            dims = whole_dims(ORDERS[part][:stage])
            scratch.append(pltpu.VMEM((2,) + dims + (32, cut[1]), HALF))
            scratch.append(pltpu.VMEM((2,) + dims + (SHARD, cut[1]), HALF))
    scratch += [pltpu.SemaphoreType.DMA((12,))] * 3 + [pltpu.SemaphoreType.DMA((36,))] * 2
    return pl.pallas_call(
        scatter_kernel,
        out_shape=jax.ShapeDtypeStruct((SHARD, WIDTH), FLOAT),
        in_specs=[pl.BlockSpec(memory_space=pl.ANY)],
        out_specs=pl.BlockSpec(memory_space=pltpu.VMEM),
        scratch_shapes=scratch,
        compiler_params=pltpu.CompilerParams(
            collective_id=1, has_side_effects=True, vmem_limit_bytes=60 * 2**20
        ),
    )(grads.reshape(4, 2, 4, 2, 2, SHARD, WIDTH))


def exchange_kernel(src_ref, dst_ref, send_sem, recv_sem, own_sem):
    me = lax.axis_index("hid")
    tok = lax.axis_index("tok")
    barrier = pltpu.get_barrier_semaphore()
    for step in range(1, 8):
        pl.semaphore_signal(
            barrier, inc=1, device_id=(tok, lax.rem(me + step, 8)), device_id_type=MESH
        )
    own = pltpu.make_async_copy(src_ref.at[me], dst_ref.at[me], own_sem)
    own.start()
    pl.semaphore_wait(barrier, 7)
    copies = []
    for step in range(1, 8):
        target = lax.rem(me + step, 8)
        copy = pltpu.make_async_remote_copy(
            src_ref=src_ref.at[target], dst_ref=dst_ref.at[me],
            send_sem=send_sem.at[step - 1], recv_sem=recv_sem.at[step - 1],
            device_id=(tok, target), device_id_type=MESH,
        )
        copy.start()
        copies.append(copy)
    own.wait()
    for copy in copies:
        copy.wait()


def exchange(blocks, number):
    return pl.pallas_call(
        exchange_kernel,
        out_shape=jax.ShapeDtypeStruct(blocks.shape, blocks.dtype),
        in_specs=[pl.BlockSpec(memory_space=pl.ANY)],
        out_specs=pl.BlockSpec(memory_space=pl.ANY),
        scratch_shapes=[
            pltpu.SemaphoreType.DMA((7,)),
            pltpu.SemaphoreType.DMA((7,)),
            pltpu.SemaphoreType.DMA,
        ],
        compiler_params=pltpu.CompilerParams(collective_id=number, has_side_effects=True),
    )(blocks)


def weight_grad_kernel(
    h1_ref, g1_ref, h2_ref, mem_ref, g2_ref, h3_ref, cot_ref,
    dqkv_ref, o1_ref, dq2_ref, dkv2_ref, o2_ref, dgu_ref, hid_ref, pad_ref,
    out_ref,
):
    def put(at, left, right):
        value = dot(left[...], right[0])
        out_ref[0, :, at : at + value.shape[1]] = value.astype(HALF)

    put(0, h1_ref, dqkv_ref)
    put(256, g1_ref, o1_ref)
    put(384, h2_ref, dq2_ref)
    put(512, mem_ref, dkv2_ref)
    put(640, g2_ref, o2_ref)
    put(768, h3_ref, dgu_ref)
    value = dot(cot_ref[...], hid_ref[0])
    out_ref[0, :, 1536:1792] = value[:, :256].astype(HALF)
    out_ref[0, :, 1792:1920] = (value[:, 256:] + pad_ref[0]).astype(HALF)


def weight_grads(lefts, rights, pads):
    return pl.pallas_call(
        weight_grad_kernel,
        grid=(8,),
        out_shape=jax.ShapeDtypeStruct((8, 1024, WIDTH), HALF),
        in_specs=[pl.BlockSpec(left.shape, lambda j: (0, 0)) for left in lefts]
        + [
            pl.BlockSpec((1,) + right.shape[1:], lambda j: (j, 0, 0))
            for right in rights + [pads]
        ],
        out_specs=pl.BlockSpec((1, 1024, WIDTH), lambda j: (j, 0, 0)),
        compiler_params=pltpu.CompilerParams(vmem_limit_bytes=56 * 2**20),
    )(*lefts, *rights, pads)


def rms_norm(row_vals, gain_vec):
    return (
        row_vals * lax.rsqrt(jnp.mean(row_vals * row_vals, axis=-1, keepdims=True) + EPS) * gain_vec
    )


def norm_back(row_vals, gain_vec, gradient):
    _, pullback = jax.vjp(rms_norm, row_vals, gain_vec)
    return pullback(gradient)


def spread_cols(rows, weights):
    return jnp.einsum("rd,jdc->jrc", rows, weights, preferred_element_type=FLOAT)


def join_cols(blocks, weights):
    return jnp.einsum("jrc,jdc->rd", blocks, weights, preferred_element_type=FLOAT)


def from_windows(sums):
    sums = sums.reshape(-1, 2, PAIR)
    tail = jnp.concatenate([sums[1:, :, TILE:], jnp.zeros((1, 2, TILE), FLOAT)], axis=0)
    return (sums[:, :, :TILE] + tail).transpose(1, 0, 2).reshape(2, -1)


def local(
    tokens, memory, cotangent, norm1, w_query, w_key, w_value, w_out, rel_bias, norm2,
    cross_query, cross_key, cross_value, cross_out, norm3, w_gate, w_up, w_down,
    doc_lengths, memory_slot, enc_lengths, rel_bucket,
):
    widen = ((0, 0), (0, FF_PAD - w_gate.shape[1]))
    core = lax.rem(lax.axis_index("tok"), 2)
    hid = lax.axis_index("hid")
    packed = jnp.concatenate(
        [
            w_query, w_key, w_value, w_out.T, cross_query, cross_key, cross_value, cross_out.T,
            jnp.pad(w_gate, widen), jnp.pad(w_up, widen), jnp.pad(w_down.T, widen),
        ],
        axis=1,
    )
    norms = jnp.stack([norm1, norm2, norm3])
    blank = jnp.zeros_like(norms)
    norms = jnp.where(
        core == 0,
        jnp.concatenate([norms, blank], axis=1),
        jnp.concatenate([blank, norms], axis=1),
    )
    small = jnp.concatenate(
        [norms, jnp.broadcast_to(rel_bias.reshape(4, 1), (4, 128)), jnp.zeros((9, 128), HALF)]
    )
    tile_buckets = rel_bucket.reshape(-1, TILE)
    before = jnp.concatenate([tile_buckets[:1], tile_buckets[:-1]])
    buckets = jnp.pad(jnp.concatenate([tile_buckets, before], axis=1), ((0, 2), (0, 0)))
    (
        wf, wa, gains, windows, h_one, h_two, qkv, kv_two, o_one, o_one_rows, lse_one, x_one, q_two
    ) = forward(packed, small, tokens, memory, doc_lengths, buckets)
    wa = wa.reshape(8, 16 * SHARD, 768)
    wf = wf.reshape(8, 16 * SHARD, 1152)
    gain_one, gain_two = gains[0], gains[1]
    onehot = (
        rel_bucket[:, None] == jnp.arange(32, dtype=jnp.int32)[None, :]
    ).astype(FLOAT)
    w_qkv, w_o1, w_q2, w_kv2 = (
        wa[:, :, 0:256], wa[:, :, 256:384], wa[:, :, 384:512], wa[:, :, 512:640]
    )
    rows = tokens.shape[0]
    group_rows = rows * 8
    residual = tokens.astype(FLOAT)
    o_two, lse_two = cross_forward(doc_lengths, memory_slot, enc_lengths, q_two, kv_two)
    o_two_rows, mixed, h_three, hidden, d_gate_up, d_rows, d_out, d_norm3 = middle(
        o_two, x_one, cotangent, gains, wa, wf
    )
    d_norm3 = d_norm3[0]
    g_two = d_rows.astype(HALF)
    dq_two, dkv_two = cross_backward(
        doc_lengths, memory_slot, enc_lengths, q_two, kv_two, d_out, o_two, lse_two
    )
    dq_two = exchange(dq_two.reshape(8, rows, 128), 8)
    dkv_two = exchange(dkv_two.reshape(8, -1, 128), 9)
    d_memory = join_cols(dkv_two, w_kv2)
    d_inner, d_norm2 = norm_back(x_one, gain_two, join_cols(dq_two, w_q2))
    d_rows = d_rows + d_inner
    g_one = d_rows.astype(HALF)
    d_out = exchange(spread_cols(g_one, w_o1).astype(HALF), 10).reshape(group_rows, 128)
    dqkv, diagonals = self_backward(doc_lengths, qkv, windows, d_out, o_one, lse_one)
    dqkv = exchange(dqkv.reshape(8, rows, 256), 11)
    d_inner, d_norm1 = norm_back(residual, gain_one, join_cols(dqkv, w_qkv))
    d_tokens = d_rows + d_inner

    d_table = jnp.dot(onehot.T, from_windows(diagonals).T, precision=HIGH)
    d_table = jnp.pad(d_table.reshape(16, 2, 2), ((0, 0), (0, SHARD - 2), (0, 0)))
    d_table = d_table.reshape(1, 16 * SHARD, 2)
    owned = (jnp.arange(8, dtype=jnp.int32) == hid)[:, None, None]
    norms = jnp.stack([d_norm1, d_norm2, d_norm3], axis=1)
    pads = jnp.concatenate(
        [
            jnp.broadcast_to(norms[None], (8,) + norms.shape),
            jnp.where(owned, d_table, 0.0),
        ],
        axis=2,
    )
    pads = jnp.pad(pads, ((0, 0), (0, 0), (96, 27)))
    grads = weight_grads(
        [
            left.T for left in (h_one, g_one, h_two, memory, g_two, h_three, cotangent)
        ],
        [
            dqkv, o_one_rows, dq_two, dkv_two, o_two_rows,
            d_gate_up, hidden,
        ],
        pads,
    )
    shard = scatter_grads(grads)
    return (
        mixed,
        d_tokens,
        d_memory,
        shard[:, PAD_AT],
        shard[:, 0:128],
        shard[:, 128:192],
        shard[:, 192:256],
        shard[:, 256:384].T,
        shard[:2, PAD_AT + 3 : PAD_AT + 5],
        shard[:, PAD_AT + 1],
        shard[:, 384:512],
        shard[:, 512:576],
        shard[:, 576:640],
        shard[:, 640:768].T,
        shard[:, PAD_AT + 2],
        shard[:, 768:1120],
        shard[:, 1152:1504],
        shard[:, 1536:1888].T,
    )


def solution(mesh):
    return jax.shard_map(
        local,
        mesh=mesh,
        in_specs=(
            P(("tok", "hid"), None),
            P(("tok", "hid"), None),
            P(("tok", "hid"), None),
            P("tok"),
            P("tok", "hid"),
            P("tok", "hid"),
            P("tok", "hid"),
            P("hid", "tok"),
            P("tok", "hid"),
            P("tok"),
            P("tok", "hid"),
            P("tok", "hid"),
            P("tok", "hid"),
            P("hid", "tok"),
            P("tok"),
            P("tok", "hid"),
            P("tok", "hid"),
            P("hid", "tok"),
            P("tok", None),
            P("tok", None),
            P("tok", None),
            P(),
        ),
        out_specs=(
            P(("tok", "hid"), None),
            P(("tok", "hid"), None),
            P(("tok", "hid"), None),
            P("tok"),
            P("tok", "hid"),
            P("tok", "hid"),
            P("tok", "hid"),
            P("hid", "tok"),
            P("tok", "hid"),
            P("tok"),
            P("tok", "hid"),
            P("tok", "hid"),
            P("tok", "hid"),
            P("hid", "tok"),
            P("tok"),
            P("tok", "hid"),
            P("tok", "hid"),
            P("hid", "tok"),
        ),
        check_vma=False,
    )
```

```python
import jax
import jax.numpy as jnp
from jax import lax
from jax.experimental import pallas as pl
from jax.experimental.pallas import tpu as pltpu
from jax.sharding import PartitionSpec as P

EPS = 1e-06
HIGH = lax.Precision.HIGHEST
MESH = pl.DeviceIdType.MESH

HDIM = 64
ENC = 1024
FLOAT = jnp.float32
HALF = jnp.bfloat16
TILE = 256
PAIR = 2 * TILE
NEG = -1e30
NT_DIMS = (((1,), (1,)), ((), ()))


def dot(first, second):
    return jnp.dot(first, second, preferred_element_type=FLOAT)


def dot_nt(first, second):
    return lax.dot_general(first, second, NT_DIMS, preferred_element_type=FLOAT)


def stack_heads(block):
    return jnp.concatenate([block[:, :HDIM], block[:, HDIM:]], axis=0)


def unstack_heads(columns):
    return jnp.concatenate(
        [columns[:, :TILE].T, columns[:, TILE:].T], axis=1
    )


def tile_rows(tile):
    return pl.ds(pl.multiple_of(tile * TILE, TILE), TILE)


def lane_positions(first):
    lane = lax.broadcasted_iota(jnp.int32, (1, PAIR), 1)
    return first + jnp.where(lane >= TILE, lane - TILE, lane)


def doc_ends(len_ref):
    first_end = len_ref[0, 0]
    return first_end, first_end + len_ref[0, 1]


def start_of(position, ends):
    return jnp.where(position >= ends[1], ends[1], jnp.where(position >= ends[0], ends[0], 0))


def build_bias(win_ref, bias, tiles):
    for diag in range(tiles):
        for head in range(2):
            row = win_ref[pl.ds(head * 8 + diag, 1), :]
            spread = jnp.broadcast_to(row, (TILE, PAIR))
            rolled = pltpu.roll(spread, 0, 1, stride=1, stride_axis=0)
            bias[diag, :, pl.ds(head * TILE, TILE)] = rolled[:, :TILE]


def online(state, scores, values_t):
    peak, total, acc = state
    new_peak = jnp.maximum(peak, jnp.max(scores, axis=0, keepdims=True))
    shrink = jnp.exp(peak - new_peak)
    weights = jnp.exp(scores - new_peak)
    total = total * shrink + jnp.sum(weights, axis=0, keepdims=True)
    acc = acc * shrink + dot(values_t, weights.astype(HALF))
    return new_peak, total, acc


def fresh_state():
    return (
        jnp.full((1, PAIR), NEG, FLOAT),
        jnp.zeros((1, PAIR), FLOAT),
        jnp.zeros((HDIM, PAIR), FLOAT),
    )


def finish(state, tile, out_ref, lse_ref):
    peak, total, acc = state
    out_ref[tile_rows(tile), :] = unstack_heads(acc / total).astype(HALF)
    lse_ref[pl.ds(tile, 1), :] = peak + jnp.log(total)


def row_prepare(tiles, q_of, do_ref, o_ref, queries, grads, deltas):
    for tile in range(tiles):
        rows = slice(tile * TILE, (tile + 1) * TILE)
        queries[tile] = stack_heads(q_of(rows))
        block = do_ref[rows, :]
        grads[tile] = stack_heads(block)
        product = (block.astype(FLOAT) * o_ref[rows, :].astype(FLOAT)).T
        deltas[tile] = jnp.concatenate(
            [
                jnp.sum(product[:HDIM], axis=0, keepdims=True),
                jnp.sum(product[HDIM:], axis=0, keepdims=True),
            ],
            axis=1,
        )


def fold_diagonals(block):
    half = TILE // 2
    while half >= 8:
        block = block[:half] + pltpu.roll(block[half:], PAIR - half, 1)
        half //= 2
    total = block[0:1]
    for row in range(1, 8):
        total = total + pltpu.roll(block[row : row + 1], PAIR - row, 1)
    return total


def cross_forward_kernel(
    len_ref, slot_ref, enc_ref, q_ref, kv_ref, out_ref, lse_ref, keys, values_t
):
    tiles = q_ref.shape[0] // TILE
    key_tiles = kv_ref.shape[0] // TILE
    for tile in range(key_tiles):
        block = kv_ref[tile * TILE : (tile + 1) * TILE, :]
        keys[tile] = block[:, :HDIM]
        values_t[tile] = block[:, HDIM:].astype(FLOAT).T.astype(HALF)
    ends = doc_ends(len_ref)

    def doc_at(position):
        return (position >= ends[0]).astype(jnp.int32) + (position >= ends[1]).astype(jnp.int32)

    @pl.loop(0, tiles)
    def row_tile(tile):
        first = tile * TILE
        queries = stack_heads(q_ref[tile_rows(tile), :])
        row_doc = doc_at(lane_positions(first))

        def one_doc(doc, state):
            slot = slot_ref[0, doc]
            valid = enc_ref[0, slot]
            mine = row_doc == doc
            base = slot * (ENC // TILE)

            def key_tile(other, inner):
                scores = dot_nt(keys[base + other], queries)
                key_pos = other * TILE + lax.broadcasted_iota(jnp.int32, (TILE, 1), 0)
                scores = jnp.where(mine & (key_pos < valid), scores, NEG)
                return online(inner, scores, values_t[base + other])

            return lax.fori_loop(0, (valid + TILE - 1) // TILE, key_tile, state)

        state = lax.fori_loop(doc_at(first), doc_at(first + TILE - 1) + 1, one_doc, fresh_state())
        finish(state, tile, out_ref, lse_ref)


def cross_forward(doc_lens, slots, enc_lens, queries, kv):
    rows = queries.shape[0]
    key_tiles = kv.shape[0] // TILE
    vmem = pl.BlockSpec(memory_space=pltpu.VMEM)
    return pl.pallas_call(
        cross_forward_kernel,
        out_shape=(
            jax.ShapeDtypeStruct((rows, 128), HALF),
            jax.ShapeDtypeStruct((8, PAIR), FLOAT),
        ),
        in_specs=[pl.BlockSpec(memory_space=pltpu.SMEM)] * 3 + [vmem] * 2,
        out_specs=(vmem, vmem),
        scratch_shapes=[
            pltpu.VMEM((key_tiles, TILE, HDIM), HALF),
            pltpu.VMEM((key_tiles, HDIM, TILE), HALF),
        ],
        compiler_params=pltpu.CompilerParams(vmem_limit_bytes=48 * 2**20),
    )(doc_lens, slots, enc_lens, queries, kv)


def cross_backward_kernel(
    len_ref, slot_ref, enc_ref, q_ref, kv_ref, do_ref, o_ref, lse_ref,
    dq_ref, dkv_ref,
    keys, values, keys_t, queries, grads, deltas, dq,
):
    tiles = q_ref.shape[0] // TILE
    key_tiles = kv_ref.shape[0] // TILE
    for tile in range(key_tiles):
        block = kv_ref[tile * TILE : (tile + 1) * TILE, :]
        keys[tile] = block[:, :HDIM]
        values[tile] = block[:, HDIM:]
        keys_t[tile] = block[:, :HDIM].astype(FLOAT).T.astype(HALF)
    row_prepare(tiles, lambda rows: q_ref[rows, :], do_ref, o_ref, queries, grads, deltas)
    dq[...] = jnp.zeros_like(dq)
    dkv_ref[...] = jnp.zeros_like(dkv_ref)
    ends = doc_ends(len_ref)
    total_rows = q_ref.shape[0]

    @pl.loop(0, 3)
    def one_doc(doc):
        start = jnp.where(doc == 0, 0, jnp.where(doc == 1, ends[0], ends[1]))
        stop = jnp.where(doc == 0, ends[0], jnp.where(doc == 1, ends[1], total_rows))
        slot = slot_ref[0, doc]
        valid = enc_ref[0, slot]
        base = slot * (ENC // TILE)

        @pl.loop(0, (valid + TILE - 1) // TILE)
        def key_tile(other):
            key_pos = other * TILE + lax.broadcasted_iota(jnp.int32, (TILE, 1), 0)
            place = base + other

            def row_tile(tile, state):
                dk, dv = state
                row_pos = lane_positions(tile * TILE)
                scores = dot_nt(keys[place], queries[tile])
                allowed = (row_pos >= start) & (row_pos < stop) & (key_pos < valid)
                scores = jnp.where(allowed, scores, NEG)
                weights = jnp.exp(scores - lse_ref[pl.ds(tile, 1), :])
                d_weights = dot_nt(values[place], grads[tile])
                d_half = (weights * (d_weights - deltas[tile])).astype(HALF)
                dv = dv + dot(weights.astype(HALF), grads[tile])
                dk = dk + dot(d_half, queries[tile])
                dq[tile] += dot(keys_t[place], d_half)
                return dk, dv

            zero = jnp.zeros((TILE, HDIM), FLOAT)
            dk, dv = lax.fori_loop(
                start // TILE, (stop - 1) // TILE + 1, row_tile, (zero, zero)
            )
            dkv_ref[tile_rows(place), :] = jnp.concatenate([dk, dv], axis=1).astype(HALF)

    for tile in range(tiles):
        dq_ref[tile * TILE : (tile + 1) * TILE, :] = unstack_heads(dq[tile]).astype(HALF)


def cross_backward(doc_lens, slots, enc_lens, queries, kv, d_out, out, lse):
    rows = queries.shape[0]
    tiles = rows // TILE
    key_tiles = kv.shape[0] // TILE
    vmem = pl.BlockSpec(memory_space=pltpu.VMEM)
    return pl.pallas_call(
        cross_backward_kernel,
        out_shape=(
            jax.ShapeDtypeStruct((rows, 128), HALF),
            jax.ShapeDtypeStruct((kv.shape[0], 128), HALF),
        ),
        in_specs=[pl.BlockSpec(memory_space=pltpu.SMEM)] * 3 + [vmem] * 5,
        out_specs=(vmem, vmem),
        scratch_shapes=[
            pltpu.VMEM((key_tiles, TILE, HDIM), HALF),
            pltpu.VMEM((key_tiles, TILE, HDIM), HALF),
            pltpu.VMEM((key_tiles, HDIM, TILE), HALF),
            pltpu.VMEM((tiles, PAIR, HDIM), HALF),
            pltpu.VMEM((tiles, PAIR, HDIM), HALF),
            pltpu.VMEM((tiles, 1, PAIR), FLOAT),
            pltpu.VMEM((tiles, HDIM, PAIR), FLOAT),
        ],
        compiler_params=pltpu.CompilerParams(vmem_limit_bytes=48 * 2**20),
    )(doc_lens, slots, enc_lens, queries, kv, d_out, out, lse)


WIDTH = 1920
SHARD = 64
FF_PAD = 384
PAD_AT = 1536 + 352
CUTS = ((0, 640), (640, 640), (1280, 640))
ORDERS = ("zyx", "yxz", "xzy")


class Torus:
    def __init__(self):
        tok, hid = lax.axis_index("tok"), lax.axis_index("hid")
        self.core = lax.rem(tok, 2)
        self.pos = {
            "x": lax.rem(tok // 2, 2) * 2 + lax.rem(hid, 2),
            "y": tok // 4,
            "z": hid // 2,
        }

    def moved(self, axis, step):
        place = dict(self.pos)
        place[axis] = lax.rem(place[axis] + step + 4, 4)
        return place

    def device(self, place, core=None):
        core = self.core if core is None else core
        return (
            (place["y"] * 2 + place["x"] // 2) * 2 + core,
            place["z"] * 2 + lax.rem(place["x"], 2),
        )

    def neighbour(self, axis, step):
        return self.device(self.moved(axis, step))

    def sibling(self):
        return self.device(self.pos, 1 - self.core)

    def greet(self):
        barrier = pltpu.get_barrier_semaphore()
        peers = [self.neighbour(axis, step) for axis in "xyz" for step in (1, -1)]
        for peer in peers + [self.sibling()]:
            pl.semaphore_signal(barrier, inc=1, device_id=peer, device_id_type=MESH)
        return barrier


def block_index(place, whole):
    return (
        slice(None) if "z" in whole else place["z"],
        slice(None) if "x" in whole else lax.rem(place["x"], 2),
        slice(None) if "y" in whole else place["y"],
        slice(None) if "x" in whole else place["x"] // 2,
    )


def whole_dims(whole):
    dims = (4,) if "z" in whole else ()
    dims += (2,) if "x" in whole else ()
    dims += (4,) if "y" in whole else ()
    return dims + ((2,) if "x" in whole else ())


class Flow:
    def __init__(self, torus, out_ref, cuts, orders, sems):
        self.torus, self.out_ref, self.cuts, self.orders = torus, out_ref, cuts, orders
        self.sems = sems
        self.rows = out_ref.shape[5]
        self.sends, self.siblings = [], []
        self.last = {}

    def view(self, place, whole, cut, rows=None):
        rows = (0, self.rows) if rows is None else rows
        return self.out_ref.at[
            block_index(place, whole) + (self.torus.core, pl.ds(*rows), pl.ds(*cut))
        ]

    def copy(self, ref, target, first, log):
        at = len(log)
        copy = pltpu.make_async_remote_copy(
            src_ref=ref, dst_ref=ref,
            send_sem=self.sems[first].at[at], recv_sem=self.sems[first + 1].at[at],
            device_id=target, device_id_type=MESH,
        )
        copy.start()
        log.append(copy)
        return copy

    def to_sibling(self, place, whole, cut):
        self.copy(self.view(place, whole, cut), self.torus.sibling(), 2, self.siblings)

    def plan(self, stage):
        for part, cut in enumerate(self.cuts):
            yield part, cut, self.orders[part][stage], self.orders[part][:stage]

    def near(self, stage):
        torus = self.torus
        for part, cut, axis, whole in self.plan(stage):
            if stage == 0:
                self.to_sibling(torus.pos, "", cut)
            ref = self.view(torus.pos, whole, cut)
            self.last[part] = [
                self.copy(ref, torus.neighbour(axis, step), 0, self.sends) for step in (1, -1)
            ]

    def far(self, stage):
        torus, half = self.torus, self.rows // 2
        for part, cut, axis, whole in self.plan(stage):
            copies = []
            for copy, step, first in zip(self.last[part], (1, -1), (0, half)):
                origin = torus.moved(axis, -step)
                copy.wait_recv()
                if half >= 16:
                    ref = self.view(origin, whole, cut, (first, half))
                    copies.append(self.copy(ref, torus.neighbour(axis, step), 0, self.sends))
                elif step == 1:
                    ref = self.view(origin, whole, cut)
                    copies.append(self.copy(ref, torus.neighbour(axis, step), 0, self.sends))
                self.to_sibling(origin, whole, cut)
            self.last[part] = copies

    def done(self, stage):
        for part, cut, axis, whole in self.plan(stage):
            for copy in self.last[part]:
                copy.wait_recv()
            self.to_sibling(self.torus.moved(axis, 2), whole, cut)

    def arrived(self):
        for copy in self.siblings:
            copy.wait_recv()

    def finish(self):
        for copy in self.sends + self.siblings:
            copy.wait_send()


def flow_sems(parts, split):
    sends = parts * 3 * (2 + split)
    return [pltpu.SemaphoreType.DMA((sends,))] * 2 + [pltpu.SemaphoreType.DMA((parts * 10,))] * 2


class Trade:
    def __init__(self, src, land, sems):
        self.src, self.land, self.sems = src, land, sems
        self.me = lax.axis_index("hid")
        self.tok = lax.axis_index("tok")

    def copy(self, step):
        target = lax.rem(self.me + step, 8)
        return pltpu.make_async_remote_copy(
            src_ref=self.src(target), dst_ref=self.land(self.me),
            send_sem=self.sems[0].at[step - 1], recv_sem=self.sems[1].at[step - 1],
            device_id=(self.tok, target), device_id_type=MESH,
        )

    def start(self, step):
        self.copy(step).start()

    def start_all(self):
        for step in range(1, 8):
            self.start(step)

    def arrived(self):
        for step in range(1, 8):
            self.copy(step).wait_recv()

    def finish(self):
        for step in range(1, 8):
            self.copy(step).wait_send()


def trade_sems():
    return [pltpu.SemaphoreType.DMA((7,))] * 2


def greet_all(torus):
    barrier = pltpu.get_barrier_semaphore()
    tok, me = lax.axis_index("tok"), lax.axis_index("hid")
    outside = 2 * lax.rem(me, 2) - 1
    peers = [(tok, lax.rem(me + step, 8)) for step in range(1, 8)]
    peers += [torus.neighbour("y", 1), torus.neighbour("y", -1), torus.neighbour("x", outside)]
    peers += [torus.sibling()]
    for peer in peers:
        pl.semaphore_signal(barrier, inc=1, device_id=peer, device_id_type=MESH)
    return barrier, len(peers)


def greet_hid():
    barrier = pltpu.get_barrier_semaphore()
    tok, me = lax.axis_index("tok"), lax.axis_index("hid")
    for step in range(1, 8):
        pl.semaphore_signal(
            barrier, inc=1, device_id=(tok, lax.rem(me + step, 8)), device_id_type=MESH
        )
    return barrier


def rows_at(index, rows):
    return pl.ds(pl.multiple_of(index * rows, 64), rows)


def each_target(body):
    me = lax.axis_index("hid")

    @pl.loop(1, 9)
    def one(step):
        body(step, lax.rem(me + step, 8), step < 8)


def scale_of(row_vals):
    return lax.rsqrt(jnp.mean(row_vals * row_vals, axis=-1, keepdims=True) + EPS)


def norm_backward(row_vals, gain, gradient):
    scale = scale_of(row_vals)
    normal = row_vals * scale
    d_gain = jnp.sum(gradient * normal, axis=0, keepdims=True)
    weighted = gradient * gain
    inner = jnp.mean(weighted * normal, axis=-1, keepdims=True)
    return scale * (weighted - normal * inner), d_gain


def forward_kernel(
    packed_ref, small_ref, tok_ref, mem_ref, len_ref, bucket_ref,
    wf_ref, wa_ref, gain_ref, win_ref, h1_ref, h2_ref, qkv_ref, kv_ref,
    o1_ref, o1r_ref, lse_ref, x1_ref, q2_ref,
    wa, small, send_qkv, send_kv, send_q2, keys, values_t, bias, own_sem, *sems,
):
    torus = Torus()
    me = lax.axis_index("hid")
    rows, mem_rows = tok_ref.shape[0], mem_ref.shape[0]
    tiles = qkv_ref.shape[0] // TILE
    barrier, count = greet_all(torus)
    here = block_index(torus.pos, "") + (torus.core,)
    owns = [
        pltpu.make_async_copy(packed_ref.at[:, pl.ds(0, 768)], wa.at[here], own_sem.at[0]),
        pltpu.make_async_copy(packed_ref.at[:, pl.ds(768, 1152)], wf_ref.at[here], own_sem.at[1]),
        pltpu.make_async_copy(small_ref, small.at[here], own_sem.at[2]),
    ]
    for own in owns:
        own.start()
    for own in owns:
        own.wait()
    pl.semaphore_wait(barrier, count)

    cuts_a = tuple((at, 256) for at in (0, 256, 512))
    cuts_f = tuple((at, 384) for at in (0, 384, 768))
    flow_a = Flow(torus, wa, cuts_a, ORDERS, sems[0:4])
    flow_f = Flow(torus, wf_ref, cuts_f, ORDERS, sems[4:8])
    flow_s = Flow(torus, small, ((0, 128),), ORDERS, sems[8:12])
    flow_a.near(0)
    flow_s.near(0)
    flow_f.near(0)
    flow_a.far(0)
    flow_s.far(0)
    flow_f.far(0)
    for stage in (1, 2):
        flow_a.done(stage - 1)
        flow_s.done(stage - 1)
        flow_a.near(stage)
        flow_s.near(stage)
        if stage == 1:
            flow_f.done(0)
            flow_f.near(1)
        flow_a.far(stage)
        flow_s.far(stage)
        if stage == 1:
            flow_f.far(1)
    flow_s.done(2)
    flow_f.done(1)
    flow_s.arrived()
    z, xlo = torus.pos["z"], lax.rem(me, 2)
    gain_parts = []
    heads = [jnp.zeros((8, PAIR), FLOAT), jnp.zeros((8, PAIR), FLOAT)]
    buckets = bucket_ref[...]
    for pair in range(8):
        blocks = [small[z, xlo, pair // 2, pair % 2, core].astype(FLOAT) for core in range(2)]
        gain_parts.append((blocks[0] + blocks[1])[0:8])
        for core in range(2):
            for part in range(2):
                bucket = (pair * 2 + core) * 2 + part
                for head in range(2):
                    at = 3 + part * 2 + head
                    value = blocks[core][at : at + 1]
                    value = jnp.concatenate([value] * 4, axis=1)
                    heads[head] = jnp.where(buckets == bucket, value, heads[head])
    gain_ref[...] = jnp.concatenate(gain_parts, axis=1)
    win_ref[0:8] = heads[0]
    win_ref[8:16] = heads[1]
    residual = tok_ref[...].astype(FLOAT)
    h1_ref[...] = (residual * scale_of(residual) * gain_ref[0:1, :]).astype(HALF)
    build_bias(win_ref, bias, tiles)

    flow_a.done(2)
    flow_f.near(2)
    flow_a.arrived()
    keep = pltpu.make_async_copy(wa, wa_ref, own_sem.at[0])
    keep.start()

    def weights(j, first, width):
        block = wa[j // 2, lax.rem(j, 2), :, :, :, :, first : first + width]
        return block.reshape(16 * SHARD, width)

    qkv_trade = Trade(
        lambda j: send_qkv.at[j], lambda j: qkv_ref.at[rows_at(j, rows)], sems[12:14]
    )
    kv_trade = Trade(
        lambda j: send_kv.at[j], lambda j: kv_ref.at[rows_at(j, mem_rows)], sems[14:16]
    )
    o1_trade = Trade(
        lambda j: o1_ref.at[rows_at(j, rows)], lambda j: o1r_ref.at[j], sems[16:18]
    )
    q2_trade = Trade(
        lambda j: send_q2.at[j], lambda j: q2_ref.at[rows_at(j, rows)], sems[18:20]
    )

    def spread(trade, left_ref, first, width, send_ref, land_ref):
        def one(step, j, remote):
            value = dot(left_ref[...], weights(j, first, width)).astype(HALF)

            @pl.when(remote)
            def _():
                send_ref[j] = value
                trade.start(step)

            @pl.when(jnp.logical_not(remote))
            def _():
                land_ref[rows_at(me, left_ref.shape[0]), :] = value

        each_target(one)

    spread(qkv_trade, h1_ref, 0, 256, send_qkv, qkv_ref)
    spread(kv_trade, mem_ref, 512, 128, send_kv, kv_ref)
    qkv_trade.arrived()
    flow_f.far(2)

    for tile in range(tiles):
        block = qkv_ref[tile * TILE : (tile + 1) * TILE, 128:256]
        keys[tile] = block[:, :HDIM]
        values_t[tile] = block[:, HDIM:].astype(FLOAT).T.astype(HALF)
    ends = doc_ends(len_ref)

    @pl.loop(0, tiles)
    def row_tile(tile):
        queries = stack_heads(qkv_ref[tile_rows(tile), 0:128])
        row_pos = lane_positions(tile * TILE)
        row_start = start_of(row_pos, ends)

        def key_tile(other, state):
            scores = dot_nt(keys[other], queries) + bias[tile - other]
            key_pos = other * TILE + lax.broadcasted_iota(jnp.int32, (TILE, 1), 0)
            allowed = (key_pos <= row_pos) & (key_pos >= row_start)
            scores = jnp.where(allowed, scores, NEG)
            return online(state, scores, values_t[other])

        finish(lax.fori_loop(0, tile + 1, key_tile, fresh_state()), tile, o1_ref, lse_ref)

    o1_trade.start_all()
    o1r_ref[me] = o1_ref[rows_at(me, rows), :]
    o1_trade.arrived()
    total = tok_ref[...].astype(FLOAT)
    for pair in range(4):
        left = jnp.concatenate([o1r_ref[2 * pair], o1r_ref[2 * pair + 1]], axis=1)
        right = jnp.concatenate(
            [weights(2 * pair, 256, 128), weights(2 * pair + 1, 256, 128)], axis=1
        )
        total = total + dot_nt(left, right)
    x1_ref[...] = total
    h2_ref[...] = (total * scale_of(total) * gain_ref[1:2, :]).astype(HALF)
    spread(q2_trade, h2_ref, 384, 128, send_q2, q2_ref)
    flow_f.done(2)
    q2_trade.arrived()
    kv_trade.arrived()
    flow_f.arrived()
    for trade in (qkv_trade, kv_trade, o1_trade, q2_trade):
        trade.finish()
    for flow in (flow_a, flow_f, flow_s):
        flow.finish()
    keep.wait()


def forward(packed, small, tokens, memory, doc_lens, buckets):
    rows, mem_rows = tokens.shape[0], memory.shape[0]
    group, keys = rows * 8, mem_rows * 8
    tiles = group // TILE
    vmem = pl.BlockSpec(memory_space=pltpu.VMEM)
    anywhere = pl.BlockSpec(memory_space=pl.ANY)
    shape = jax.ShapeDtypeStruct
    places = (4, 2, 4, 2, 2)
    return pl.pallas_call(
        forward_kernel,
        out_shape=(
            shape(places + (SHARD, 1152), HALF),
            shape(places + (SHARD, 768), HALF),
            shape((8, 1024), FLOAT),
            shape((16, PAIR), FLOAT),
            shape((rows, 1024), HALF),
            shape((rows, 1024), HALF),
            shape((group, 256), HALF),
            shape((keys, 128), HALF),
            shape((group, 128), HALF),
            shape((8, rows, 128), HALF),
            shape((8, PAIR), FLOAT),
            shape((rows, 1024), FLOAT),
            shape((group, 128), HALF),
        ),
        in_specs=[anywhere, anywhere, vmem, vmem, pl.BlockSpec(memory_space=pltpu.SMEM), vmem],
        out_specs=(anywhere, anywhere) + (vmem,) * 11,
        scratch_shapes=[
            pltpu.VMEM(places + (SHARD, 768), HALF),
            pltpu.VMEM(places + (16, 128), HALF),
            pltpu.VMEM((8, rows, 256), HALF),
            pltpu.VMEM((8, mem_rows, 128), HALF),
            pltpu.VMEM((8, rows, 128), HALF),
            pltpu.VMEM((tiles, TILE, HDIM), HALF),
            pltpu.VMEM((tiles, HDIM, TILE), HALF),
            pltpu.VMEM((tiles, TILE, PAIR), FLOAT),
            pltpu.SemaphoreType.DMA((3,)),
        ]
        + flow_sems(3, 2) + flow_sems(3, 2) + flow_sems(1, 1)
        + trade_sems() * 4,
        compiler_params=pltpu.CompilerParams(
            collective_id=0, has_side_effects=True, vmem_limit_bytes=56 * 2**20
        ),
    )(packed, small, tokens, memory, doc_lens, buckets)


def middle_kernel(
    o2_ref, x1_ref, cot_ref, gain_ref, wa_ref, wf_ref,
    o2r_ref, mixed_ref, g2_ref, do_ref, dnorm_ref, yff_ref, xt3_ref, xtc_ref,
    h3, y_stage, xs3, xsc, w_out, w_ff, send_do, out_acc, in_acc, load_sem, ff_sem, y_sem, *sems,
):
    torus = Torus()
    me = lax.axis_index("hid")
    rows = x1_ref.shape[0]
    barrier = greet_hid()
    pl.semaphore_signal(barrier, inc=1, device_id=torus.sibling(), device_id_type=MESH)
    pairs = Pairs(torus, sems[4:6])
    load = pltpu.make_async_copy(wa_ref.at[:, :, pl.ds(640, 128)], w_out, load_sem)
    load.start()

    def fetch(j):
        slot = lax.rem(j, 2)
        return pltpu.make_async_copy(wf_ref.at[j], w_ff.at[slot], ff_sem.at[slot])

    fetch(0).start()
    o2_trade = Trade(
        lambda j: o2_ref.at[rows_at(j, rows)], lambda j: o2r_ref.at[j], sems[0:2]
    )
    do_trade = Trade(
        lambda j: send_do.at[j], lambda j: do_ref.at[rows_at(j, rows)], sems[2:4]
    )
    o2r_ref[me] = o2_ref[rows_at(me, rows), :]
    split_columns(torus, cot_ref[...].astype(FLOAT), xtc_ref.at[0], xsc)
    pl.semaphore_wait(barrier, 8)
    o2_trade.start_all()
    copies = [pairs.send(lambda: xsc, lambda: xtc_ref.at[1])]
    load.wait()
    o2_trade.arrived()
    x_two = x1_ref[...]
    for pair in range(4):
        left = jnp.concatenate([o2r_ref[2 * pair], o2r_ref[2 * pair + 1]], axis=1)
        right = jnp.concatenate([w_out[2 * pair], w_out[2 * pair + 1]], axis=1)
        x_two = x_two + dot_nt(left, right)
    out_acc[...] = x_two
    g2_ref[...] = x_two
    in_acc[...] = jnp.zeros_like(in_acc)
    h3[...] = (x_two * scale_of(x_two) * gain_ref[2:3, :]).astype(HALF)
    split_columns(torus, h3[...].astype(FLOAT), xt3_ref.at[0], xs3)
    copies.append(pairs.send(lambda: xs3, lambda: xt3_ref.at[1]))

    def keep(j):
        return pltpu.make_async_copy(
            y_stage.at[j], yff_ref.at[j, pl.ds(0, rows)], y_sem.at[0, j]
        )

    def share(j):
        return pltpu.make_async_remote_copy(
            src_ref=y_stage.at[j], dst_ref=yff_ref.at[j, pl.ds(rows, rows)],
            send_sem=y_sem.at[1, j], recv_sem=y_sem.at[2, j],
            device_id=torus.sibling(), device_id_type=MESH,
        )

    @pl.loop(0, 8)
    def one_block(j):
        @pl.when(j < 7)
        def _():
            fetch(j + 1).start()

        fetch(j).wait()
        slot = lax.rem(j, 2)
        gate_up = dot(h3[...], w_ff[slot, :, 0:768])
        gate, up = gate_up[:, :FF_PAD], gate_up[:, FF_PAD:]
        d_hidden = dot(cot_ref[...], w_ff[slot, :, 768:1152])
        curve = 0.7978845608028654 * (gate + 0.044715 * gate * gate * gate)
        bend = jnp.tanh(curve)
        gelu = 0.5 * gate * (1.0 + bend)
        slope = 0.5 * (1.0 + bend) + 0.5 * gate * (1.0 - bend * bend) * (
            0.7978845608028654 * (1.0 + 3.0 * 0.044715 * gate * gate)
        )
        hidden = (gelu * up).astype(HALF)
        y_stage[j, :, 768:1152] = hidden
        d_both = jnp.concatenate([d_hidden * up * slope, d_hidden * gelu], axis=1).astype(HALF)
        y_stage[j, :, 0:768] = d_both
        keep(j).start()
        share(j).start()
        out_acc[...] += dot_nt(hidden, w_ff[slot, :, 768:1152])
        in_acc[...] += dot_nt(d_both, w_ff[slot, :, 0:768])

    mixed_ref[...] = out_acc[...].astype(HALF)
    d_inner, d_gain = norm_backward(g2_ref[...], gain_ref[2:3, :], in_acc[...])
    dnorm_ref[...] = d_gain
    g_two = cot_ref[...].astype(FLOAT) + d_inner
    g2_ref[...] = g_two
    in_acc[...] = g_two

    def one(step, j, remote):
        value = dot(in_acc[...].astype(HALF), w_out[j]).astype(HALF)

        @pl.when(remote)
        def _():
            send_do[j] = value
            do_trade.start(step)

        @pl.when(jnp.logical_not(remote))
        def _():
            do_ref[rows_at(me, rows), :] = value

    each_target(one)
    do_trade.arrived()
    o2_trade.finish()
    do_trade.finish()
    for copy in copies:
        copy.wait_recv()
    pairs.finish()

    @pl.loop(0, 8)
    def settle(j):
        keep(j).wait()
        share(j).wait()


def middle(o_two, x_one, cotangent, gains, wa, wf):
    rows = x_one.shape[0]
    vmem = pl.BlockSpec(memory_space=pltpu.VMEM)
    anywhere = pl.BlockSpec(memory_space=pl.ANY)
    shape = jax.ShapeDtypeStruct
    return pl.pallas_call(
        middle_kernel,
        out_shape=(
            shape((8, rows, 128), HALF),
            shape((rows, 1024), HALF),
            shape((rows, 1024), FLOAT),
            shape((rows * 8, 128), HALF),
            shape((1, 1024), FLOAT),
            shape((8, 2 * rows, 3 * FF_PAD), HALF),
            shape((2, 4, 2, SHARD, rows), HALF),
            shape((2, 4, 2, SHARD, rows), HALF),
        ),
        in_specs=[vmem] * 4 + [anywhere] * 2,
        out_specs=(vmem,) * 5 + (anywhere, vmem, vmem),
        scratch_shapes=[
            pltpu.VMEM((rows, 1024), HALF),
            pltpu.VMEM((8, rows, 3 * FF_PAD), HALF),
            pltpu.VMEM((4, 2, SHARD, rows), HALF),
            pltpu.VMEM((4, 2, SHARD, rows), HALF),
            pltpu.VMEM((8, 1024, 128), HALF),
            pltpu.VMEM((2, 1024, 1152), HALF),
            pltpu.VMEM((8, rows, 128), HALF),
            pltpu.VMEM((rows, 1024), FLOAT),
            pltpu.VMEM((rows, 1024), FLOAT),
            pltpu.SemaphoreType.DMA,
            pltpu.SemaphoreType.DMA((2,)),
            pltpu.SemaphoreType.DMA((3, 8)),
        ]
        + trade_sems() * 2
        + [pltpu.SemaphoreType.DMA((2,))] * 2,
        compiler_params=pltpu.CompilerParams(
            collective_id=2, has_side_effects=True, vmem_limit_bytes=56 * 2**20
        ),
    )(o_two, x_one, cotangent, gains, wa, wf)


class Remote:
    def __init__(self, src, dst, sems, at, target):
        self.src, self.dst, self.sems, self.at, self.target = src, dst, sems, at, target

    def copy(self):
        return pltpu.make_async_remote_copy(
            src_ref=self.src(), dst_ref=self.dst(),
            send_sem=self.sems[0].at[self.at], recv_sem=self.sems[1].at[self.at],
            device_id=self.target(), device_id_type=MESH,
        )

    def start(self):
        self.copy().start()

    def wait_recv(self):
        self.copy().wait_recv()

    def wait_send(self):
        self.copy().wait_send()


class Drain:
    def __init__(self, torus, acc, out_ref, cuts, orders, halves, fill, buffers, sems):
        self.torus, self.acc, self.out_ref, self.fill = torus, acc, out_ref, fill
        self.cuts, self.orders, self.halves = cuts, orders, halves
        self.buffers, self.sems = buffers, sems
        self.rows = (0, acc.shape[4])
        self.sends, self.last = [], {}

    def plan(self, stage):
        for part, cut in enumerate(self.cuts):
            first = (stage * len(self.cuts) + part) * 2
            got, final = self.buffers[first : first + 2]
            yield part, cut, self.orders[part][stage], self.orders[part][:stage], got, final

    def view(self, place, whole, rows, cut):
        return self.acc.at[block_index(place, whole) + (pl.ds(*rows), pl.ds(*cut))]

    def send(self, axis, hops, step, whole, rows, cut, buffer, slot):
        copy = Remote(
            lambda: self.view(self.torus.moved(axis, hops), whole, rows, cut),
            lambda: buffer.at[slot],
            self.sems, len(self.sends),
            lambda: self.torus.neighbour(axis, step),
        )
        copy.start()
        self.sends.append(copy)
        return copy

    def add(self, place, whole, rows, cut, sources):
        dims = whole_dims(whole)
        count = 1
        for dim in dims:
            count *= dim

        def one(step):
            index, rest_of = [], step
            for dim in reversed(dims):
                index.append(lax.rem(rest_of, dim))
                rest_of = rest_of // dim
            index = index[::-1]
            left = iter(index)
            at = tuple(
                next(left) if isinstance(entry, slice) else entry
                for entry in block_index(place, whole)
            )
            where = at + (pl.ds(*rows), pl.ds(*cut))
            total = self.acc[where].astype(FLOAT)
            for buffer, slot in sources:
                total = total + buffer[(slot,) + tuple(index)].astype(FLOAT)
            self.acc[where] = total.astype(self.acc.dtype)

        if count == 1:
            one(jnp.int32(0))
        else:
            pl.loop(0, count)(one)

    def begin(self, stage):
        torus = self.torus
        for part, cut, axis, whole, got, _ in self.plan(stage):
            across = torus.moved(axis, 2)
            if stage == 2:
                self.fill(part, across, axis)
            self.last[part] = [
                self.send(axis, 2, 1 - 2 * slot, whole, rows, cut, got, slot)
                for slot, rows in enumerate(self.halves)
            ]

    def fill_rest(self):
        for part, cut, axis, whole, _, _ in self.plan(2):
            for step in (1, -1, 0):
                self.fill(part, self.torus.moved(axis, step), axis)

    def turn(self, stage):
        torus = self.torus
        for part, cut, axis, whole, got, final in self.plan(stage):
            copies = []
            for slot, step in enumerate((1, -1)):
                place = torus.moved(axis, step)
                if slot < len(self.halves):
                    self.last[part][slot].wait_recv()
                    self.add(place, whole, self.halves[slot], cut, [(got, slot)])
                copies.append(self.send(axis, step, step, whole, self.rows, cut, final, slot))
            self.last[part] = copies

    def settle(self, stage):
        for part, cut, axis, whole, _, final in self.plan(stage):
            for copy in self.last[part]:
                copy.wait_recv()
            if stage > 0:
                self.add(self.torus.pos, whole, self.rows, cut, [(final, 0), (final, 1)])
            else:
                mine = self.acc[block_index(self.torus.pos, "") + (slice(None), pl.ds(*cut))]
                self.out_ref[:, pl.ds(*cut)] = (
                    mine.astype(FLOAT) + final[0].astype(FLOAT) + final[1].astype(FLOAT)
                )

    def finish(self):
        for copy in self.sends:
            copy.wait_send()


def drain_scratch(cuts, orders, halves, rows, dtype):
    width = sum(cut[1] for cut in cuts)
    scratch = [pltpu.VMEM((4, 2, 4, 2, rows, width), dtype)]
    for stage in range(3):
        for part, cut in enumerate(cuts):
            dims = whole_dims(orders[part][:stage])
            scratch.append(pltpu.VMEM((len(halves),) + dims + (halves[0][1], cut[1]), dtype))
            scratch.append(pltpu.VMEM((2,) + dims + (rows, cut[1]), dtype))
    count = len(cuts) * 3 * (2 + len(halves))
    return scratch + [pltpu.SemaphoreType.DMA((count,))] * 2


class Pairs:
    def __init__(self, torus, sems):
        self.torus, self.sems, self.log = torus, sems, []

    def send(self, src, dst):
        copy = Remote(src, dst, self.sems, len(self.log), self.torus.sibling)
        copy.start()
        self.log.append(copy)
        return copy

    def finish(self):
        for copy in self.log:
            copy.wait_send()


def split_columns(torus, value, mine_ref, other_ref):
    turned = value.T.astype(HALF).reshape(4, 2, 2, SHARD, value.shape[0])
    first = torus.core == 0
    mine_ref[...] = jnp.where(first, turned[:, :, 0], turned[:, :, 1])
    other_ref[...] = jnp.where(first, turned[:, :, 1], turned[:, :, 0])


def fill_product(acc, first, width, turned, right, place, axis):
    cols = pl.ds(first, width)

    def block(j, pick, count):
        total = None
        for side in range(2):
            left = pick(side).reshape(count, turned.shape[-1])
            value = dot(left, right(j, side))
            total = value if total is None else total + value
        return total.astype(HALF)

    if axis == "x":
        xlo, xhi = lax.rem(place["x"], 2), place["x"] // 2

        @pl.loop(0, 4)
        def one_z(z):
            value = block(z * 2 + xlo, lambda side: turned[side, :, xhi], 256)
            acc[z, xlo, :, xhi, :, cols] = value.reshape(4, SHARD, width)

    elif axis == "z":
        z = place["z"]

        @pl.loop(0, 2)
        def one_x(xlo):
            value = block(z * 2 + xlo, lambda side: turned[side], 512)
            acc[z, xlo, :, :, :, cols] = value.reshape(4, 2, SHARD, width)

    else:
        y = place["y"]

        @pl.loop(0, 8)
        def one_j(j):
            value = block(j, lambda side: turned[side, y], 128)
            acc[j // 2, lax.rem(j, 2), y, :, :, cols] = value.reshape(2, SHARD, width)


FF_CUTS = ((0, 384), (384, 384), (768, 384))
MIX_CUTS = ((0, 128), (128, 128), (256, 256))
QKV_CUTS = ((0, 128), (128, 128))
LAST_CUTS = ((0, 128),)
QKV_ORDERS = (ORDERS[0], ORDERS[2])
LAST_ORDERS = (ORDERS[1],)
HALVES = ((0, 32), (32, 32))
WHOLE = ((0, 16),)


def backward_kernel(
    dq2_ref, dkv2_ref, g2_ref, x1_ref, tok_ref, mem_ref, h1_ref, h2_ref, o1r_ref, o2r_ref,
    gain_ref, wa_ref, yff_ref, xt3_ref, xtc_ref, qkv_ref, win_ref, o1_ref, lse_ref, len_ref,
    bucket_ref, dnorm3_ref,
    dtok_ref, dmem_ref, ff_out, mix_out, qkv_out, last_out,
    *rest,
):
    rest = list(rest)

    def take(count):
        taken = rest[:count]
        del rest[:count]
        return taken

    y_o1, y_o2, y_q2, y_kv2, y_qkv = take(5)
    xt_h1, xt_h2, xt_mem, xt_g1, xt_g2 = take(5)
    xs_h1, xs_h2, xs_mem, xs_g1, xs_g2 = take(5)
    g1_half, send_do, do_ref, dqkv_ref, last_own, last_in, norms = take(7)
    ff_scratch, mix_scratch, qkv_scratch, last_scratch = take(19), take(19), take(13), take(7)
    local_sem = rest.pop(0)
    sems = rest
    ff_sems, mix_sems, qkv_sems, last_sems = sems[0:2], sems[2:4], sems[4:6], sems[6:8]
    pair_sems, trade_sem = sems[8:10], sems[10:18]

    torus = Torus()
    me = lax.axis_index("hid")
    rows, mem_rows = tok_ref.shape[0], mem_ref.shape[0]
    tiles = qkv_ref.shape[0] // TILE
    barrier, count = greet_all(torus)
    owns = [
        pltpu.make_async_copy(o1r_ref, y_o1.at[:, pl.ds(0, rows)], local_sem.at[0]),
        pltpu.make_async_copy(o2r_ref, y_o2.at[:, pl.ds(0, rows)], local_sem.at[1]),
    ]
    for own in owns:
        own.start()
    dq2_trade = Trade(
        lambda j: dq2_ref.at[rows_at(j, rows)], lambda j: y_q2.at[j, pl.ds(0, rows)],
        trade_sem[0:2],
    )
    dkv2_trade = Trade(
        lambda j: dkv2_ref.at[rows_at(j, mem_rows)], lambda j: y_kv2.at[j, pl.ds(0, mem_rows)],
        trade_sem[2:4],
    )
    do_trade = Trade(
        lambda j: send_do.at[j], lambda j: do_ref.at[rows_at(j, rows)], trade_sem[4:6]
    )
    dqkv_trade = Trade(
        lambda j: dqkv_ref.at[rows_at(j, rows)], lambda j: y_qkv.at[j, pl.ds(0, rows)],
        trade_sem[6:8],
    )
    pairs = Pairs(torus, pair_sems)

    def share(buffer, size):
        return pairs.send(
            lambda: buffer.at[:, pl.ds(0, size)], lambda: buffer.at[:, pl.ds(size, size)]
        )

    def fill_mix(part, place, axis):
        def right(ref, size):
            return lambda j, side: ref[j, side * size : (side + 1) * size, :]

        if part == 0:
            fill_product(mix_scratch[0], 0, 128, xt_g1, right(y_o1, rows), place, axis)
        elif part == 1:
            fill_product(mix_scratch[0], 128, 128, xt_h2, right(y_q2, rows), place, axis)
        else:
            fill_product(mix_scratch[0], 256, 128, xt_mem, right(y_kv2, mem_rows), place, axis)
            fill_product(mix_scratch[0], 384, 128, xt_g2, right(y_o2, rows), place, axis)

    def fill_qkv(part, place, axis):
        first = part * 128

        def right(j, side):
            return y_qkv[j, side * rows : (side + 1) * rows, first : first + 128]

        fill_product(qkv_scratch[0], first, 128, xt_h1, right, place, axis)

    drain_ff = Drain(
        torus, ff_scratch[0], ff_out, FF_CUTS, ORDERS, HALVES, None, ff_scratch[1:], ff_sems
    )
    drain_mix = Drain(
        torus, mix_scratch[0], mix_out, MIX_CUTS, ORDERS, HALVES, fill_mix, mix_scratch[1:],
        mix_sems,
    )
    drain_qkv = Drain(
        torus, qkv_scratch[0], qkv_out, QKV_CUTS, QKV_ORDERS, HALVES, fill_qkv, qkv_scratch[1:],
        qkv_sems,
    )
    drain_last = Drain(
        torus, last_scratch[0], last_out, LAST_CUTS, LAST_ORDERS, WHOLE,
        lambda part, place, axis: None, last_scratch[1:], last_sems,
    )

    y_q2[me, 0:rows] = dq2_ref[rows_at(me, rows), :]
    y_kv2[me, 0:mem_rows] = dkv2_ref[rows_at(me, mem_rows), :]
    pl.semaphore_wait(barrier, count)
    dq2_trade.start_all()
    dkv2_trade.start_all()

    def load_ff(yff):
        load = pltpu.make_async_copy(yff_ref, yff, local_sem.at[2])
        load.start()
        split_columns(torus, g2_ref[...], xt_g2.at[0], xs_g2)
        split_columns(torus, h2_ref[...].astype(FLOAT), xt_h2.at[0], xs_h2)
        load.wait()

        def fill(part, place, axis):
            first = part * 384

            def right(j, side):
                return yff[j, side * rows : (side + 1) * rows, first : first + 384]

            turned = xtc_ref if part == 2 else xt3_ref
            fill_product(ff_scratch[0], first, 384, turned, right, place, axis)

        drain_ff.fill = fill
        drain_ff.begin(2)
        drain_ff.fill_rest()

    pl.run_scoped(load_ff, pltpu.VMEM((8, 2 * rows, 1152), HALF))
    pair_g2 = pairs.send(lambda: xs_g2, lambda: xt_g2.at[1])
    pair_h2 = pairs.send(lambda: xs_h2, lambda: xt_h2.at[1])

    def inner(w_in, w_out, dmem):
        loads = [
            pltpu.make_async_copy(wa_ref.at[:, :, pl.ds(384, 256)], w_in, local_sem.at[2]),
            pltpu.make_async_copy(wa_ref.at[:, :, pl.ds(256, 128)], w_out, local_sem.at[3]),
        ]
        for load in loads:
            load.start()
        split_columns(torus, mem_ref[...].astype(FLOAT), xt_mem.at[0], xs_mem)
        split_columns(torus, h1_ref[...].astype(FLOAT), xt_h1.at[0], xs_h1)
        pair_mem = pairs.send(lambda: xs_mem, lambda: xt_mem.at[1])
        pair_h1 = pairs.send(lambda: xs_h1, lambda: xt_h1.at[1])
        for own in owns:
            own.wait()
        pair_y = [
            share(y, size) for y, size in ((y_o1, rows), (y_o2, rows))
        ]
        for load in loads:
            load.wait()
        dq2_trade.arrived()
        pair_q2 = share(y_q2, rows)
        total = jnp.zeros((rows, 1024), FLOAT)
        for pair in range(4):
            left = [y_q2[2 * pair + side, 0:rows] for side in range(2)]
            right = [w_in[2 * pair + side, :, 0:128] for side in range(2)]
            total = total + dot_nt(
                jnp.concatenate(left, axis=1), jnp.concatenate(right, axis=1)
            )
        d_inner, d_gain = norm_backward(x1_ref[...], gain_ref[1:2, :], total)
        norms[1:2, :] = d_gain
        norms[2:3, :] = dnorm3_ref[...]
        g_one = g2_ref[...] + d_inner
        dtok_ref[...] = g_one
        g1_half[...] = g_one.astype(HALF)

        def one(step, j, remote):
            value = dot(g1_half[...], w_out[j]).astype(HALF)

            @pl.when(remote)
            def _():
                send_do[j] = value
                do_trade.start(step)

            @pl.when(jnp.logical_not(remote))
            def _():
                do_ref[rows_at(me, rows), :] = value

        each_target(one)
        drain_ff.turn(2)
        split_columns(torus, dtok_ref[...], xt_g1.at[0], xs_g1)
        pair_g1 = pairs.send(lambda: xs_g1, lambda: xt_g1.at[1])
        dkv2_trade.arrived()
        pair_kv2 = share(y_kv2, mem_rows)
        for pair in range(4):
            left = [y_kv2[2 * pair + side, 0:mem_rows] for side in range(2)]
            right = [w_in[2 * pair + side, :, 128:256] for side in range(2)]
            value = dot_nt(jnp.concatenate(left, axis=1), jnp.concatenate(right, axis=1))
            dmem[...] = value if pair == 0 else dmem[...] + value
        store = pltpu.make_async_copy(dmem, dmem_ref, local_sem.at[2])
        store.start()
        for copy in [pair_g2, pair_h2, pair_mem, pair_q2, pair_g1, pair_kv2] + pair_y:
            copy.wait_recv()
        drain_mix.begin(2)
        drain_mix.fill_rest()
        pair_h1.wait_recv()
        store.wait()

    pl.run_scoped(
        inner,
        pltpu.VMEM((8, 1024, 256), HALF),
        pltpu.VMEM((8, 1024, 128), HALF),
        pltpu.VMEM((mem_rows, 1024), FLOAT),
    )
    drain_ff.settle(2)
    drain_ff.begin(1)
    do_trade.arrived()

    def self_attention(keys, values, keys_t, queries, grads, deltas, bias, bias_grad, dq):
        build_bias(win_ref, bias, tiles)
        for tile in range(tiles):
            block = qkv_ref[tile * TILE : (tile + 1) * TILE, 128:256]
            keys[tile] = block[:, :HDIM]
            values[tile] = block[:, HDIM:]
            keys_t[tile] = block[:, :HDIM].astype(FLOAT).T.astype(HALF)
        row_prepare(
            tiles, lambda at: qkv_ref[at, 0:128], do_ref, o1_ref, queries, grads, deltas
        )
        bias_grad[...] = jnp.zeros_like(bias_grad)
        dq[...] = jnp.zeros_like(dq)
        ends = doc_ends(len_ref)

        def key_tile(other):
            key_pos = other * TILE + lax.broadcasted_iota(jnp.int32, (TILE, 1), 0)

            def row_tile(tile, state):
                dk, dv = state
                row_pos = lane_positions(tile * TILE)
                row_start = start_of(row_pos, ends)
                scores = dot_nt(keys[other], queries[tile]) + bias[tile - other]
                allowed = (key_pos <= row_pos) & (key_pos >= row_start)
                scores = jnp.where(allowed, scores, NEG)
                weights = jnp.exp(scores - lse_ref[pl.ds(tile, 1), :])
                d_weights = dot_nt(values[other], grads[tile])
                d_scores = weights * (d_weights - deltas[tile])
                bias_grad[tile - other] += d_scores
                d_half = d_scores.astype(HALF)
                dv = dv + dot(weights.astype(HALF), grads[tile])
                dk = dk + dot(d_half, queries[tile])
                dq[tile] += dot(keys_t[other], d_half)
                return dk, dv

            zero = jnp.zeros((TILE, HDIM), FLOAT)
            dk, dv = lax.fori_loop(other, tiles, row_tile, (zero, zero))
            dqkv_ref[tile_rows(other), 128:256] = jnp.concatenate([dk, dv], axis=1).astype(HALF)

        pl.loop(0, 2)(key_tile)
        drain_ff.turn(1)
        drain_mix.turn(2)
        pl.loop(2, tiles)(key_tile)
        drain_ff.settle(1)
        drain_ff.begin(0)
        for tile in range(tiles):
            dqkv_ref[tile * TILE : (tile + 1) * TILE, 0:128] = unstack_heads(dq[tile]).astype(HALF)
        dqkv_trade.start_all()
        y_qkv[me, 0:rows] = dqkv_ref[rows_at(me, rows), :]
        sums = []
        for head in range(2):
            parts = []
            for tile in range(tiles):
                part = bias_grad[tile, :, head * TILE : (head + 1) * TILE]
                part = jnp.concatenate([part, jnp.zeros_like(part)], axis=1)
                parts.append(fold_diagonals(part))
            parts.append(jnp.zeros((8 - tiles, PAIR), FLOAT))
            sums.append(jnp.concatenate(parts, axis=0))
        buckets = bucket_ref[...]
        last_own[...] = jnp.zeros_like(last_own)
        for bucket in range(32):
            mask = buckets == bucket
            shard, part = bucket // 2, bucket % 2
            for head in range(2):
                picked = jnp.where(mask, sums[head], 0.0)
                value = jnp.sum(jnp.sum(picked, axis=0, keepdims=True), axis=1, keepdims=True)
                at = 3 + part * 2 + head
                last_own[shard % 2, shard // 2, at : at + 1, :] = jnp.broadcast_to(value, (1, 128))

    pl.run_scoped(
        self_attention,
        pltpu.VMEM((tiles, TILE, HDIM), HALF),
        pltpu.VMEM((tiles, TILE, HDIM), HALF),
        pltpu.VMEM((tiles, HDIM, TILE), HALF),
        pltpu.VMEM((tiles, PAIR, HDIM), HALF),
        pltpu.VMEM((tiles, PAIR, HDIM), HALF),
        pltpu.VMEM((tiles, 1, PAIR), FLOAT),
        pltpu.VMEM((tiles, TILE, PAIR), FLOAT),
        pltpu.VMEM((tiles, TILE, PAIR), FLOAT),
        pltpu.VMEM((tiles, HDIM, PAIR), FLOAT),
    )

    def first_inputs(w_in):
        load = pltpu.make_async_copy(wa_ref.at[:, :, pl.ds(0, 256)], w_in, local_sem.at[2])
        load.start()
        drain_mix.settle(2)
        drain_mix.begin(1)
        drain_ff.turn(0)
        load.wait()
        dqkv_trade.arrived()
        pair_qkv = share(y_qkv, rows)
        total = jnp.zeros((rows, 1024), FLOAT)
        for j in range(8):
            total = total + dot_nt(y_qkv[j, 0:rows], w_in[j])
        residual = tok_ref[...].astype(FLOAT)
        d_inner, d_gain = norm_backward(residual, gain_ref[0:1, :], total)
        norms[0:1, :] = d_gain
        dtok_ref[...] += d_inner
        return pair_qkv

    pair_qkv = []

    def scoped_first(w_in):
        pair_qkv.append(first_inputs(w_in))

    pl.run_scoped(scoped_first, pltpu.VMEM((8, 1024, 256), HALF))
    for pair in range(8):
        part = norms[0:3, pair * 128 : (pair + 1) * 128]
        for core in range(2):
            last_own[core, pair, 0:3, :] = part
    pair_last = pairs.send(lambda: last_own.at[1 - torus.core], lambda: last_in)
    pair_qkv[0].wait_recv()
    drain_qkv.begin(2)
    drain_qkv.fill_rest()
    drain_mix.turn(1)
    drain_ff.settle(0)
    pair_last.wait_recv()
    line = lax.broadcasted_iota(jnp.int32, (8, 16, 128), 1)
    total = last_own[torus.core] + last_in[...]
    shared = jnp.where(line < 3, total, 0.0)

    @pl.loop(0, 8)
    def one_j(j):
        value = jnp.where(j == me, total, shared)
        last_scratch[0][j // 2, lax.rem(j, 2)] = value.reshape(4, 2, 16, 128)

    drain_last.begin(2)
    drain_qkv.turn(2)
    drain_last.turn(2)
    drain_mix.settle(1)
    drain_mix.begin(0)
    drain_qkv.settle(2)
    drain_qkv.begin(1)
    drain_last.settle(2)
    drain_last.begin(1)
    drain_mix.turn(0)
    drain_qkv.turn(1)
    drain_last.turn(1)
    drain_mix.settle(0)
    drain_qkv.settle(1)
    drain_qkv.begin(0)
    drain_last.settle(1)
    drain_last.begin(0)
    drain_qkv.turn(0)
    drain_last.turn(0)
    drain_qkv.settle(0)
    drain_last.settle(0)
    for drain in (drain_ff, drain_mix, drain_qkv, drain_last):
        drain.finish()
    for trade in (dq2_trade, dkv2_trade, do_trade, dqkv_trade):
        trade.finish()
    pairs.finish()


def backward(
    dq2, dkv2, g2, x1, tokens, memory, h1, h2, o1r, o2r, gains, wa, yff, xt3, xtc, qkv, windows,
    o1, lse, doc_lens, buckets, dnorm3,
):
    rows, mem_rows = tokens.shape[0], memory.shape[0]
    group = rows * 8
    vmem = pl.BlockSpec(memory_space=pltpu.VMEM)
    smem = pl.BlockSpec(memory_space=pltpu.SMEM)
    anywhere = pl.BlockSpec(memory_space=pl.ANY)
    shape = jax.ShapeDtypeStruct
    drains = [
        drain_scratch(FF_CUTS, ORDERS, HALVES, SHARD, HALF),
        drain_scratch(MIX_CUTS, ORDERS, HALVES, SHARD, HALF),
        drain_scratch(QKV_CUTS, QKV_ORDERS, HALVES, SHARD, HALF),
        drain_scratch(LAST_CUTS, LAST_ORDERS, WHOLE, 16, FLOAT),
    ]
    scratch = [pltpu.VMEM((8, 2 * rows, 128), HALF)] * 3
    scratch += [pltpu.VMEM((8, 2 * mem_rows, 128), HALF), pltpu.VMEM((8, 2 * rows, 256), HALF)]
    counts = (rows, rows, mem_rows, rows, rows)
    scratch += [pltpu.VMEM((2, 4, 2, SHARD, size), HALF) for size in counts]
    scratch += [pltpu.VMEM((4, 2, SHARD, size), HALF) for size in counts]
    scratch += [
        pltpu.VMEM((rows, 1024), HALF),
        pltpu.VMEM((8, rows, 128), HALF),
        pltpu.VMEM((group, 128), HALF),
        pltpu.VMEM((group, 256), HALF),
        pltpu.VMEM((2, 8, 16, 128), FLOAT),
        pltpu.VMEM((8, 16, 128), FLOAT),
        pltpu.VMEM((8, 1024), FLOAT),
    ]
    for drain in drains:
        scratch += drain[:-2]
    scratch.append(pltpu.SemaphoreType.DMA((4,)))
    for drain in drains:
        scratch += drain[-2:]
    scratch += [pltpu.SemaphoreType.DMA((11,))] * 2 + trade_sems() * 4
    specs = [vmem] * 22
    for at in (8, 9, 11, 12):
        specs[at] = anywhere
    specs[19] = smem
    return pl.pallas_call(
        backward_kernel,
        out_shape=(
            shape((rows, 1024), FLOAT),
            shape((mem_rows, 1024), FLOAT),
            shape((SHARD, 1152), FLOAT),
            shape((SHARD, 512), FLOAT),
            shape((SHARD, 256), FLOAT),
            shape((16, 128), FLOAT),
        ),
        in_specs=specs,
        out_specs=(vmem, anywhere, vmem, vmem, vmem, vmem),
        scratch_shapes=scratch,
        compiler_params=pltpu.CompilerParams(
            collective_id=1, has_side_effects=True, vmem_limit_bytes=64 * 2**20
        ),
    )(
        dq2, dkv2, g2, x1, tokens, memory, h1, h2, o1r, o2r, gains, wa, yff, xt3, xtc, qkv,
        windows, o1, lse, doc_lens, buckets, dnorm3,
    )


def local(
    tokens, memory, cotangent, norm1, w_query, w_key, w_value, w_out, rel_bias, norm2,
    cross_query, cross_key, cross_value, cross_out, norm3, w_gate, w_up, w_down,
    doc_lengths, memory_slot, enc_lengths, rel_bucket,
):
    widen = ((0, 0), (0, FF_PAD - w_gate.shape[1]))
    core = lax.rem(lax.axis_index("tok"), 2)
    hid = lax.axis_index("hid")
    packed = jnp.concatenate(
        [
            w_query, w_key, w_value, w_out.T, cross_query, cross_key, cross_value, cross_out.T,
            jnp.pad(w_gate, widen), jnp.pad(w_up, widen), jnp.pad(w_down.T, widen),
        ],
        axis=1,
    )
    norms = jnp.stack([norm1, norm2, norm3])
    blank = jnp.zeros_like(norms)
    norms = jnp.where(
        core == 0,
        jnp.concatenate([norms, blank], axis=1),
        jnp.concatenate([blank, norms], axis=1),
    )
    small = jnp.concatenate(
        [norms, jnp.broadcast_to(rel_bias.reshape(4, 1), (4, 128)), jnp.zeros((9, 128), HALF)]
    )
    tile_buckets = rel_bucket.reshape(-1, TILE)
    before = jnp.concatenate([tile_buckets[:1], tile_buckets[:-1]])
    buckets = jnp.pad(jnp.concatenate([tile_buckets, before], axis=1), ((0, 2), (0, 0)))
    (
        wf, wa, gains, windows, h_one, h_two, qkv, kv_two, o_one, o_one_rows, lse_one, x_one, q_two
    ) = forward(packed, small, tokens, memory, doc_lengths, buckets)
    wa = wa.reshape(8, 16 * SHARD, 768)
    wf = wf.reshape(8, 16 * SHARD, 1152)
    o_two, lse_two = cross_forward(doc_lengths, memory_slot, enc_lengths, q_two, kv_two)
    o_two_rows, mixed, g_two, d_out, d_norm3, y_ff, xt_three, xt_cot = middle(
        o_two, x_one, cotangent, gains, wa, wf
    )
    dq_two, dkv_two = cross_backward(
        doc_lengths, memory_slot, enc_lengths, q_two, kv_two, d_out, o_two, lse_two
    )
    d_tokens, d_memory, ff, mix, qkv_grad, last = backward(
        dq_two, dkv_two, g_two, x_one, tokens, memory, h_one, h_two, o_one_rows, o_two_rows,
        gains, wa, y_ff, xt_three, xt_cot, qkv, windows, o_one, lse_one, doc_lengths, buckets,
        d_norm3,
    )
    d_norms = jnp.where(core == 0, last[:3, :SHARD], last[:3, SHARD:])
    return (
        mixed,
        d_tokens,
        d_memory,
        d_norms[0],
        qkv_grad[:, 0:128],
        qkv_grad[:, 128:192],
        qkv_grad[:, 192:256],
        mix[:, 0:128].T,
        last[3:7, 0].reshape(2, 2),
        d_norms[1],
        mix[:, 128:256],
        mix[:, 256:320],
        mix[:, 320:384],
        mix[:, 384:512].T,
        d_norms[2],
        ff[:, 0:352],
        ff[:, 384:736],
        ff[:, 768:1120].T,
    )


def solution(mesh):
    return jax.shard_map(
        local,
        mesh=mesh,
        in_specs=(
            P(("tok", "hid"), None),
            P(("tok", "hid"), None),
            P(("tok", "hid"), None),
            P("tok"),
            P("tok", "hid"),
            P("tok", "hid"),
            P("tok", "hid"),
            P("hid", "tok"),
            P("tok", "hid"),
            P("tok"),
            P("tok", "hid"),
            P("tok", "hid"),
            P("tok", "hid"),
            P("hid", "tok"),
            P("tok"),
            P("tok", "hid"),
            P("tok", "hid"),
            P("hid", "tok"),
            P("tok", None),
            P("tok", None),
            P("tok", None),
            P(),
        ),
        out_specs=(
            P(("tok", "hid"), None),
            P(("tok", "hid"), None),
            P(("tok", "hid"), None),
            P("tok"),
            P("tok", "hid"),
            P("tok", "hid"),
            P("tok", "hid"),
            P("hid", "tok"),
            P("tok", "hid"),
            P("tok"),
            P("tok", "hid"),
            P("tok", "hid"),
            P("tok", "hid"),
            P("hid", "tok"),
            P("tok"),
            P("tok", "hid"),
            P("tok", "hid"),
            P("hid", "tok"),
        ),
        check_vma=False,
    )
```

```python
import functools

import jax
import jax.numpy as jnp
from jax import lax
from jax.experimental import pallas as pl
from jax.experimental.pallas import tpu as pltpu
from jax.sharding import PartitionSpec as P

EPS = 1e-06
MESH = pl.DeviceIdType.MESH

HDIM = 64
ENC = 1024
LONG = 1024
FLOAT = jnp.float32
HALF = jnp.bfloat16
TILE = 256
PAIR = 2 * TILE
NEG = -1e30
NT_DIMS = (((1,), (1,)), ((), ()))


def dot(first, second):
    return jnp.dot(first, second, preferred_element_type=FLOAT)


def dot_nt(first, second):
    return lax.dot_general(first, second, NT_DIMS, preferred_element_type=FLOAT)


def stack_heads(block):
    return jnp.concatenate([block[:, :HDIM], block[:, HDIM:]], axis=0)


def unstack_heads(columns):
    return jnp.concatenate(
        [columns[:, :TILE].T, columns[:, TILE:].T], axis=1
    )


def tile_rows(tile):
    return pl.ds(pl.multiple_of(tile * TILE, TILE), TILE)


def lane_positions(first):
    lane = lax.broadcasted_iota(jnp.int32, (1, PAIR), 1)
    return first + jnp.where(lane >= TILE, lane - TILE, lane)


def doc_ends(len_ref):
    first_end = len_ref[0, 0]
    return first_end, first_end + len_ref[0, 1]


def start_of(position, ends):
    return jnp.where(position >= ends[1], ends[1], jnp.where(position >= ends[0], ends[0], 0))


def build_bias(win_ref, bias, tiles):
    for diag in range(tiles):
        for head in range(2):
            row = win_ref[pl.ds(head * 8 + diag, 1), :]
            spread = jnp.broadcast_to(row, (TILE, PAIR))
            rolled = pltpu.roll(spread, 0, 1, stride=1, stride_axis=0)
            bias[diag, :, pl.ds(head * TILE, TILE)] = rolled[:, :TILE]


def soft_sum(scores, values_t):
    peak = jnp.max(scores[0], axis=0, keepdims=True)
    for tile in scores[1:]:
        peak = jnp.maximum(peak, jnp.max(tile, axis=0, keepdims=True))
    total, acc = None, None
    for at, tile in enumerate(scores):
        weights = jnp.exp(tile - peak)
        part = jnp.sum(weights, axis=0, keepdims=True)
        value = dot(values_t(at), weights.astype(HALF))
        total = part if at == 0 else total + part
        acc = value if at == 0 else acc + value
    return acc / total, peak + jnp.log(total)


def row_prepare(tiles, q_of, do_ref, o_ref, queries, grads, deltas):
    for tile in range(tiles):
        rows = slice(tile * TILE, (tile + 1) * TILE)
        queries[tile] = stack_heads(q_of(rows))
        block = do_ref[rows, :]
        grads[tile] = stack_heads(block)
        product = (block.astype(FLOAT) * o_ref[rows, :].astype(FLOAT)).T
        deltas[tile] = jnp.concatenate(
            [
                jnp.sum(product[:HDIM], axis=0, keepdims=True),
                jnp.sum(product[HDIM:], axis=0, keepdims=True),
            ],
            axis=1,
        )


def fold_diagonals(block):
    half = TILE // 2
    while half >= 8:
        block = block[:half] + pltpu.roll(block[half:], PAIR - half, 1)
        half //= 2
    total = block[0:1]
    for row in range(1, 8):
        total = total + pltpu.roll(block[row : row + 1], PAIR - row, 1)
    return total


SEGMENTS = 8


def build_segments(seg_ref, len_ref, slot_ref, enc_ref, tiles):
    ends = doc_ends(len_ref)
    starts = [(ends[0], (ends[0] + TILE - 1) // TILE), (ends[1], (ends[1] + TILE - 1) // TILE + 1)]
    for tile in range(tiles):
        first = tile * TILE
        before = (ends[0] <= first).astype(jnp.int32) + (ends[1] <= first).astype(jnp.int32)
        starts.append((first, tile + before))
    points = []
    for at in range(SEGMENTS):
        point = 0
        for value, order in starts:
            point = point + jnp.where(order == at, value, 0)
        points.append(point)
    points.append(tiles * TILE)
    for at in range(SEGMENTS):
        start = points[at]
        slot = jnp.where(
            start >= ends[1], slot_ref[0, 2],
            jnp.where(start >= ends[0], slot_ref[0, 1], slot_ref[0, 0]),
        )
        tile = 0
        for first in range(1, tiles):
            tile = tile + (start >= first * TILE).astype(jnp.int32)
        seg_ref[at, 0] = start
        seg_ref[at, 1] = points[at + 1]
        seg_ref[at, 2] = tile
        seg_ref[at, 3] = slot
        seg_ref[at, 4] = jnp.where(
            slot == 2, enc_ref[0, 2], jnp.where(slot == 1, enc_ref[0, 1], enc_ref[0, 0])
        )


def of_tile(at, tile, tiles, load):
    picked = load(jnp.minimum(at, tiles - 1))
    for back in (1, 2):
        other = jnp.maximum(jnp.minimum(at - back, tiles - 1), 0)
        picked = jnp.where(tile == at - back, load(other), picked)
    return picked


def of_slot(slot, other, load):
    picked = load(other)
    for memory in (1, 2):
        picked = jnp.where(slot == memory, load(memory * (ENC // TILE) + other), picked)
    return picked


def masked_keys(scores, tile, valid):
    key_pos = tile * TILE + lax.broadcasted_iota(jnp.int32, (scores.shape[0], 1), 0)
    return jnp.where(key_pos < valid, scores, NEG)


def cross_segment(at, seg_ref, q_ref, keys, values_t, out, lse_ref):
    tiles = q_ref.shape[0] // TILE
    tile, slot, valid = seg_ref[at, 2], seg_ref[at, 3], seg_ref[at, 4]
    queries = stack_heads(of_tile(at, tile, tiles, lambda place: q_ref[tile_rows(place), :]))
    row_pos = lane_positions(tile * TILE)

    scores = []
    for other in range(ENC // TILE):
        tile_scores = dot_nt(of_slot(slot, other, lambda place: keys[place]), queries)
        scores.append(masked_keys(tile_scores, other, valid))
    value, log_total = soft_sum(
        scores, lambda other: of_slot(slot, other, lambda place: values_t[place])
    )
    mine = (row_pos >= seg_ref[at, 0]) & (row_pos < seg_ref[at, 1])
    out[at] = value
    lse_ref[pl.ds(at, 1), :] = jnp.where(mine, log_total, -NEG)


def join_segments(seg_ref, out, out_ref, tiles):
    for tile in range(tiles):
        row_pos = lane_positions(tile * TILE)
        total = jnp.zeros((HDIM, PAIR), FLOAT)
        for at in range(SEGMENTS):
            mine = (row_pos >= seg_ref[at, 0]) & (row_pos < seg_ref[at, 1])
            total = jnp.where(mine, out[at], total)
        out_ref[tile * TILE : (tile + 1) * TILE, :] = unstack_heads(total).astype(HALF)


SHARD = 64
FF_PAD = 384
ORDERS = ("zyx", "yxz", "xzy")
Y_LAST = ("xzy", "zxy")


class Torus:
    def __init__(self):
        tok, hid = lax.axis_index("tok"), lax.axis_index("hid")
        self.core = lax.rem(tok, 2)
        self.pos = {
            "x": lax.rem(tok // 2, 2) * 2 + lax.rem(hid, 2),
            "y": tok // 4,
            "z": hid // 2,
        }

    def moved(self, axis, step):
        place = dict(self.pos)
        place[axis] = lax.rem(place[axis] + step + 4, 4)
        return place

    def device(self, place, core=None):
        core = self.core if core is None else core
        return (
            (place["y"] * 2 + place["x"] // 2) * 2 + core,
            place["z"] * 2 + lax.rem(place["x"], 2),
        )

    def neighbour(self, axis, step):
        return self.device(self.moved(axis, step))

    def sibling(self):
        return self.device(self.pos, 1 - self.core)

    def beyond(self):
        return self.neighbour("x", 2)


def block_index(place, whole):
    return (
        slice(None) if "z" in whole else place["z"],
        slice(None) if "x" in whole else lax.rem(place["x"], 2),
        slice(None) if "y" in whole else place["y"],
        slice(None) if "x" in whole else place["x"] // 2,
    )


def whole_dims(whole):
    dims = (4,) if "z" in whole else ()
    dims += (2,) if "x" in whole else ()
    dims += (4,) if "y" in whole else ()
    return dims + ((2,) if "x" in whole else ())


class Flow:
    def __init__(self, torus, out_ref, cuts, orders, sems, own_ref=None):
        self.torus, self.out_ref, self.cuts, self.orders = torus, out_ref, cuts, orders
        self.sems, self.own_ref = sems, own_ref
        self.rows = out_ref.shape[5]
        self.sends, self.siblings = [], []
        self.last = {}

    def view(self, place, whole, cut, rows=None):
        rows = (0, self.rows) if rows is None else rows
        return self.out_ref.at[
            block_index(place, whole) + (self.torus.core, pl.ds(*rows), pl.ds(*cut))
        ]

    def copy(self, ref, target, first, log, src=None):
        at = len(log)
        copy = pltpu.make_async_remote_copy(
            src_ref=ref if src is None else src, dst_ref=ref,
            send_sem=self.sems[first].at[at], recv_sem=self.sems[first + 1].at[at],
            device_id=target, device_id_type=MESH,
        )
        copy.start()
        log.append(copy)
        return copy

    def to_sibling(self, place, whole, cut, src=None):
        self.copy(self.view(place, whole, cut), self.torus.sibling(), 2, self.siblings, src)

    def plan(self, stage):
        for part, cut in enumerate(self.cuts):
            yield part, cut, self.orders[part][stage], self.orders[part][:stage]

    def near(self, stage):
        torus = self.torus
        for part, cut, axis, whole in self.plan(stage):
            src = None
            if stage == 0:
                src = None if self.own_ref is None else self.own_ref.at[:, pl.ds(*cut)]
            ref = self.view(torus.pos, whole, cut)
            self.last[part] = [
                self.copy(ref, torus.neighbour(axis, step), 0, self.sends, src)
                for step in (1, -1)
            ]
            if stage == 0:
                self.to_sibling(torus.pos, "", cut, src)

    def far(self, stage):
        torus, half = self.torus, self.rows // 2
        for part, cut, axis, whole in self.plan(stage):
            copies = []
            for copy, step, first in zip(self.last[part], (1, -1), (0, half)):
                origin = torus.moved(axis, -step)
                copy.wait_recv()
                if half >= 16:
                    ref = self.view(origin, whole, cut, (first, half))
                    copies.append(self.copy(ref, torus.neighbour(axis, step), 0, self.sends))
                elif step == 1:
                    ref = self.view(origin, whole, cut)
                    copies.append(self.copy(ref, torus.neighbour(axis, step), 0, self.sends))
                self.to_sibling(origin, whole, cut)
            self.last[part] = copies

    def done(self, stage):
        for part, cut, axis, whole in self.plan(stage):
            for copy in self.last[part]:
                copy.wait_recv()
            self.to_sibling(self.torus.moved(axis, 2), whole, cut)

    def arrived(self):
        for copy in self.siblings:
            copy.wait_recv()

    def finish(self):
        for copy in self.sends + self.siblings:
            copy.wait_send()


def flow_sems(parts, split):
    sends = parts * 3 * (2 + split)
    return [pltpu.SemaphoreType.DMA((sends,))] * 2 + [pltpu.SemaphoreType.DMA((parts * 10,))] * 2


class Trade:
    def __init__(self, src, land, sems):
        self.src, self.land, self.sems = src, land, sems
        self.me = lax.axis_index("hid")
        self.tok = lax.axis_index("tok")

    def copy(self, step):
        target = lax.rem(self.me + step, 8)
        return pltpu.make_async_remote_copy(
            src_ref=self.src(target), dst_ref=self.land(self.me),
            send_sem=self.sems[0].at[step - 1], recv_sem=self.sems[1].at[step - 1],
            device_id=(self.tok, target), device_id_type=MESH,
        )

    def start(self, step):
        self.copy(step).start()

    def start_all(self):
        for step in range(1, 8):
            self.start(step)

    def arrived(self):
        for step in range(1, 8):
            self.copy(step).wait_recv()

    def finish(self):
        for step in range(1, 8):
            self.copy(step).wait_send()


def trade_sems():
    return [pltpu.SemaphoreType.DMA((7,))] * 2


def greet(peers):
    barrier = pltpu.get_barrier_semaphore()
    for peer in peers:
        pl.semaphore_signal(barrier, inc=1, device_id=peer, device_id_type=MESH)
    return barrier, len(peers)


def hid_peers():
    tok, me = lax.axis_index("tok"), lax.axis_index("hid")
    return [(tok, lax.rem(me + step, 8)) for step in range(1, 8)]


def torus_peers(torus):
    outside = 2 * lax.rem(lax.axis_index("hid"), 2) - 1
    return [
        torus.neighbour("y", 1), torus.neighbour("y", -1), torus.neighbour("x", outside),
        torus.sibling(),
    ]


def rows_at(index, rows):
    return pl.ds(pl.multiple_of(index * rows, 64), rows)


def scale_of(row_vals):
    return lax.rsqrt(jnp.mean(row_vals * row_vals, axis=-1, keepdims=True) + EPS)


def norm_backward(row_vals, gain, gradient):
    scale = scale_of(row_vals)
    normal = row_vals * scale
    weighted = gradient * gain
    inner = jnp.mean(weighted * normal, axis=-1, keepdims=True)
    return scale * (weighted - normal * inner)


class Remote:
    def __init__(self, src, dst, sems, at, target):
        self.src, self.dst, self.sems, self.at, self.target = src, dst, sems, at, target

    def copy(self):
        return pltpu.make_async_remote_copy(
            src_ref=self.src(), dst_ref=self.dst(),
            send_sem=self.sems[0].at[self.at], recv_sem=self.sems[1].at[self.at],
            device_id=self.target(), device_id_type=MESH,
        )

    def start(self):
        self.copy().start()

    def wait_recv(self):
        self.copy().wait_recv()

    def wait_send(self):
        self.copy().wait_send()


class Pairs:
    def __init__(self, torus, sems):
        self.torus, self.sems, self.log = torus, sems, []

    def send(self, src, dst, target=None):
        target = self.torus.sibling if target is None else target
        copy = Remote(src, dst, self.sems, len(self.log), target)
        copy.start()
        self.log.append(copy)
        return copy

    def finish(self):
        for copy in self.log:
            copy.wait_send()


class Columns:
    def __init__(self, torus, buffer, sends):
        self.torus, self.buffer, self.sends = torus, buffer, sends
        self.siblings = []

    def send(self, step, half, target):
        torus = self.torus

        def ref():
            y = torus.moved("y", step)["y"]
            xhi = torus.pos["x"] // 2
            at = (slice(None), xhi, 1 - xhi)[0 if half is None else half + 1]
            return self.buffer.at[y, at, torus.core]

        return self.sends.send(ref, ref, target)

    def up(self):
        return self.torus.neighbour("y", 1)

    def down(self):
        return self.torus.neighbour("y", -1)

    def start(self):
        self.first = self.send(0, 0, self.torus.beyond)
        self.siblings.append(self.send(0, 0, None))

    def near(self):
        self.first.wait_recv()
        self.last = [self.send(0, None, self.up), self.send(0, None, self.down)]
        self.siblings.append(self.send(0, 1, None))

    def far(self):
        self.last[0].wait_recv()
        one = self.send(-1, 0, self.up)
        self.siblings.append(self.send(-1, None, None))
        self.last[1].wait_recv()
        two = self.send(1, 1, self.down)
        self.siblings.append(self.send(1, None, None))
        self.last = [one, two]

    def done(self):
        for copy in self.last:
            copy.wait_recv()
        self.siblings.append(self.send(2, None, None))

    def arrived(self):
        for copy in self.siblings:
            copy.wait_recv()


class Rows:
    def __init__(self, torus, buffer, sends):
        self.torus, self.buffer, self.sends = torus, buffer, sends
        self.half = buffer.shape[2] // 2

    def send(self, step, whole, rows, target):
        torus = self.torus

        def ref():
            z = torus.moved("z", step)["z"]
            xlo = slice(None) if whole else lax.rem(torus.pos["x"], 2)
            return self.buffer.at[z, xlo, pl.ds(*rows)]

        return self.sends.send(ref, ref, target)

    def partner(self):
        me = lax.axis_index("hid")
        return lax.axis_index("tok"), me + 1 - 2 * lax.rem(me, 2)

    def up(self):
        return self.torus.neighbour("z", 1)

    def down(self):
        return self.torus.neighbour("z", -1)

    def start(self):
        half = self.half
        self.one = [self.send(0, False, (0, half), to) for to in (self.up, self.down)]
        self.across = self.send(0, False, (half, half), self.partner)
        self.others = [self.send(0, False, (0, half), self.partner)]

    def near(self):
        half = self.half
        self.across.wait_recv()
        self.two = [self.send(0, True, (half, half), to) for to in (self.up, self.down)]

    def far(self, first):
        half, part = self.half, self.half // 2
        near, base, whole = (self.one, 0, False) if first else (self.two, half, True)
        near[0].wait_recv()
        copies = [self.send(-1, whole, (base, part), self.up)]
        if first:
            self.others.append(self.send(-1, False, (0, half), self.partner))
        near[1].wait_recv()
        copies.append(self.send(1, whole, (base + part, part), self.down))
        if first:
            self.others.append(self.send(1, False, (0, half), self.partner))
            self.one = copies
        else:
            self.two = copies

    def done(self, first):
        for copy in self.one if first else self.two:
            copy.wait_recv()
        if first:
            self.others.append(self.send(2, False, (0, self.half), self.partner))
        else:
            for copy in self.others:
                copy.wait_recv()


GATE_UP_CUTS = ((0, 256), (256, 256), (512, 256))
DOWN_CUTS = ((0, 128), (128, 128), (256, 128))
MIX_CUTS = ((0, 128), (128, 128))
EARLY_CUTS = ((0, 256),)
HALVES = ((0, 32), (32, 32))
QKV_CUTS = ((0, 128), (128, 128))
GATHER_MIX = ((0, 128), (128, 128), (256, 128))
GATHER_LAST = ((384, 128),)
GATHER_ONE = ((0, 128), (128, 256), (384, 256))
GATHER_TWO = ((640, 128), (768, 128), (896, 256))
TWO_ORDERS = ORDERS[:2] + Y_LAST[1:]
GATHERS = {
    "start": ("w near 0", "b near 0", "two near 0"),
    "sent": ("one near 0", "w far 0", "b far 0", "last near 0", "two far 0"),
    "columns far": ("one far 0",),
    "rows far": ("b done 0", "two done 0"),
    "columns done": ("b near 1", "last far 0"),
    "rows second": ("one done 0",),
    "bias": ("one near 1", "b far 1", "last done 0", "last near 1"),
    "rows done": ("one far 1", "b done 1", "b near 2", "last far 1"),
    "qkv": ("one done 1", "one near 2", "b far 2", "last done 1", "two near 1"),
    "self 4": ("w done 0", "last near 2"),
    "o1 sent": ("w near 1", "b done 2", "two far 1"),
    "kv sent": ("w far 1",),
    "o1 here": ("last far 2", "two done 1"),
    "q2 sent": ("two near 2",),
    "q2 here": ("one far 2",),
    "kv here": ("w done 1",),
    "cross 4": ("last done 2", "two far 2"),
    "cross 6": ("w near 2",),
    "o2 sent": ("one done 2", "two done 2"),
    "ff 6": ("w far 2",),
    "do sent": ("w done 2",),
}
DRAINS = {
    "start": ("gu begin 2", "down begin 2"),
    "cross 4": ("gu turn 2",),
    "dq2 here": ("gu settle 2",),
    "do sent": ("gu begin 1", "down turn 2"),
    "early": ("early begin 2",),
    "mix": ("mix begin 2",),
    "self": ("gu turn 1",),
    "self 2": ("mix turn 2", "early turn 2"),
    "dqkv sent": ("gu settle 1", "down settle 2", "down begin 1", "mix settle 2"),
    "first": ("mix begin 1",),
    "fold": ("early settle 2", "early begin 1"),
    "x sent": ("gu begin 0", "down turn 1", "mix turn 1", "early turn 1"),
    "e1": (
        "gu turn 0", "down settle 1", "down begin 0", "mix settle 1", "mix begin 0",
        "early settle 1", "early begin 0",
    ),
    "y sent": ("gu settle 0", "down turn 0", "mix turn 0", "early turn 0"),
    "y here": ("down settle 0", "mix settle 0", "early settle 0"),
}


def run_steps(table, transfers, point):
    for step in table[point]:
        name, action, stage = step.split()
        getattr(transfers[name], action)(int(stage))


def forward_kernel(
    wq_ref, wk_ref, wv_ref, wo_ref, cq_ref, ck_ref, cv_ref, co_ref, wg_ref, wu_ref, wd_ref,
    small_ref, tok_ref, mem_ref, bucket_ref, cot_ref, len_ref, slot_ref, enc_ref,
    wf_ref, wa_ref, wqkv_ref, yff_ref,
    gain_ref, win_ref, h1_ref, h2_ref, qkv_ref, kv_ref, o1_ref, o1r_ref, lse_ref, x1_ref, q2_ref,
    o2_ref, o2r_ref, lse2_ref, mixed_ref, g2_ref, do_ref, xt3_ref, xtc_ref,
    wa, pack, w_first, small, token_rows, send_kv, send_q2, keys, values_t, bias,
    cross_keys, cross_values_t, cross_out, seg,
    h3, y_stage, xs3, xsc, xr3, xrc, w_ff, send_do, out_acc, in_acc,
    own_sem, ff_sem, y_sem, *sems,
):
    torus = Torus()
    me = lax.axis_index("hid")
    rows, mem_rows = tok_ref.shape[0], mem_ref.shape[0]
    tiles = qkv_ref.shape[0] // TILE
    barrier, count = greet(hid_peers() + torus_peers(torus) + [torus.beyond()])
    here = block_index(torus.pos, "") + (torus.core,)
    z, xlo = torus.pos["z"], lax.rem(me, 2)
    y, xhi = torus.pos["y"], torus.pos["x"] // 2
    token_rows[z, xlo] = tok_ref[...]
    small[y, xhi, torus.core] = small_ref[...]
    w_first[y, xhi, torus.core] = jnp.concatenate(
        [wq_ref[...], wk_ref[...], wv_ref[...]], axis=1
    )
    wa[here] = jnp.concatenate(
        [wo_ref[...], cq_ref[...], ck_ref[...], cv_ref[...], co_ref[...]], axis=1
    )
    blank = jnp.zeros((SHARD, FF_PAD - wg_ref.shape[1]), HALF)
    pack[...] = jnp.concatenate(
        [wg_ref[...], blank, wu_ref[...], blank, wd_ref[...], blank], axis=1
    )
    own = pltpu.make_async_copy(pack, wf_ref.at[here], own_sem.at[0])
    own.start()
    flow_b = Flow(torus, wa, GATHER_MIX, ORDERS, sems[0:4])
    flow_c = Flow(torus, wa, GATHER_LAST, ORDERS[2:], sems[28:32])
    flow_f = Flow(torus, wf_ref, GATHER_ONE, ORDERS, sems[4:8], pack)
    flow_g = Flow(torus, wf_ref, GATHER_TWO, TWO_ORDERS, sems[32:36], pack)
    row_sends, column_sends = Pairs(torus, sems[8:10]), Pairs(torus, sems[10:12])
    gather_rows = Rows(torus, token_rows, row_sends)
    columns = [Columns(torus, w_first, column_sends), Columns(torus, small, column_sends)]
    kv_trade = Trade(
        lambda j: send_kv.at[j], lambda j: kv_ref.at[rows_at(j, mem_rows)], sems[12:14]
    )
    o1_trade = Trade(
        lambda j: o1_ref.at[rows_at(j, rows)], lambda j: o1r_ref.at[j], sems[14:16]
    )
    q2_trade = Trade(
        lambda j: send_q2.at[j], lambda j: q2_ref.at[rows_at(j, rows)], sems[16:18]
    )
    o2_trade = Trade(
        lambda j: o2_ref.at[rows_at(j, rows)], lambda j: o2r_ref.at[j], sems[18:20]
    )
    do_trade = Trade(
        lambda j: send_do.at[j], lambda j: do_ref.at[rows_at(j, rows)], sems[20:22]
    )
    pairs = Pairs(torus, sems[22:24])
    flow_w = Flow(
        torus, wqkv_ref, QKV_CUTS, Y_LAST, sems[24:28], w_first.at[y, xhi, torus.core]
    )
    own_first = pltpu.make_async_copy(
        w_first.at[y, xhi, torus.core], wqkv_ref.at[here], own_sem.at[1]
    )
    own_first.start()
    build_segments(seg, len_ref, slot_ref, enc_ref, tiles)
    split_columns(torus, cot_ref[...].astype(FLOAT), xtc_ref, xsc)
    transfers = {"b": flow_b, "last": flow_c, "one": flow_f, "two": flow_g, "w": flow_w}
    at_point = functools.partial(run_steps, GATHERS, transfers)
    pl.semaphore_wait(barrier, count)
    at_point("start")
    gather_rows.start()
    for column in columns:
        column.start()
    at_point("sent")
    for column in columns:
        column.near()
    gather_rows.near()
    for column in columns:
        column.far()
    own.wait()
    own_first.wait()
    at_point("columns far")
    gather_rows.far(True)
    at_point("rows far")
    for column in columns:
        column.done()
    at_point("columns done")
    gather_rows.far(False)
    at_point("rows second")
    for column in columns:
        column.arrived()
    gain_parts = []
    heads = [jnp.zeros((8, PAIR), FLOAT), jnp.zeros((8, PAIR), FLOAT)]
    buckets = bucket_ref[...]
    for pair in range(8):
        blocks = [small[pair // 2, pair % 2, core].astype(FLOAT) for core in range(2)]
        gain_parts.append((blocks[0] + blocks[1])[0:8])
        for core in range(2):
            for part in range(2):
                bucket = (pair * 2 + core) * 2 + part
                for head in range(2):
                    at = 3 + part * 2 + head
                    value = blocks[core][at : at + 1]
                    value = jnp.concatenate([value] * 4, axis=1)
                    heads[head] = jnp.where(buckets == bucket, value, heads[head])
    gain_ref[...] = jnp.concatenate(gain_parts, axis=1)
    after = lax.broadcasted_iota(jnp.int32, (8, PAIR), 0) * PAIR + lax.broadcasted_iota(
        jnp.int32, (8, PAIR), 1
    )
    after = (after >= TILE) & (after < PAIR)
    win_ref[0:8] = jnp.where(after, NEG, heads[0])
    win_ref[8:16] = jnp.where(after, NEG, heads[1])
    build_bias(win_ref, bias, tiles)
    at_point("bias")
    gather_rows.done(True)
    at_point("rows done")
    gather_rows.done(False)
    for j in range(8):
        block = token_rows[j // 2, j % 2].astype(FLOAT)
        h1 = (block * scale_of(block) * gain_ref[0:1, :]).astype(HALF)
        h1_ref[j] = h1
        qkv = dot(h1, w_first[...].reshape(16 * SHARD, 256))
        qkv_ref[j * rows : (j + 1) * rows, :] = qkv.astype(HALF)
    at_point("qkv")

    def weights(j, first, width):
        block = wa[j // 2, j % 2, :, :, :, :, first : first + width]
        return block.reshape(16 * SHARD, width)

    def spread_trade(trade, left_ref, first, send_ref, land_ref):
        width = send_ref.shape[-1]
        spread(left_ref, lambda j: weights(j, first, width), send_ref)
        trade.start_all()
        land_ref[rows_at(me, left_ref.shape[0]), :] = send_ref[me]

    for tile in range(tiles):
        block = qkv_ref[tile * TILE : (tile + 1) * TILE, 128:256]
        keys[tile] = block[:, :HDIM]
        values_t[tile] = block[:, HDIM:].astype(FLOAT).T.astype(HALF)
    ends = doc_ends(len_ref)

    def row_tile(tile):
        at = slice(tile * TILE, (tile + 1) * TILE)
        queries = stack_heads(qkv_ref[at, 0:128])
        row_start = start_of(lane_positions(tile * TILE), ends)
        first = max(0, tile - LONG // TILE)
        scores = []
        for other in range(first, tile + 1):
            tile_scores = dot_nt(keys[other], queries) + bias[tile - other]
            key_pos = other * TILE + lax.broadcasted_iota(jnp.int32, (TILE, 1), 0)
            scores.append(jnp.where(key_pos >= row_start, tile_scores, NEG))
        value, log_total = soft_sum(scores, lambda other: values_t[first + other])
        o1_ref[at, :] = unstack_heads(value).astype(HALF)
        lse_ref[tile : tile + 1, :] = log_total

    for tile in range(4):
        row_tile(tile)
    at_point("self 4")
    for tile in range(4, tiles):
        row_tile(tile)
    o1_trade.start_all()
    o1r_ref[me] = o1_ref[rows_at(me, rows), :]
    at_point("o1 sent")
    flow_b.arrived()
    spread_trade(kv_trade, mem_ref, 256, send_kv, kv_ref)
    at_point("kv sent")
    copies = [pairs.send(lambda: xsc, lambda: xrc)]
    o1_trade.arrived()
    at_point("o1 here")
    total = tok_ref[...].astype(FLOAT)
    for pair in range(4):
        left = jnp.concatenate([o1r_ref[2 * pair], o1r_ref[2 * pair + 1]], axis=1)
        right = jnp.concatenate(
            [weights(2 * pair, 0, 128), weights(2 * pair + 1, 0, 128)], axis=1
        )
        total = total + dot_nt(left, right)
    x1_ref[...] = total
    h2_ref[...] = (total * scale_of(total) * gain_ref[1:2, :]).astype(HALF)
    spread_trade(q2_trade, h2_ref, 128, send_q2, q2_ref)
    at_point("q2 sent")
    q2_trade.arrived()
    at_point("q2 here")
    kv_trade.arrived()
    at_point("kv here")
    for tile in range(kv_ref.shape[0] // TILE):
        block = kv_ref[tile * TILE : (tile + 1) * TILE, :]
        cross_keys[tile] = block[:, :HDIM]
        cross_values_t[tile] = block[:, HDIM:].astype(FLOAT).T.astype(HALF)

    def segment(at):
        cross_segment(at, seg, q2_ref, cross_keys, cross_values_t, cross_out, lse2_ref)

    pl.loop(0, 4)(segment)
    at_point("cross 4")
    pl.loop(4, 6)(segment)
    at_point("cross 6")
    pl.loop(6, SEGMENTS)(segment)
    join_segments(seg, cross_out, o2_ref, tiles)
    o2_trade.start_all()
    at_point("o2 sent")
    o2r_ref[me] = o2_ref[rows_at(me, rows), :]
    flow_c.arrived()
    keep = pltpu.make_async_copy(wa, wa_ref, own_sem.at[0])
    keep.start()
    flow_f.arrived()
    flow_g.arrived()

    def fetch(j):
        slot = lax.rem(j, 2)
        return pltpu.make_async_copy(
            wf_ref.at[j // 2, lax.rem(j, 2)], w_ff.at[slot], ff_sem.at[slot]
        )

    fetch(0).start()
    o2_trade.arrived()
    x_two = x1_ref[...]
    for pair in range(4):
        left = jnp.concatenate([o2r_ref[2 * pair], o2r_ref[2 * pair + 1]], axis=1)
        right = jnp.concatenate(
            [weights(2 * pair, 384, 128), weights(2 * pair + 1, 384, 128)], axis=1
        )
        x_two = x_two + dot_nt(left, right)
    out_acc[...] = x_two
    g2_ref[...] = x_two
    in_acc[...] = jnp.zeros_like(in_acc)
    h3[...] = (x_two * scale_of(x_two) * gain_ref[2:3, :]).astype(HALF)
    split_columns(torus, h3[...].astype(FLOAT), xt3_ref, xs3)
    copies.append(pairs.send(lambda: xs3, lambda: xr3))

    def stash(j):
        return pltpu.make_async_copy(
            y_stage.at[j], yff_ref.at[j, pl.ds(0, rows)], y_sem.at[0, j]
        )

    def share(j):
        return pltpu.make_async_remote_copy(
            src_ref=y_stage.at[j], dst_ref=yff_ref.at[j, pl.ds(rows, rows)],
            send_sem=y_sem.at[1, j], recv_sem=y_sem.at[2, j],
            device_id=torus.sibling(), device_id_type=MESH,
        )

    def ff_weight(slot, first, width):
        return w_ff[slot, :, :, :, :, first : first + width].reshape(16 * SHARD, width)

    def one_block(j):
        @pl.when(j < 7)
        def _():
            fetch(j + 1).start()

        fetch(j).wait()
        slot = lax.rem(j, 2)
        gate_up = dot(h3[...], ff_weight(slot, 0, 2 * FF_PAD))
        gate, up = gate_up[:, :FF_PAD], gate_up[:, FF_PAD:]
        d_hidden = dot(cot_ref[...], ff_weight(slot, 2 * FF_PAD, FF_PAD))
        curve = 0.7978845608028654 * (gate + 0.044715 * gate * gate * gate)
        bend = jnp.tanh(curve)
        gelu = 0.5 * gate * (1.0 + bend)
        slope = 0.5 * (1.0 + bend) + 0.5 * gate * (1.0 - bend * bend) * (
            0.7978845608028654 * (1.0 + 3.0 * 0.044715 * gate * gate)
        )
        hidden = (gelu * up).astype(HALF)
        y_stage[j, :, 2 * FF_PAD :] = hidden
        d_both = jnp.concatenate([d_hidden * up * slope, d_hidden * gelu], axis=1).astype(HALF)
        y_stage[j, :, 0 : 2 * FF_PAD] = d_both
        stash(j).start()
        share(j).start()
        out_acc[...] += dot_nt(hidden, ff_weight(slot, 2 * FF_PAD, FF_PAD))
        in_acc[...] += dot_nt(d_both, ff_weight(slot, 0, 2 * FF_PAD))

    pl.loop(0, 6)(one_block)
    at_point("ff 6")
    pl.loop(6, 8)(one_block)
    mixed_ref[...] = out_acc[...].astype(HALF)
    d_inner = norm_backward(g2_ref[...], gain_ref[2:3, :], in_acc[...])
    g_two = cot_ref[...].astype(FLOAT) + d_inner
    g2_ref[...] = g_two
    h3[...] = g_two.astype(HALF)
    spread(h3, lambda j: weights(j, 384, 128), send_do)
    do_trade.start_all()
    do_ref[rows_at(me, rows), :] = send_do[me]
    at_point("do sent")
    for copy in copies:
        copy.wait_recv()
    join_columns(xtc_ref, xrc)
    join_columns(xt3_ref, xr3)
    do_trade.arrived()
    flow_w.arrived()
    for trade in (kv_trade, o1_trade, q2_trade, o2_trade, do_trade):
        trade.finish()
    for flow in (flow_b, flow_c, flow_f, flow_g, flow_w, row_sends, column_sends, pairs):
        flow.finish()
    keep.wait()

    @pl.loop(0, 8)
    def settle(j):
        stash(j).wait()
        share(j).wait()


def forward(vectors, scalars):
    tokens, memory = vectors[12:14]
    rows, mem_rows = tokens.shape[0], memory.shape[0]
    group, keys = rows * 8, mem_rows * 8
    tiles, key_tiles = group // TILE, keys // TILE
    vmem = pl.BlockSpec(memory_space=pltpu.VMEM)
    smem = pl.BlockSpec(memory_space=pltpu.SMEM)
    anywhere = pl.BlockSpec(memory_space=pl.ANY)
    shape = jax.ShapeDtypeStruct
    places = (4, 2, 4, 2, 2)
    turned = (4, 2, SHARD, rows)
    return pl.pallas_call(
        forward_kernel,
        out_shape=(
            shape(places + (SHARD, 1152), HALF),
            shape(places + (SHARD, 512), HALF),
            shape(places + (SHARD, 256), HALF),
            shape((8, 2 * rows, 3 * FF_PAD), HALF),
            shape((8, 1024), FLOAT),
            shape((16, PAIR), FLOAT),
            shape((8, rows, 1024), HALF),
            shape((rows, 1024), HALF),
            shape((group, 256), HALF),
            shape((keys, 128), HALF),
            shape((group, 128), HALF),
            shape((8, rows, 128), HALF),
            shape((8, PAIR), FLOAT),
            shape((rows, 1024), FLOAT),
            shape((group, 128), HALF),
            shape((group, 128), HALF),
            shape((8, rows, 128), HALF),
            shape((8, PAIR), FLOAT),
            shape((rows, 1024), HALF),
            shape((rows, 1024), FLOAT),
            shape((group, 128), HALF),
            shape((4, 2, SHARD, 2 * rows), HALF),
            shape((4, 2, SHARD, 2 * rows), HALF),
        ),
        in_specs=[vmem] * 16 + [smem] * 3,
        out_specs=(anywhere,) * 4 + (vmem,) * 19,
        scratch_shapes=[
            pltpu.VMEM(places + (SHARD, 512), HALF),
            pltpu.VMEM((SHARD, 1152), HALF),
            pltpu.VMEM((4, 2, 2, SHARD, 256), HALF),
            pltpu.VMEM((4, 2, 2, 16, 128), HALF),
            pltpu.VMEM((4, 2, rows, 1024), HALF),
            pltpu.VMEM((8, mem_rows, 128), HALF),
            pltpu.VMEM((8, rows, 128), HALF),
            pltpu.VMEM((tiles, TILE, HDIM), HALF),
            pltpu.VMEM((tiles, HDIM, TILE), HALF),
            pltpu.VMEM((tiles, TILE, PAIR), FLOAT),
            pltpu.VMEM((key_tiles, TILE, HDIM), HALF),
            pltpu.VMEM((key_tiles, HDIM, TILE), HALF),
            pltpu.VMEM((SEGMENTS, HDIM, PAIR), FLOAT),
            pltpu.SMEM((SEGMENTS, 8), jnp.int32),
            pltpu.VMEM((rows, 1024), HALF),
            pltpu.VMEM((8, rows, 3 * FF_PAD), HALF),
        ]
        + [pltpu.VMEM(turned, HALF)] * 4
        + [
            pltpu.VMEM((2, 4, 2, 2, SHARD, 1152), HALF),
            pltpu.VMEM((8, rows, 128), HALF),
            pltpu.VMEM((rows, 1024), FLOAT),
            pltpu.VMEM((rows, 1024), FLOAT),
            pltpu.SemaphoreType.DMA((2,)),
            pltpu.SemaphoreType.DMA((2,)),
            pltpu.SemaphoreType.DMA((3, 8)),
        ]
        + flow_sems(3, 2) + flow_sems(3, 2)
        + [pltpu.SemaphoreType.DMA((13,))] * 2 + [pltpu.SemaphoreType.DMA((20,))] * 2
        + trade_sems() * 5
        + [pltpu.SemaphoreType.DMA((2,))] * 2 + flow_sems(2, 2)
        + flow_sems(1, 2) + flow_sems(3, 2),
        compiler_params=pltpu.CompilerParams(
            collective_id=0, has_side_effects=True, vmem_limit_bytes=62 * 2**20
        ),
    )(*vectors, *scalars)


class Drain:
    def __init__(self, torus, acc, out_ref, cuts, orders, halves, buffers, sems):
        self.torus, self.acc, self.out_ref = torus, acc, out_ref
        self.cuts, self.orders, self.halves = cuts, orders, halves
        self.buffers, self.sems = buffers, sems
        self.rows = (0, acc.shape[4])
        self.sends, self.last = [], {}

    def plan(self, stage):
        for part, cut in enumerate(self.cuts):
            first = (stage * len(self.cuts) + part) * 2
            got, final = self.buffers[first : first + 2]
            yield part, cut, self.orders[part][stage], self.orders[part][:stage], got, final

    def view(self, place, whole, rows, cut):
        return self.acc.at[block_index(place, whole) + (pl.ds(*rows), pl.ds(*cut))]

    def send(self, axis, hops, step, whole, rows, cut, buffer, slot):
        copy = Remote(
            lambda: self.view(self.torus.moved(axis, hops), whole, rows, cut),
            lambda: buffer.at[slot],
            self.sems, len(self.sends),
            lambda: self.torus.neighbour(axis, step),
        )
        copy.start()
        self.sends.append(copy)
        return copy

    def add(self, place, whole, rows, cut, sources):
        dims = whole_dims(whole)
        count = 1
        for dim in dims:
            count *= dim

        def one(step):
            index, rest_of = [], step
            for dim in reversed(dims):
                index.append(lax.rem(rest_of, dim))
                rest_of = rest_of // dim
            index = index[::-1]
            left = iter(index)
            at = tuple(
                next(left) if isinstance(entry, slice) else entry
                for entry in block_index(place, whole)
            )
            where = at + (pl.ds(*rows), pl.ds(*cut))
            total = self.acc[where].astype(FLOAT)
            for buffer, slot in sources:
                total = total + buffer[(slot,) + tuple(index)].astype(FLOAT)
            self.acc[where] = total.astype(self.acc.dtype)

        if count == 1:
            one(jnp.int32(0))
        else:
            pl.loop(0, count)(one)

    def begin(self, stage):
        for part, cut, axis, whole, got, _ in self.plan(stage):
            self.last[part] = [
                self.send(axis, 2, 1 - 2 * slot, whole, rows, cut, got, slot)
                for slot, rows in enumerate(self.halves)
            ]

    def turn(self, stage):
        torus = self.torus
        for part, cut, axis, whole, got, final in self.plan(stage):
            copies = []
            for slot, step in enumerate((1, -1)):
                place = torus.moved(axis, step)
                if slot < len(self.halves):
                    self.last[part][slot].wait_recv()
                    self.add(place, whole, self.halves[slot], cut, [(got, slot)])
                copies.append(self.send(axis, step, step, whole, self.rows, cut, final, slot))
            self.last[part] = copies

    def settle(self, stage):
        for part, cut, axis, whole, _, final in self.plan(stage):
            for copy in self.last[part]:
                copy.wait_recv()
            if stage > 0:
                self.add(self.torus.pos, whole, self.rows, cut, [(final, 0), (final, 1)])
            else:
                mine = self.acc[block_index(self.torus.pos, "") + (slice(None), pl.ds(*cut))]
                self.out_ref[:, pl.ds(*cut)] = (
                    mine.astype(FLOAT) + final[0].astype(FLOAT) + final[1].astype(FLOAT)
                )

    def finish(self):
        for copy in self.sends:
            copy.wait_send()


def drain_scratch(cuts, orders, halves, rows, dtype):
    width = sum(cut[1] for cut in cuts)
    scratch = [pltpu.VMEM((4, 2, 4, 2, rows, width), dtype)]
    for stage in range(3):
        for part, cut in enumerate(cuts):
            dims = whole_dims(orders[part][:stage])
            scratch.append(pltpu.VMEM((len(halves),) + dims + (halves[0][1], cut[1]), dtype))
            scratch.append(pltpu.VMEM((2,) + dims + (rows, cut[1]), dtype))
    count = len(cuts) * 3 * (2 + len(halves))
    return scratch + [pltpu.SemaphoreType.DMA((count,))] * 2


def split_columns(torus, value, mine_ref, other_ref):
    size = value.shape[0]
    turned = value.T.astype(HALF).reshape(4, 2, 2, SHARD, size)
    first = torus.core == 0
    mine_ref[:, :, :, 0:size] = jnp.where(first, turned[:, :, 0], turned[:, :, 1])
    other_ref[...] = jnp.where(first, turned[:, :, 1], turned[:, :, 0])


def join_columns(turned, arrived):
    size = arrived.shape[-1]
    turned[...] = jnp.concatenate([turned[:, :, :, 0:size], arrived[...]], axis=-1)


def fill_product(acc, first, width, turned, right, unroll):
    @pl.loop(0, 8, unroll=unroll)
    def one_j(j):
        left = turned[...].reshape(8 * SHARD, turned.shape[-1])
        value = dot(left, right(j)).astype(HALF)
        acc[j // 2, lax.rem(j, 2), :, :, :, first : first + width] = value.reshape(
            4, 2, SHARD, width
        )


def spread(left_ref, weights, send_ref):
    width = send_ref.shape[-1]
    group = max(1, 256 // width)
    for first in range(0, 8, group):
        right = [weights(first + at) for at in range(group)]
        right = right[0] if group == 1 else jnp.concatenate(right, axis=1)
        value = dot(left_ref[...], right).astype(HALF)
        for at in range(group):
            send_ref[first + at] = value[:, at * width : (at + 1) * width]


def backward_kernel(
    q2_ref, kv2_ref, do2_ref, o2_ref, lse2_ref, g2_ref, x1_ref, tok_ref, mem_ref, h2_ref, gain_ref, xt3_ref, xtc_ref,
    qkv_ref, win_ref, o1_ref, lse_ref, bucket_ref, wq_ref, wk_ref, wv_ref, cq_ref, wg_ref, wu_ref,
    norm_ref, len_ref, slot_ref, enc_ref, h1_ref, o1r_ref, o2r_ref, wa_ref, wqkv_ref, yff_ref,
    dtok_ref, gu_out, down_out, mix_out, early_out, qkv_out, last_out, dnorm_ref, dmem_ref,
    *rest,
):
    rest = list(rest)

    def take(count):
        taken = rest[:count]
        del rest[:count]
        return taken

    y_o1, y_o2, y_q2, y_kv2, y_qkv, h1_turned = take(6)
    xt_h2, xt_mem, xt_g1, xt_g2 = take(4)
    xs_h2, xs_mem, xs_g1, xs_g2 = take(4)
    xr_h2, xr_mem, xr_g1, xr_g2 = take(4)
    g1_half, send_do, do_ref, dqkv_ref, dq2_ref, dkv2_ref, seg = take(7)
    t_acc, t_send, t_recv, tx_send, tx_recv, ty_send, ty_recv = take(7)
    s_all, s_acc, s_recv, sx_send, sx_recv, sy_send, sy_recv = take(7)
    n_send, n_recv = take(2)
    gu_scratch, down_scratch, mix_scratch, early_scratch = take(19), take(19), take(13), take(7)
    local_sem = rest.pop(0)
    sems = rest
    gu_sems, down_sems, mix_sems, early_sems = sems[0:2], sems[2:4], sems[4:6], sems[6:8]
    pair_sems, trade_sem = sems[8:10], sems[10:20]

    torus = Torus()
    me = lax.axis_index("hid")
    y, xhi = torus.pos["y"], torus.pos["x"] // 2
    rows, mem_rows = tok_ref.shape[0], mem_ref.shape[0]
    tiles = qkv_ref.shape[0] // TILE
    barrier, count = greet(
        hid_peers() + torus_peers(torus) + [torus.beyond(), torus.neighbour("y", 2)]
    )
    owns = [
        pltpu.make_async_copy(o1r_ref, y_o1.at[:, pl.ds(0, rows)], local_sem.at[0]),
        pltpu.make_async_copy(o2r_ref, y_o2.at[:, pl.ds(0, rows)], local_sem.at[1]),
    ]
    for own in owns:
        own.start()
    dq2_trade = Trade(
        lambda j: dq2_ref.at[rows_at(j, rows)], lambda j: y_q2.at[j, pl.ds(0, rows)],
        trade_sem[0:2],
    )
    dkv2_trade = Trade(
        lambda j: dkv2_ref.at[rows_at(j, mem_rows)], lambda j: y_kv2.at[j, pl.ds(0, mem_rows)],
        trade_sem[2:4],
    )
    do_trade = Trade(
        lambda j: send_do.at[j], lambda j: do_ref.at[rows_at(j, rows)], trade_sem[4:6]
    )
    dqkv_trade = Trade(
        lambda j: dqkv_ref.at[rows_at(j, rows)], lambda j: y_qkv.at[j], trade_sem[6:8]
    )
    norm_trade = Trade(lambda j: n_send, lambda j: n_recv.at[j], trade_sem[8:10])
    pairs = Pairs(torus, pair_sems)

    def share(buffer, size):
        return pairs.send(
            lambda: buffer.at[:, pl.ds(0, size)], lambda: buffer.at[:, pl.ds(size, size)]
        )

    drain_gu = Drain(
        torus, gu_scratch[0], gu_out, GATE_UP_CUTS, ORDERS, HALVES, gu_scratch[1:], gu_sems
    )
    drain_down = Drain(
        torus, down_scratch[0], down_out, DOWN_CUTS, ORDERS, HALVES, down_scratch[1:], down_sems
    )
    drain_mix = Drain(
        torus, mix_scratch[0], mix_out, MIX_CUTS, ORDERS, HALVES, mix_scratch[1:], mix_sems,
    )
    drain_early = Drain(
        torus, early_scratch[0], early_out, EARLY_CUTS, (ORDERS[2],), HALVES, early_scratch[1:],
        early_sems,
    )

    build_segments(seg, len_ref, slot_ref, enc_ref, tiles)
    transfers = {"gu": drain_gu, "down": drain_down, "mix": drain_mix, "early": drain_early}
    at_point = functools.partial(run_steps, DRAINS, transfers)

    def load_ff(yff, h1):
        load = pltpu.make_async_copy(yff_ref, yff, local_sem.at[2])
        load.start()
        load_h1 = pltpu.make_async_copy(h1_ref, h1, local_sem.at[3])
        load_h1.start()
        split_columns(torus, g2_ref[...], xt_g2, xs_g2)
        split_columns(torus, h2_ref[...].astype(FLOAT), xt_h2, xs_h2)
        split_columns(torus, mem_ref[...].astype(FLOAT), xt_mem, xs_mem)
        load.wait()
        fill_product(gu_scratch[0], 0, 768, xt3_ref, lambda j: yff[j, :, 0:768], 4)
        fill_product(down_scratch[0], 0, 384, xtc_ref, lambda j: yff[j, :, 768:1152], 4)
        load_h1.wait()
        for pair in range(4):
            block = h1[2 * pair : 2 * pair + 2].reshape(2 * rows, 1024)
            h1_turned[:, 2 * rows * pair : 2 * rows * (pair + 1)] = (
                block.astype(FLOAT).T.astype(HALF)
            )

    pl.run_scoped(
        load_ff, pltpu.VMEM((8, 2 * rows, 1152), HALF), pltpu.VMEM((8, rows, 1024), HALF)
    )

    pl.semaphore_wait(barrier, count)
    at_point("start")
    pair_g2 = pairs.send(lambda: xs_g2, lambda: xr_g2)
    pair_h2 = pairs.send(lambda: xs_h2, lambda: xr_h2)
    pair_mem = pairs.send(lambda: xs_mem, lambda: xr_mem)
    for own in owns:
        own.wait()
    pair_y = [share(y, size) for y, size in ((y_o1, rows), (y_o2, rows))]

    def cross_attention(keys, values, keys_t, queries, grads, deltas, dq, dkv):
        for tile in range(kv2_ref.shape[0] // TILE):
            block = kv2_ref[tile * TILE : (tile + 1) * TILE, :]
            keys[tile] = block[:, :HDIM]
            values[tile] = block[:, HDIM:]
            keys_t[tile] = block[:, :HDIM].astype(FLOAT).T.astype(HALF)
        row_prepare(tiles, lambda at: q2_ref[at, :], do2_ref, o2_ref, queries, grads, deltas)
        dkv[...] = jnp.zeros_like(dkv)

        def segment(at):
            tile, slot, valid = seg[at, 2], seg[at, 3], seg[at, 4]
            query = of_tile(at, tile, tiles, lambda place: queries[place])
            grad = of_tile(at, tile, tiles, lambda place: grads[place])
            delta = of_tile(at, tile, tiles, lambda place: deltas[place])

            def whole(ref, axis):
                parts = [of_slot(slot, other, lambda place: ref[place]) for other in range(4)]
                return jnp.concatenate(parts, axis=axis)

            scores = masked_keys(dot_nt(whole(keys, 0), query), 0, valid)
            weights = jnp.exp(scores - lse2_ref[pl.ds(at, 1), :])
            d_weights = dot_nt(whole(values, 0), grad)
            d_half = (weights * (d_weights - delta)).astype(HALF)
            dq[at] = dot(whole(keys_t, 1), d_half)
            both = jnp.concatenate(
                [dot(d_half, query), dot(weights.astype(HALF), grad)], axis=1
            )
            for memory in range(3):
                dkv[memory] += jnp.where(slot == memory, both, 0.0)

        pl.loop(0, 4)(segment)
        at_point("cross 4")
        pl.loop(4, SEGMENTS)(segment)
        for memory in range(3):
            dkv2_ref[memory * ENC : (memory + 1) * ENC, :] = dkv[memory].astype(HALF)
        for tile in range(tiles):
            total = jnp.zeros((HDIM, PAIR), FLOAT)
            for at in range(SEGMENTS):
                total = total + jnp.where(seg[at, 2] == tile, dq[at], 0.0)
            dq2_ref[tile * TILE : (tile + 1) * TILE, :] = unstack_heads(total).astype(HALF)
        dq2_trade.start_all()
        dkv2_trade.start_all()
        y_q2[me, 0:rows] = dq2_ref[rows_at(me, rows), :]
        y_kv2[me, 0:mem_rows] = dkv2_ref[rows_at(me, mem_rows), :]

    key_tiles = kv2_ref.shape[0] // TILE
    pl.run_scoped(
        cross_attention,
        pltpu.VMEM((key_tiles, TILE, HDIM), HALF),
        pltpu.VMEM((key_tiles, TILE, HDIM), HALF),
        pltpu.VMEM((key_tiles, HDIM, TILE), HALF),
        pltpu.VMEM((tiles, PAIR, HDIM), HALF),
        pltpu.VMEM((tiles, PAIR, HDIM), HALF),
        pltpu.VMEM((tiles, 1, PAIR), FLOAT),
        pltpu.VMEM((SEGMENTS, HDIM, PAIR), FLOAT),
        pltpu.VMEM((3, ENC, 2 * HDIM), FLOAT),
    )

    def inner(w_in, w_out, dmem):
        loads = [
            pltpu.make_async_copy(wa_ref.at[:, :, pl.ds(128, 256)], w_in, local_sem.at[2]),
            pltpu.make_async_copy(wa_ref.at[:, :, pl.ds(0, 128)], w_out, local_sem.at[3]),
        ]
        for load in loads:
            load.start()
        for load in loads:
            load.wait()
        dq2_trade.arrived()
        at_point("dq2 here")
        pair_q2 = share(y_q2, rows)
        total = jnp.zeros((rows, 1024), FLOAT)
        for pair in range(4):
            left = [y_q2[2 * pair + side, 0:rows] for side in range(2)]
            right = [w_in[2 * pair + side, :, 0:128] for side in range(2)]
            total = total + dot_nt(
                jnp.concatenate(left, axis=1), jnp.concatenate(right, axis=1)
            )
        d_inner = norm_backward(x1_ref[...], gain_ref[1:2, :], total)
        g_one = g2_ref[...] + d_inner
        dtok_ref[...] = g_one
        g1_half[...] = g_one.astype(HALF)

        spread(g1_half, lambda j: w_out[j], send_do)
        do_trade.start_all()
        do_ref[rows_at(me, rows), :] = send_do[me]
        at_point("do sent")
        split_columns(torus, dtok_ref[...], xt_g1, xs_g1)
        pair_g1 = pairs.send(lambda: xs_g1, lambda: xr_g1)
        dkv2_trade.arrived()
        pair_kv2 = share(y_kv2, mem_rows)
        for pair in range(4):
            left = [y_kv2[2 * pair + side, 0:mem_rows] for side in range(2)]
            right = [w_in[2 * pair + side, :, 128:256] for side in range(2)]
            value = dot_nt(jnp.concatenate(left, axis=1), jnp.concatenate(right, axis=1))
            dmem[...] = value if pair == 0 else dmem[...] + value
        store = pltpu.make_async_copy(dmem, dmem_ref, local_sem.at[2])
        store.start()
        for copy in [pair_g2, pair_mem, pair_kv2, pair_y[1]]:
            copy.wait_recv()
        join_columns(xt_mem, xr_mem)
        join_columns(xt_g2, xr_g2)
        fill_product(early_scratch[0], 0, 128, xt_mem, lambda j: y_kv2[j], 4)
        fill_product(early_scratch[0], 128, 128, xt_g2, lambda j: y_o2[j], 8)
        at_point("early")
        for copy in [pair_h2, pair_q2, pair_g1, pair_y[0]]:
            copy.wait_recv()
        join_columns(xt_g1, xr_g1)
        join_columns(xt_h2, xr_h2)
        fill_product(mix_scratch[0], 128, 128, xt_h2, lambda j: y_q2[j], 8)
        fill_product(mix_scratch[0], 0, 128, xt_g1, lambda j: y_o1[j], 8)
        at_point("mix")
        store.wait()

    pl.run_scoped(
        inner,
        pltpu.VMEM((8, 1024, 256), HALF),
        pltpu.VMEM((8, 1024, 128), HALF),
        pltpu.VMEM((mem_rows, 1024), FLOAT),
    )

    core_copies = []

    def self_attention(keys, values, keys_t, queries, grads, deltas, bias, bias_grad, dq):
        build_bias(win_ref, bias, tiles)
        for tile in range(tiles):
            block = qkv_ref[tile * TILE : (tile + 1) * TILE, 128:256]
            keys[tile] = block[:, :HDIM]
            values[tile] = block[:, HDIM:]
            keys_t[tile] = block[:, :HDIM].astype(FLOAT).T.astype(HALF)
        bias_grad[...] = jnp.zeros_like(bias_grad)
        dq[...] = jnp.zeros_like(dq)
        ends = doc_ends(len_ref)
        at_point("self")
        do_trade.arrived()
        row_prepare(
            tiles, lambda at: qkv_ref[at, 0:128], do_ref, o1_ref, queries, grads, deltas
        )

        def key_tile(other):
            key_pos = other * TILE + lax.broadcasted_iota(jnp.int32, (TILE, 1), 0)
            dk, dv = jnp.zeros((TILE, HDIM), FLOAT), jnp.zeros((TILE, HDIM), FLOAT)
            for tile in range(other, min(tiles, other + LONG // TILE + 1)):
                row_start = start_of(lane_positions(tile * TILE), ends)
                scores = dot_nt(keys[other], queries[tile]) + bias[tile - other]
                scores = jnp.where(key_pos >= row_start, scores, NEG)
                weights = jnp.exp(scores - lse_ref[tile : tile + 1, :])
                d_weights = dot_nt(values[other], grads[tile])
                d_scores = weights * (d_weights - deltas[tile])
                bias_grad[tile - other] += d_scores
                d_half = d_scores.astype(HALF)
                dv = dv + dot(weights.astype(HALF), grads[tile])
                dk = dk + dot(d_half, queries[tile])
                dq[tile] += dot(keys_t[other], d_half)
            at = slice(other * TILE, (other + 1) * TILE)
            dqkv_ref[at, 128:256] = jnp.concatenate([dk, dv], axis=1).astype(HALF)

        for other in range(2):
            key_tile(other)
        at_point("self 2")
        for other in range(2, tiles):
            key_tile(other)
        for tile in range(tiles):
            dqkv_ref[tile * TILE : (tile + 1) * TILE, 0:128] = unstack_heads(dq[tile]).astype(HALF)
        dqkv_trade.start_all()
        y_qkv[me] = dqkv_ref[rows_at(me, rows), :]
        at_point("dqkv sent")
        value = dot(h1_turned[...], dqkv_ref[...]).reshape(4, 2, 2, SHARD, 256)
        first = torus.core == 0
        t_acc[...] = jnp.where(first, value[:, :, 0], value[:, :, 1])
        t_send[...] = jnp.where(first, value[:, :, 1], value[:, :, 0]).astype(HALF)
        core_copies.append(pairs.send(lambda: t_send, lambda: t_recv))
        at_point("first")
        sums = []
        for head in range(2):
            parts = []
            for tile in range(tiles):
                part = bias_grad[tile, :, head * TILE : (head + 1) * TILE]
                part = jnp.concatenate([part, jnp.zeros_like(part)], axis=1)
                parts.append(fold_diagonals(part))
            parts.append(jnp.zeros((8 - tiles, PAIR), FLOAT))
            sums.append(jnp.concatenate(parts, axis=0))
        buckets = bucket_ref[...]
        s_all[...] = jnp.zeros_like(s_all)
        for bucket in range(32):
            mask = buckets == bucket
            shard, part = bucket // 2, bucket % 2
            for head in range(2):
                picked = jnp.where(mask, sums[head], 0.0)
                value = jnp.sum(jnp.sum(picked, axis=0, keepdims=True), axis=1, keepdims=True)
                at = 3 + part * 2 + head
                place = (shard % 2, shard // 4, shard // 2 % 2)
                s_all[place + (slice(at, at + 1), slice(None))] = jnp.broadcast_to(
                    value, (1, 128)
                )
        core_copies.append(pairs.send(lambda: s_all.at[1 - torus.core], lambda: s_recv))
        at_point("fold")

    pl.run_scoped(
        self_attention,
        pltpu.VMEM((tiles, TILE, HDIM), HALF),
        pltpu.VMEM((tiles, TILE, HDIM), HALF),
        pltpu.VMEM((tiles, HDIM, TILE), HALF),
        pltpu.VMEM((tiles, PAIR, HDIM), HALF),
        pltpu.VMEM((tiles, PAIR, HDIM), HALF),
        pltpu.VMEM((tiles, 1, PAIR), FLOAT),
        pltpu.VMEM((tiles, TILE, PAIR), FLOAT),
        pltpu.VMEM((tiles, TILE, PAIR), FLOAT),
        pltpu.VMEM((tiles, HDIM, PAIR), FLOAT),
    )

    x_copies = []

    def first_inputs(w_in):
        load = pltpu.make_async_copy(wqkv_ref, w_in, local_sem.at[2])
        load.start()
        core_copies[0].wait_recv()
        t_acc[...] += t_recv[...].astype(FLOAT)
        tx_send[...] = t_acc[:, 1 - xhi].astype(HALF)
        x_copies.append(pairs.send(lambda: tx_send, lambda: tx_recv, torus.beyond))
        core_copies[1].wait_recv()
        s_acc[...] = s_all[torus.core] + s_recv[...]
        sx_send[...] = s_acc[:, 1 - xhi]
        x_copies.append(pairs.send(lambda: sx_send, lambda: sx_recv, torus.beyond))
        at_point("x sent")
        load.wait()
        dqkv_trade.arrived()
        total = jnp.zeros((rows, 1024), FLOAT)
        for j in range(8):
            total = total + dot_nt(y_qkv[j], w_in[j])
        residual = tok_ref[...].astype(FLOAT)
        dtok_ref[...] += norm_backward(residual, gain_ref[0:1, :], total)
        at_point("e1")

    pl.run_scoped(first_inputs, pltpu.VMEM((8, 1024, 256), HALF))
    for copy in x_copies:
        copy.wait_recv()
    t_acc[:, xhi] += tx_recv[...].astype(FLOAT)
    s_acc[:, xhi] += sx_recv[...]
    y_copies = []
    for at, step in enumerate((1, -1, 2)):
        place = torus.moved("y", step)["y"]
        ty_send[at] = t_acc[place, xhi].astype(HALF)
        sy_send[at] = s_acc[place, xhi]
        for src, dst in ((ty_send, ty_recv), (sy_send, sy_recv)):
            y_copies.append(
                pairs.send(
                    functools.partial(src.at.__getitem__, at),
                    functools.partial(dst.at.__getitem__, at),
                    functools.partial(torus.neighbour, "y", step),
                )
            )
    at_point("y sent")
    for copy in y_copies:
        copy.wait_recv()
    total, last = t_acc[y, xhi], s_acc[y, xhi]
    for at in range(3):
        total = total + ty_recv[at].astype(FLOAT)
        last = last + sy_recv[at]
    qkv_out[...] = total
    last_out[...] = last
    at_point("y here")

    def dotted(value, weight):
        return jnp.sum(value * weight.astype(FLOAT), axis=1, keepdims=True)

    width = wg_ref.shape[1]
    sums = [
        dotted(qkv_out[:, 0:128], wq_ref[...])
        + dotted(qkv_out[:, 128:192], wk_ref[...])
        + dotted(qkv_out[:, 192:256], wv_ref[...]),
        dotted(mix_out[:, 128:256], cq_ref[...]),
        dotted(gu_out[:, 0:width], wg_ref[...])
        + dotted(gu_out[:, FF_PAD : FF_PAD + width], wu_ref[...]),
    ]
    lane = lax.broadcasted_iota(jnp.int32, (SHARD, 128), 1)
    block = jnp.zeros((SHARD, 128), FLOAT)
    for at, value in enumerate(sums):
        block = jnp.where(lane == at, value, block)
    n_send[...] = block.T[0:8]
    norm_trade.start_all()
    n_recv[me] = n_send[...]
    norm_trade.arrived()
    value = n_recv[0]
    for j in range(1, 8):
        value = value + n_recv[j]
    dnorm_ref[...] = value / norm_ref[...]
    for drain in transfers.values():
        drain.finish()
    for trade in (dq2_trade, dkv2_trade, do_trade, dqkv_trade, norm_trade):
        trade.finish()
    pairs.finish()


def backward(vectors, scalars, arrays):
    tokens, memory = vectors[7:9]
    rows, mem_rows = tokens.shape[0], memory.shape[0]
    group = rows * 8
    vmem = pl.BlockSpec(memory_space=pltpu.VMEM)
    smem = pl.BlockSpec(memory_space=pltpu.SMEM)
    anywhere = pl.BlockSpec(memory_space=pl.ANY)
    shape = jax.ShapeDtypeStruct
    drains = [
        drain_scratch(GATE_UP_CUTS, ORDERS, HALVES, SHARD, HALF),
        drain_scratch(DOWN_CUTS, ORDERS, HALVES, SHARD, HALF),
        drain_scratch(MIX_CUTS, ORDERS, HALVES, SHARD, HALF),
        drain_scratch(EARLY_CUTS, (ORDERS[2],), HALVES, SHARD, HALF),
    ]
    counts = (rows, mem_rows, rows, rows)
    scratch = [pltpu.VMEM((8, 2 * rows, 128), HALF)] * 3
    scratch += [pltpu.VMEM((8, 2 * mem_rows, 128), HALF), pltpu.VMEM((8, rows, 256), HALF)]
    scratch += [pltpu.VMEM((1024, group), HALF)]
    scratch += [pltpu.VMEM((4, 2, SHARD, 2 * size), HALF) for size in counts]
    scratch += [pltpu.VMEM((4, 2, SHARD, size), HALF) for size in counts + counts]
    scratch += [
        pltpu.VMEM((rows, 1024), HALF),
        pltpu.VMEM((8, rows, 128), HALF),
        pltpu.VMEM((group, 128), HALF),
        pltpu.VMEM((group, 256), HALF),
        pltpu.VMEM((group, 128), HALF),
        pltpu.VMEM((mem_rows * 8, 128), HALF),
        pltpu.SMEM((SEGMENTS, 8), jnp.int32),
        pltpu.VMEM((4, 2, SHARD, 256), FLOAT),
        pltpu.VMEM((4, 2, SHARD, 256), HALF),
        pltpu.VMEM((4, 2, SHARD, 256), HALF),
        pltpu.VMEM((4, SHARD, 256), HALF),
        pltpu.VMEM((4, SHARD, 256), HALF),
        pltpu.VMEM((3, SHARD, 256), HALF),
        pltpu.VMEM((3, SHARD, 256), HALF),
        pltpu.VMEM((2, 4, 2, 16, 128), FLOAT),
        pltpu.VMEM((4, 2, 16, 128), FLOAT),
        pltpu.VMEM((4, 2, 16, 128), FLOAT),
        pltpu.VMEM((4, 16, 128), FLOAT),
        pltpu.VMEM((4, 16, 128), FLOAT),
        pltpu.VMEM((3, 16, 128), FLOAT),
        pltpu.VMEM((3, 16, 128), FLOAT),
        pltpu.VMEM((8, SHARD), FLOAT),
        pltpu.VMEM((8, 8, SHARD), FLOAT),
    ]
    for drain in drains:
        scratch += drain[:-2]
    scratch.append(pltpu.SemaphoreType.DMA((4,)))
    for drain in drains:
        scratch += drain[-2:]
    scratch += [pltpu.SemaphoreType.DMA((18,))] * 2 + trade_sems() * 5
    return pl.pallas_call(
        backward_kernel,
        out_shape=(
            shape((rows, 1024), FLOAT),
            shape((SHARD, 2 * FF_PAD), FLOAT),
            shape((SHARD, FF_PAD), FLOAT),
            shape((SHARD, 256), FLOAT),
            shape((SHARD, 256), FLOAT),
            shape((SHARD, 256), FLOAT),
            shape((16, 128), FLOAT),
            shape((8, SHARD), FLOAT),
            shape((mem_rows, 1024), FLOAT),
        ),
        in_specs=[vmem] * 25 + [smem] * 3 + [anywhere] * 6,
        out_specs=(vmem,) * 8 + (anywhere,),
        scratch_shapes=scratch,
        compiler_params=pltpu.CompilerParams(
            collective_id=1, has_side_effects=True, vmem_limit_bytes=64 * 2**20
        ),
    )(*vectors, *scalars, *arrays)


def finish_kernel(
    mixed_ref, dtok_ref, dmem_ref, gu_ref, down_ref, mix_ref, early_ref, qkv_ref, last_ref, dnorm_ref,
    mixed_out, dtok_out, dmem_out, n1_out, wq_out, wk_out, wv_out, wo_out, rel_out, n2_out,
    cq_out, ck_out, cv_out, co_out, n3_out, wg_out, wu_out, wd_out,
):
    mixed_out[...] = mixed_ref[...]
    dtok_out[...] = dtok_ref[...]
    dmem_out[...] = dmem_ref[...]
    for at, out in enumerate((n1_out, n2_out, n3_out)):
        out[...] = dnorm_ref[at : at + 1, :]
    rel_out[0:1, 0:1] = last_ref[3:4, 0:1]
    rel_out[0:1, 1:2] = last_ref[4:5, 0:1]
    rel_out[1:2, 0:1] = last_ref[5:6, 0:1]
    rel_out[1:2, 1:2] = last_ref[6:7, 0:1]
    wq_out[...] = qkv_ref[:, 0:128]
    wk_out[...] = qkv_ref[:, 128:192]
    wv_out[...] = qkv_ref[:, 192:256]
    wo_out[...] = mix_ref[:, 0:128]
    cq_out[...] = mix_ref[:, 128:256]
    ck_out[...] = early_ref[:, 0:64]
    cv_out[...] = early_ref[:, 64:128]
    co_out[...] = early_ref[:, 128:256]
    width = wg_out.shape[1]
    wg_out[...] = gu_ref[:, 0:width]
    wu_out[...] = gu_ref[:, FF_PAD : FF_PAD + width]
    wd_out[...] = down_ref[:, 0:width]


def finish_outputs(mixed, d_tokens, d_memory, grads, ff_width):
    vmem = pl.BlockSpec(memory_space=pltpu.VMEM)

    def shape(*dims):
        return jax.ShapeDtypeStruct(dims, FLOAT)

    return pl.pallas_call(
        finish_kernel,
        out_shape=(
            jax.ShapeDtypeStruct(mixed.shape, HALF),
            shape(*d_tokens.shape),
            shape(*d_memory.shape),
            shape(1, SHARD), shape(SHARD, 128), shape(SHARD, HDIM), shape(SHARD, HDIM),
            shape(SHARD, 128), shape(2, 2), shape(1, SHARD),
            shape(SHARD, 128), shape(SHARD, HDIM), shape(SHARD, HDIM), shape(SHARD, 128),
            shape(1, SHARD), shape(SHARD, ff_width), shape(SHARD, ff_width),
            shape(SHARD, ff_width),
        ),
        in_specs=[vmem] * 10,
        out_specs=(vmem,) * 18,
    )(mixed, d_tokens, d_memory, *grads)


def local(
    tokens, memory, cotangent, norm1, w_query, w_key, w_value, w_out, rel_bias, norm2,
    cross_query, cross_key, cross_value, cross_out, norm3, w_gate, w_up, w_down,
    doc_lengths, memory_slot, enc_lengths, rel_bucket,
):
    core = lax.rem(lax.axis_index("tok"), 2)
    norms = jnp.stack([norm1, norm2, norm3])
    own_gains = jnp.pad(norms.astype(FLOAT), ((0, 5), (0, 0)), constant_values=1.0)
    blank = jnp.zeros_like(norms)
    norms = jnp.where(
        core == 0,
        jnp.concatenate([norms, blank], axis=1),
        jnp.concatenate([blank, norms], axis=1),
    )
    small = jnp.concatenate(
        [norms, jnp.broadcast_to(rel_bias.reshape(4, 1), (4, 128)), jnp.zeros((9, 128), HALF)]
    )
    tile_buckets = rel_bucket.reshape(-1, TILE)
    before = jnp.concatenate([tile_buckets[:1], tile_buckets[:-1]])
    buckets = jnp.pad(jnp.concatenate([tile_buckets, before], axis=1), ((0, 2), (0, 0)))
    (
        _, wa, w_qkv, y_ff, gains, windows, h_one, h_two, qkv, kv_two, o_one, o_one_rows, lse_one,
        x_one, q_two, o_two, o_two_rows, lse_two, mixed, g_two, d_out, xt_three, xt_cot,
    ) = forward(
        (
            w_query, w_key, w_value, w_out.T, cross_query, cross_key, cross_value, cross_out.T,
            w_gate, w_up, w_down.T, small, tokens, memory, buckets, cotangent,
        ),
        (doc_lengths, memory_slot, enc_lengths),
    )
    d_tokens, *grads, d_memory = backward(
        (
            q_two, kv_two, d_out, o_two, lse_two, g_two, x_one, tokens, memory, h_two, gains,
            xt_three, xt_cot, qkv, windows, o_one, lse_one, buckets, w_query, w_key, w_value,
            cross_query, w_gate, w_up, own_gains,
        ),
        (doc_lengths, memory_slot, enc_lengths),
        (
            h_one, o_one_rows, o_two_rows, wa.reshape(8, 16 * SHARD, 512),
            w_qkv.reshape(8, 16 * SHARD, 256), y_ff,
        ),
    )
    outs = list(finish_outputs(mixed, d_tokens, d_memory, grads, w_gate.shape[1]))
    for at in (3, 9, 14):
        outs[at] = outs[at][0]
    for at in (7, 13, 17):
        outs[at] = outs[at].T
    return tuple(outs)


def solution(mesh):
    return jax.shard_map(
        local,
        mesh=mesh,
        in_specs=(
            P(("tok", "hid"), None),
            P(("tok", "hid"), None),
            P(("tok", "hid"), None),
            P("tok"),
            P("tok", "hid"),
            P("tok", "hid"),
            P("tok", "hid"),
            P("hid", "tok"),
            P("tok", "hid"),
            P("tok"),
            P("tok", "hid"),
            P("tok", "hid"),
            P("tok", "hid"),
            P("hid", "tok"),
            P("tok"),
            P("tok", "hid"),
            P("tok", "hid"),
            P("hid", "tok"),
            P("tok", None),
            P("tok", None),
            P("tok", None),
            P(),
        ),
        out_specs=(
            P(("tok", "hid"), None),
            P(("tok", "hid"), None),
            P(("tok", "hid"), None),
            P("tok"),
            P("tok", "hid"),
            P("tok", "hid"),
            P("tok", "hid"),
            P("hid", "tok"),
            P("tok", "hid"),
            P("tok"),
            P("tok", "hid"),
            P("tok", "hid"),
            P("tok", "hid"),
            P("hid", "tok"),
            P("tok"),
            P("tok", "hid"),
            P("tok", "hid"),
            P("hid", "tok"),
        ),
        check_vma=False,
    )
```

```python
import functools

import jax
import jax.numpy as jnp
from jax import lax
from jax.experimental import pallas as pl
from jax.experimental.pallas import tpu as pltpu
from jax.sharding import PartitionSpec as P

EPS = 1e-06
MESH = pl.DeviceIdType.MESH

HDIM = 64
ENC = 1024
LONG = 1024
FLOAT = jnp.float32
HALF = jnp.bfloat16
TILE = 256
PAIR = 2 * TILE
NEG = -1e30
NT_DIMS = (((1,), (1,)), ((), ()))


def dot(first, second):
    return jnp.dot(first, second, preferred_element_type=FLOAT)


def dot_nt(first, second):
    return lax.dot_general(first, second, NT_DIMS, preferred_element_type=FLOAT)


def stack_heads(block):
    return jnp.concatenate([block[:, :HDIM], block[:, HDIM:]], axis=0)


def unstack_heads(columns):
    return jnp.concatenate(
        [columns[:, :TILE].T, columns[:, TILE:].T], axis=1
    )


def tile_rows(tile):
    return pl.ds(pl.multiple_of(tile * TILE, TILE), TILE)


def lane_positions(first):
    lane = lax.broadcasted_iota(jnp.int32, (1, PAIR), 1)
    return first + jnp.where(lane >= TILE, lane - TILE, lane)


def doc_ends(len_ref):
    first_end = len_ref[0, 0]
    return first_end, first_end + len_ref[0, 1]


def start_of(position, ends):
    return jnp.where(position >= ends[1], ends[1], jnp.where(position >= ends[0], ends[0], 0))


def build_bias(win_ref, bias, tiles):
    for diag in range(tiles):
        for head in range(2):
            row = win_ref[pl.ds(head * 8 + diag, 1), :]
            spread = jnp.broadcast_to(row, (TILE, PAIR))
            rolled = pltpu.roll(spread, 0, 1, stride=1, stride_axis=0)
            bias[diag, :, pl.ds(head * TILE, TILE)] = rolled[:, :TILE]


def soft_sum(scores, values_t):
    peak = jnp.max(scores[0], axis=0, keepdims=True)
    for tile in scores[1:]:
        peak = jnp.maximum(peak, jnp.max(tile, axis=0, keepdims=True))
    total, acc = None, None
    for at, tile in enumerate(scores):
        weights = jnp.exp(tile - peak)
        part = jnp.sum(weights, axis=0, keepdims=True)
        value = dot(values_t(at), weights.astype(HALF))
        total = part if at == 0 else total + part
        acc = value if at == 0 else acc + value
    return acc / total, peak + jnp.log(total)


def bucket_windows(bucket_ref):
    tiles = bucket_ref[...]
    count = tiles.shape[0]
    before = jnp.concatenate([tiles[0:1], tiles[0 : count - 1]], axis=0)
    windows = jnp.concatenate([tiles, before], axis=1)
    return jnp.concatenate([windows, jnp.zeros((8 - count, PAIR), jnp.int32)], axis=0)


def row_prepare(tiles, q_of, do_ref, o_ref, queries, grads, deltas):
    for tile in range(tiles):
        rows = slice(tile * TILE, (tile + 1) * TILE)
        queries[tile] = stack_heads(q_of(rows))
        block = do_ref[rows, :]
        grads[tile] = stack_heads(block)
        product = (block.astype(FLOAT) * o_ref[rows, :].astype(FLOAT)).T
        deltas[tile] = jnp.concatenate(
            [
                jnp.sum(product[:HDIM], axis=0, keepdims=True),
                jnp.sum(product[HDIM:], axis=0, keepdims=True),
            ],
            axis=1,
        )


def fold_diagonals(block):
    half = TILE // 2
    while half >= 8:
        block = block[:half] + pltpu.roll(block[half:], PAIR - half, 1)
        half //= 2
    total = block[0:1]
    for row in range(1, 8):
        total = total + pltpu.roll(block[row : row + 1], PAIR - row, 1)
    return total


SEGMENTS = 8


def build_segments(seg_ref, len_ref, slot_ref, enc_ref, tiles):
    ends = doc_ends(len_ref)
    starts = [(ends[0], (ends[0] + TILE - 1) // TILE), (ends[1], (ends[1] + TILE - 1) // TILE + 1)]
    for tile in range(tiles):
        first = tile * TILE
        before = (ends[0] <= first).astype(jnp.int32) + (ends[1] <= first).astype(jnp.int32)
        starts.append((first, tile + before))
    points = []
    for at in range(SEGMENTS):
        point = 0
        for value, order in starts:
            point = point + jnp.where(order == at, value, 0)
        points.append(point)
    points.append(tiles * TILE)
    for at in range(SEGMENTS):
        start = points[at]
        slot = jnp.where(
            start >= ends[1], slot_ref[0, 2],
            jnp.where(start >= ends[0], slot_ref[0, 1], slot_ref[0, 0]),
        )
        tile = 0
        for first in range(1, tiles):
            tile = tile + (start >= first * TILE).astype(jnp.int32)
        seg_ref[at, 0] = start
        seg_ref[at, 1] = points[at + 1]
        seg_ref[at, 2] = tile
        seg_ref[at, 3] = slot
        seg_ref[at, 4] = jnp.where(
            slot == 2, enc_ref[0, 2], jnp.where(slot == 1, enc_ref[0, 1], enc_ref[0, 0])
        )


def of_tile(at, tile, tiles, load):
    picked = load(jnp.minimum(at, tiles - 1))
    for back in (1, 2):
        other = jnp.maximum(jnp.minimum(at - back, tiles - 1), 0)
        picked = jnp.where(tile == at - back, load(other), picked)
    return picked


def of_slot(slot, other, load):
    picked = load(other)
    for memory in (1, 2):
        picked = jnp.where(slot == memory, load(memory * (ENC // TILE) + other), picked)
    return picked


def masked_keys(scores, tile, valid):
    key_pos = tile * TILE + lax.broadcasted_iota(jnp.int32, (scores.shape[0], 1), 0)
    return jnp.where(key_pos < valid, scores, NEG)


def cross_segment(at, seg_ref, q_ref, keys, values_t, out, lse_ref):
    tiles = q_ref.shape[0] // TILE
    tile, slot, valid = seg_ref[at, 2], seg_ref[at, 3], seg_ref[at, 4]
    queries = stack_heads(of_tile(at, tile, tiles, lambda place: q_ref[tile_rows(place), :]))
    row_pos = lane_positions(tile * TILE)

    scores = []
    for other in range(ENC // TILE):
        tile_scores = dot_nt(of_slot(slot, other, lambda place: keys[place]), queries)
        scores.append(masked_keys(tile_scores, other, valid))
    value, log_total = soft_sum(
        scores, lambda other: of_slot(slot, other, lambda place: values_t[place])
    )
    mine = (row_pos >= seg_ref[at, 0]) & (row_pos < seg_ref[at, 1])
    out[at] = value
    lse_ref[pl.ds(at, 1), :] = jnp.where(mine, log_total, -NEG)


def join_segments(seg_ref, out, out_ref, tiles):
    for tile in tiles:
        row_pos = lane_positions(tile * TILE)
        total = jnp.zeros((HDIM, PAIR), FLOAT)
        for at in range(SEGMENTS):
            mine = (row_pos >= seg_ref[at, 0]) & (row_pos < seg_ref[at, 1])
            total = jnp.where(mine, out[at], total)
        out_ref[tile * TILE : (tile + 1) * TILE, :] = unstack_heads(total).astype(HALF)


SHARD = 64
FF_PAD = 384
ORDERS = ("zyx", "yxz", "xzy")
Y_LAST = ("xzy", "zxy")


class Torus:
    def __init__(self):
        tok, hid = lax.axis_index("tok"), lax.axis_index("hid")
        self.core = lax.rem(tok, 2)
        self.pos = {
            "x": lax.rem(tok // 2, 2) * 2 + lax.rem(hid, 2),
            "y": tok // 4,
            "z": hid // 2,
        }

    def moved(self, axis, step):
        place = dict(self.pos)
        place[axis] = lax.rem(place[axis] + step + 4, 4)
        return place

    def device(self, place, core=None):
        core = self.core if core is None else core
        return (
            (place["y"] * 2 + place["x"] // 2) * 2 + core,
            place["z"] * 2 + lax.rem(place["x"], 2),
        )

    def neighbour(self, axis, step):
        return self.device(self.moved(axis, step))

    def sibling(self):
        return self.device(self.pos, 1 - self.core)

    def beyond(self):
        return self.neighbour("x", 2)


def block_index(place, whole):
    return (
        slice(None) if "z" in whole else place["z"],
        slice(None) if "x" in whole else lax.rem(place["x"], 2),
        slice(None) if "y" in whole else place["y"],
        slice(None) if "x" in whole else place["x"] // 2,
    )


def whole_dims(whole):
    dims = (4,) if "z" in whole else ()
    dims += (2,) if "x" in whole else ()
    dims += (4,) if "y" in whole else ()
    return dims + ((2,) if "x" in whole else ())


class Flow:
    def __init__(self, torus, out_ref, cuts, orders, sems, own_ref=None):
        self.torus, self.out_ref, self.cuts, self.orders = torus, out_ref, cuts, orders
        self.sems, self.own_ref = sems, own_ref
        self.rows = out_ref.shape[5]
        self.sends, self.siblings = [], []
        self.last = {}

    def view(self, place, whole, cut, rows=None):
        rows = (0, self.rows) if rows is None else rows
        return self.out_ref.at[
            block_index(place, whole) + (self.torus.core, pl.ds(*rows), pl.ds(*cut))
        ]

    def copy(self, ref, target, first, log, src=None):
        at = len(log)
        copy = pltpu.make_async_remote_copy(
            src_ref=ref if src is None else src, dst_ref=ref,
            send_sem=self.sems[first].at[at], recv_sem=self.sems[first + 1].at[at],
            device_id=target, device_id_type=MESH,
        )
        copy.start()
        log.append(copy)
        return copy

    def to_sibling(self, place, whole, cut):
        self.copy(self.view(place, whole, cut), self.torus.sibling(), 2, self.siblings)

    def plan(self, stage):
        for part, cut in enumerate(self.cuts):
            yield part, cut, self.orders[part][stage], self.orders[part][:stage]

    def near(self, stage):
        torus = self.torus
        for part, cut, axis, whole in self.plan(stage):
            src = None
            if stage == 0:
                src = None if self.own_ref is None else self.own_ref.at[:, pl.ds(*cut)]
            ref = self.view(torus.pos, whole, cut)
            self.last[part] = [
                self.copy(ref, torus.neighbour(axis, step), 0, self.sends, src)
                for step in (1, -1)
            ]
            if stage == 2:
                self.to_sibling(torus.pos, whole, cut)

    def far(self, stage):
        torus, half = self.torus, self.rows // 2
        for part, cut, axis, whole in self.plan(stage):
            copies = []
            for copy, step, first in zip(self.last[part], (1, -1), (0, half)):
                origin = torus.moved(axis, -step)
                copy.wait_recv()
                if half >= 16:
                    ref = self.view(origin, whole, cut, (first, half))
                    copies.append(self.copy(ref, torus.neighbour(axis, step), 0, self.sends))
                elif step == 1:
                    ref = self.view(origin, whole, cut)
                    copies.append(self.copy(ref, torus.neighbour(axis, step), 0, self.sends))
                if stage == 2:
                    self.to_sibling(origin, whole, cut)
            self.last[part] = copies

    def done(self, stage):
        for part, cut, axis, whole in self.plan(stage):
            for copy in self.last[part]:
                copy.wait_recv()
            if stage == 2:
                self.to_sibling(self.torus.moved(axis, 2), whole, cut)

    def arrived(self):
        for copy in self.siblings:
            copy.wait_recv()

    def finish(self):
        for copy in self.sends + self.siblings:
            copy.wait_send()


def flow_sems(parts, split):
    sends = parts * 3 * (2 + split)
    return [pltpu.SemaphoreType.DMA((sends,))] * 2 + [pltpu.SemaphoreType.DMA((parts * 4,))] * 2


class Trade:
    def __init__(self, src, land, sems):
        self.src, self.land, self.sems = src, land, sems
        self.me = lax.axis_index("hid")
        self.tok = lax.axis_index("tok")

    def copy(self, step):
        target = lax.rem(self.me + step, 8)
        return pltpu.make_async_remote_copy(
            src_ref=self.src(target), dst_ref=self.land(self.me),
            send_sem=self.sems[0].at[step - 1], recv_sem=self.sems[1].at[step - 1],
            device_id=(self.tok, target), device_id_type=MESH,
        )

    def start_all(self):
        for step in range(1, 8):
            self.copy(step).start()

    def start_to(self, targets):
        for target in targets:
            step = lax.rem(target - self.me + 8, 8)

            @pl.when(step > 0)
            def _():
                self.copy(step).start()

    def arrived(self):
        for step in range(1, 8):
            self.copy(step).wait_recv()

    def finish(self):
        for step in range(1, 8):
            self.copy(step).wait_send()


def complete(tiles, rows, before):
    return range(before * TILE // rows, tiles * TILE // rows)


def trade_sems():
    return [pltpu.SemaphoreType.DMA((7,))] * 2


def greet(peers):
    barrier = pltpu.get_barrier_semaphore()
    for peer in peers:
        pl.semaphore_signal(barrier, inc=1, device_id=peer, device_id_type=MESH)
    return barrier, len(peers)


def hid_peers():
    tok, me = lax.axis_index("tok"), lax.axis_index("hid")
    return [(tok, lax.rem(me + step, 8)) for step in range(1, 8)]


def torus_peers(torus):
    outside = 2 * lax.rem(lax.axis_index("hid"), 2) - 1
    return [
        torus.neighbour("y", 1), torus.neighbour("y", -1), torus.neighbour("x", outside),
        torus.sibling(),
    ]


def rows_at(index, rows):
    return pl.ds(pl.multiple_of(index * rows, 64), rows)


def scale_of(row_vals):
    return lax.rsqrt(jnp.mean(row_vals * row_vals, axis=-1, keepdims=True) + EPS)


def norm_backward(row_vals, gain, gradient):
    scale = scale_of(row_vals)
    normal = row_vals * scale
    weighted = gradient * gain
    inner = jnp.mean(weighted * normal, axis=-1, keepdims=True)
    return scale * (weighted - normal * inner)


class Remote:
    def __init__(self, src, dst, sems, at, target):
        self.src, self.dst, self.sems, self.at, self.target = src, dst, sems, at, target

    def copy(self):
        return pltpu.make_async_remote_copy(
            src_ref=self.src(), dst_ref=self.dst(),
            send_sem=self.sems[0].at[self.at], recv_sem=self.sems[1].at[self.at],
            device_id=self.target(), device_id_type=MESH,
        )

    def start(self):
        self.copy().start()

    def wait_recv(self):
        self.copy().wait_recv()

    def wait_send(self):
        self.copy().wait_send()


class Pairs:
    def __init__(self, torus, sems):
        self.torus, self.sems, self.log = torus, sems, []

    def send(self, src, dst, target=None):
        target = self.torus.sibling if target is None else target
        copy = Remote(src, dst, self.sems, len(self.log), target)
        copy.start()
        self.log.append(copy)
        return copy

    def finish(self):
        for copy in self.log:
            copy.wait_send()


class Columns:
    def __init__(self, torus, buffer, sends):
        self.torus, self.buffer, self.sends = torus, buffer, sends
        self.siblings = []

    def send(self, step, half, target):
        torus = self.torus

        def ref():
            y = torus.moved("y", step)["y"]
            xhi = torus.pos["x"] // 2
            at = (slice(None), xhi, 1 - xhi)[0 if half is None else half + 1]
            return self.buffer.at[y, at, torus.core]

        return self.sends.send(ref, ref, target)

    def up(self):
        return self.torus.neighbour("y", 1)

    def down(self):
        return self.torus.neighbour("y", -1)

    def start(self):
        self.first = self.send(0, 0, self.torus.beyond)
        self.siblings.append(self.send(0, 0, None))

    def near(self):
        self.first.wait_recv()
        self.last = [self.send(0, None, self.up), self.send(0, None, self.down)]
        self.siblings.append(self.send(0, 1, None))

    def far(self):
        self.last[0].wait_recv()
        one = self.send(-1, 0, self.up)
        self.siblings.append(self.send(-1, None, None))
        self.last[1].wait_recv()
        two = self.send(1, 1, self.down)
        self.siblings.append(self.send(1, None, None))
        self.last = [one, two]

    def done(self):
        for copy in self.last:
            copy.wait_recv()
        self.siblings.append(self.send(2, None, None))

    def arrived(self):
        for copy in self.siblings:
            copy.wait_recv()


class Rows:
    def __init__(self, torus, buffer, sends):
        self.torus, self.buffer, self.sends = torus, buffer, sends
        self.half = buffer.shape[2] // 2

    def send(self, step, whole, rows, target):
        torus = self.torus

        def ref():
            z = torus.moved("z", step)["z"]
            xlo = slice(None) if whole else lax.rem(torus.pos["x"], 2)
            return self.buffer.at[z, xlo, pl.ds(*rows)]

        return self.sends.send(ref, ref, target)

    def partner(self):
        me = lax.axis_index("hid")
        return lax.axis_index("tok"), me + 1 - 2 * lax.rem(me, 2)

    def up(self):
        return self.torus.neighbour("z", 1)

    def down(self):
        return self.torus.neighbour("z", -1)

    def start(self):
        half = self.half
        self.one = [self.send(0, False, (0, half), to) for to in (self.up, self.down)]
        self.across = self.send(0, False, (half, half), self.partner)
        self.others = [self.send(0, False, (0, half), self.partner)]

    def near(self):
        half = self.half
        self.across.wait_recv()
        self.two = [self.send(0, True, (half, half), to) for to in (self.up, self.down)]

    def far(self, first):
        half, part = self.half, self.half // 2
        near, base, whole = (self.one, 0, False) if first else (self.two, half, True)
        near[0].wait_recv()
        copies = [self.send(-1, whole, (base, part), self.up)]
        if first:
            self.others.append(self.send(-1, False, (0, half), self.partner))
        near[1].wait_recv()
        copies.append(self.send(1, whole, (base + part, part), self.down))
        if first:
            self.others.append(self.send(1, False, (0, half), self.partner))
            self.one = copies
        else:
            self.two = copies

    def done(self, first):
        for copy in self.one if first else self.two:
            copy.wait_recv()
        if first:
            self.others.append(self.send(2, False, (0, self.half), self.partner))
        else:
            for copy in self.others:
                copy.wait_recv()


GATE_UP_CUTS = ((0, 256), (256, 256), (512, 256))
DOWN_CUTS = ((0, 128), (128, 128), (256, 128))
MIX_CUTS = ((0, 128), (128, 128))
EARLY_CUTS = ((0, 256),)
HALVES = ((0, 32), (32, 32))
QKV_CUTS = ((0, 128), (128, 128))
GATHER_MIX = ((0, 128), (128, 128), (256, 128))
GATHER_LAST = ((384, 128),)
GATHER_ONE = ((0, 128), (128, 256), (384, 256))
GATHER_TWO = ((640, 128), (768, 128), (896, 256))
TWO_ORDERS = ORDERS[:2] + Y_LAST[1:]

def forward_kernel(
    wq_ref, wk_ref, wv_ref, wo_ref, cq_ref, ck_ref, cv_ref, co_ref, wg_ref, wu_ref, wd_ref,
    norm_ref, rel_ref, tok_ref, mem_ref, bucket_ref, cot_ref, len_ref, slot_ref, enc_ref,
    wf_ref, wa_ref, wqkv_ref, yff_ref,
    h1_out, h2_out, qkv_out, kv_out, o1_out, o1r_out, x1_out, q2_out, o2_out, o2r_out,
    gain_ref, win_ref, lse_ref, lse2_ref, mixed_ref, g2_ref, do_ref, xt3_ref, xtc_ref,
    h1_ref, h2_ref, qkv_ref, kv_ref, o1_ref, o1r_ref, x1_ref, q2_ref, o2_ref, o2r_ref,
    wa, pack, w_first, small, token_rows, send_kv, send_q2, keys, values_t, bias,
    cross_keys, cross_values_t, cross_out, seg,
    h3, y_stage, xs3, xsc, xr3, xrc, w_ff, send_do, out_acc, in_acc,
    own_sem, ff_sem, y_sem, store_sem, *sems,
):
    torus = Torus()
    me = lax.axis_index("hid")
    rows, mem_rows = tok_ref.shape[0], mem_ref.shape[0]
    tiles = qkv_ref.shape[0] // TILE
    barrier, count = greet(hid_peers() + torus_peers(torus) + [torus.beyond()])
    stores = []

    def store(*pairs_of_refs):
        for src, dst in pairs_of_refs:
            copy = pltpu.make_async_copy(src, dst, store_sem.at[len(stores)])
            copy.start()
            stores.append(copy)

    here = block_index(torus.pos, "") + (torus.core,)
    z, xlo = torus.pos["z"], lax.rem(me, 2)
    y, xhi = torus.pos["y"], torus.pos["x"] // 2
    token_rows[z, xlo] = tok_ref[...]
    norms = norm_ref[...].astype(FLOAT)
    blank = jnp.zeros_like(norms)
    first = jnp.concatenate([norms, blank], axis=1)
    second = jnp.concatenate([blank, norms], axis=1)
    lines = [jnp.where(torus.core == 0, first, second)]
    table = rel_ref[...].astype(FLOAT)
    for part in range(2):
        for head in range(2):
            value = table[part : part + 1, head : head + 1]
            lines.append(jnp.broadcast_to(value, (1, 128)))
    lines.append(jnp.zeros((9, 128), FLOAT))
    small[y, xhi, torus.core] = jnp.concatenate(lines, axis=0).astype(HALF)
    w_first[y, xhi, torus.core] = jnp.concatenate(
        [wq_ref[...], wk_ref[...], wv_ref[...]], axis=1
    )
    wa[here] = jnp.concatenate(
        [wo_ref[...], cq_ref[...], ck_ref[...], cv_ref[...], co_ref[...]], axis=1
    )
    blank = jnp.zeros((SHARD, FF_PAD - wg_ref.shape[1]), HALF)
    pack[...] = jnp.concatenate(
        [wg_ref[...], blank, wu_ref[...], blank, wd_ref[...], blank], axis=1
    )
    own = pltpu.make_async_copy(pack, wf_ref.at[here], own_sem.at[0])
    own.start()
    flow_b = Flow(torus, wa, GATHER_MIX, ORDERS, sems[0:4])
    flow_c = Flow(torus, wa, GATHER_LAST, ORDERS[2:], sems[28:32])
    flow_f = Flow(torus, wf_ref, GATHER_ONE, ORDERS, sems[4:8], pack)
    flow_g = Flow(torus, wf_ref, GATHER_TWO, TWO_ORDERS, sems[32:36], pack)
    row_sends, column_sends = Pairs(torus, sems[8:10]), Pairs(torus, sems[10:12])
    gather_rows = Rows(torus, token_rows, row_sends)
    columns = [Columns(torus, w_first, column_sends), Columns(torus, small, column_sends)]
    kv_trade = Trade(
        lambda j: send_kv.at[j], lambda j: kv_ref.at[rows_at(j, mem_rows)], sems[12:14]
    )
    o1_trade = Trade(
        lambda j: o1_ref.at[rows_at(j, rows)], lambda j: o1r_ref.at[j], sems[14:16]
    )
    q2_trade = Trade(
        lambda j: send_q2.at[j], lambda j: q2_ref.at[rows_at(j, rows)], sems[16:18]
    )
    o2_trade = Trade(
        lambda j: o2_ref.at[rows_at(j, rows)], lambda j: o2r_ref.at[j], sems[18:20]
    )
    do_trade = Trade(
        lambda j: send_do.at[j], lambda j: do_ref.at[rows_at(j, rows)], sems[20:22]
    )
    pairs = Pairs(torus, sems[22:24])
    flow_w = Flow(
        torus, wqkv_ref, QKV_CUTS, Y_LAST, sems[24:28], w_first.at[y, xhi, torus.core]
    )
    own_first = pltpu.make_async_copy(
        w_first.at[y, xhi, torus.core], wqkv_ref.at[here], own_sem.at[1]
    )
    own_first.start()
    build_segments(seg, len_ref, slot_ref, enc_ref, tiles)
    split_columns(torus, cot_ref[...].astype(FLOAT), xtc_ref, xsc)
    pl.semaphore_wait(barrier, count)
    flow_w.near(0)
    flow_b.near(0)
    flow_g.near(0)
    gather_rows.start()
    for column in columns:
        column.start()
    flow_f.near(0)
    flow_w.far(0)
    flow_b.far(0)
    flow_c.near(0)
    flow_g.far(0)
    for column in columns:
        column.near()
    gather_rows.near()
    for column in columns:
        column.far()
    own.wait()
    own_first.wait()
    flow_f.far(0)
    gather_rows.far(True)
    flow_b.done(0)
    flow_g.done(0)
    for column in columns:
        column.done()
    flow_b.near(1)
    flow_c.far(0)
    gather_rows.far(False)
    flow_f.done(0)
    for column in columns:
        column.arrived()
    gain_parts = []
    heads = [jnp.zeros((8, PAIR), FLOAT), jnp.zeros((8, PAIR), FLOAT)]
    buckets = bucket_windows(bucket_ref)
    for pair in range(8):
        blocks = [small[pair // 2, pair % 2, core].astype(FLOAT) for core in range(2)]
        gain_parts.append((blocks[0] + blocks[1])[0:8])
        for core in range(2):
            for part in range(2):
                bucket = (pair * 2 + core) * 2 + part
                for head in range(2):
                    at = 3 + part * 2 + head
                    value = blocks[core][at : at + 1]
                    value = jnp.concatenate([value] * 4, axis=1)
                    heads[head] = jnp.where(buckets == bucket, value, heads[head])
    gain_ref[...] = jnp.concatenate(gain_parts, axis=1)
    after = lax.broadcasted_iota(jnp.int32, (8, PAIR), 0) * PAIR + lax.broadcasted_iota(
        jnp.int32, (8, PAIR), 1
    )
    after = (after >= TILE) & (after < PAIR)
    win_ref[0:8] = jnp.where(after, NEG, heads[0])
    win_ref[8:16] = jnp.where(after, NEG, heads[1])
    build_bias(win_ref, bias, tiles)
    flow_f.near(1)
    flow_b.far(1)
    flow_c.done(0)
    flow_c.near(1)
    gather_rows.done(True)
    flow_f.far(1)
    flow_b.done(1)
    flow_b.near(2)
    flow_c.far(1)
    gather_rows.done(False)
    for j in range(8):
        block = token_rows[j // 2, j % 2].astype(FLOAT)
        h1 = (block * scale_of(block) * gain_ref[0:1, :]).astype(HALF)
        h1_ref[j] = h1
        qkv = dot(h1, w_first[...].reshape(16 * SHARD, 256))
        qkv_ref[j * rows : (j + 1) * rows, :] = qkv.astype(HALF)
    store((h1_ref, h1_out), (qkv_ref, qkv_out))
    flow_f.done(1)
    flow_f.near(2)
    flow_b.far(2)
    flow_c.done(1)
    flow_g.near(1)

    def weights(j, first, width):
        block = wa[j // 2, j % 2, :, :, :, :, first : first + width]
        return block.reshape(16 * SHARD, width)

    def spread_trade(trade, left_ref, first, send_ref, land_ref):
        width = send_ref.shape[-1]
        spread(left_ref, lambda j: weights(j, first, width), send_ref)
        trade.start_all()
        land_ref[rows_at(me, left_ref.shape[0]), :] = send_ref[me]

    for tile in range(tiles):
        block = qkv_ref[tile * TILE : (tile + 1) * TILE, 128:256]
        keys[tile] = block[:, :HDIM]
        values_t[tile] = block[:, HDIM:].astype(FLOAT).T.astype(HALF)
    ends = doc_ends(len_ref)

    def row_tile(tile):
        at = slice(tile * TILE, (tile + 1) * TILE)
        queries = stack_heads(qkv_ref[at, 0:128])
        row_start = start_of(lane_positions(tile * TILE), ends)
        first = max(0, tile - LONG // TILE)
        scores = []
        for other in range(first, tile + 1):
            tile_scores = dot_nt(keys[other], queries) + bias[tile - other]
            key_pos = other * TILE + lax.broadcasted_iota(jnp.int32, (TILE, 1), 0)
            scores.append(jnp.where(key_pos >= row_start, tile_scores, NEG))
        value, log_total = soft_sum(scores, lambda other: values_t[first + other])
        o1_ref[at, :] = unstack_heads(value).astype(HALF)
        lse_ref[tile : tile + 1, :] = log_total

    for tile in range(tiles):
        row_tile(tile)
        o1_trade.start_to(complete(tile + 1, rows, tile))
        if tile == 3:
            flow_w.done(0)
            flow_c.near(2)
    o1r_ref[me] = o1_ref[rows_at(me, rows), :]
    flow_w.near(1)
    flow_b.done(2)
    flow_g.far(1)
    flow_b.arrived()
    spread_trade(kv_trade, mem_ref, 256, send_kv, kv_ref)
    store((o1_ref, o1_out))
    flow_w.far(1)
    copies = [pairs.send(lambda: xsc, lambda: xrc)]
    o1_trade.arrived()
    flow_c.far(2)
    flow_g.done(1)
    total = tok_ref[...].astype(FLOAT)
    for pair in range(4):
        left = jnp.concatenate([o1r_ref[2 * pair], o1r_ref[2 * pair + 1]], axis=1)
        right = jnp.concatenate(
            [weights(2 * pair, 0, 128), weights(2 * pair + 1, 0, 128)], axis=1
        )
        total = total + dot_nt(left, right)
    x1_ref[...] = total
    h2_ref[...] = (total * scale_of(total) * gain_ref[1:2, :]).astype(HALF)
    spread_trade(q2_trade, h2_ref, 128, send_q2, q2_ref)
    store((o1r_ref, o1r_out), (x1_ref, x1_out), (h2_ref, h2_out))
    flow_g.near(2)
    q2_trade.arrived()
    flow_f.far(2)
    kv_trade.arrived()
    store((q2_ref, q2_out), (kv_ref, kv_out))
    flow_w.done(1)
    for tile in range(kv_ref.shape[0] // TILE):
        block = kv_ref[tile * TILE : (tile + 1) * TILE, :]
        cross_keys[tile] = block[:, :HDIM]
        cross_values_t[tile] = block[:, HDIM:].astype(FLOAT).T.astype(HALF)

    def segment(at):
        cross_segment(at, seg, q2_ref, cross_keys, cross_values_t, cross_out, lse2_ref)

    done = 0
    for first, last in ((0, 2), (2, 4), (4, 6), (6, SEGMENTS)):
        pl.loop(first, last)(segment)
        join_segments(seg, cross_out, o2_ref, range(done, last - 2))
        o2_trade.start_to(complete(last - 2, rows, done))
        done = last - 2
        if last == 4:
            flow_c.done(2)
            flow_g.far(2)
        if last == 6:
            flow_w.near(2)
    flow_f.done(2)
    flow_g.done(2)
    o2r_ref[me] = o2_ref[rows_at(me, rows), :]
    flow_c.arrived()
    keep = pltpu.make_async_copy(wa, wa_ref, own_sem.at[0])
    keep.start()
    flow_f.arrived()
    flow_g.arrived()

    def fetch(j):
        slot = lax.rem(j, 2)
        return pltpu.make_async_copy(
            wf_ref.at[j // 2, lax.rem(j, 2)], w_ff.at[slot], ff_sem.at[slot]
        )

    fetch(0).start()
    o2_trade.arrived()
    store((o2_ref, o2_out), (o2r_ref, o2r_out))
    x_two = x1_ref[...]
    for pair in range(4):
        left = jnp.concatenate([o2r_ref[2 * pair], o2r_ref[2 * pair + 1]], axis=1)
        right = jnp.concatenate(
            [weights(2 * pair, 384, 128), weights(2 * pair + 1, 384, 128)], axis=1
        )
        x_two = x_two + dot_nt(left, right)
    out_acc[...] = x_two
    g2_ref[...] = x_two
    in_acc[...] = jnp.zeros_like(in_acc)
    h3[...] = (x_two * scale_of(x_two) * gain_ref[2:3, :]).astype(HALF)
    split_columns(torus, h3[...].astype(FLOAT), xt3_ref, xs3)
    copies.append(pairs.send(lambda: xs3, lambda: xr3))

    def stash(j):
        return pltpu.make_async_copy(
            y_stage.at[j], yff_ref.at[j, pl.ds(0, rows)], y_sem.at[0, j]
        )

    def share(j):
        return pltpu.make_async_remote_copy(
            src_ref=y_stage.at[j], dst_ref=yff_ref.at[j, pl.ds(rows, rows)],
            send_sem=y_sem.at[1, j], recv_sem=y_sem.at[2, j],
            device_id=torus.sibling(), device_id_type=MESH,
        )

    def ff_weight(slot, first, width):
        return w_ff[slot, :, :, :, :, first : first + width].reshape(16 * SHARD, width)

    def one_block(j):
        @pl.when(j < 7)
        def _():
            fetch(j + 1).start()

        fetch(j).wait()
        slot = lax.rem(j, 2)
        gate_up = dot(h3[...], ff_weight(slot, 0, 2 * FF_PAD))
        gate, up = gate_up[:, :FF_PAD], gate_up[:, FF_PAD:]
        d_hidden = dot(cot_ref[...], ff_weight(slot, 2 * FF_PAD, FF_PAD))
        curve = 0.7978845608028654 * (gate + 0.044715 * gate * gate * gate)
        bend = jnp.tanh(curve)
        gelu = 0.5 * gate * (1.0 + bend)
        slope = 0.5 * (1.0 + bend) + 0.5 * gate * (1.0 - bend * bend) * (
            0.7978845608028654 * (1.0 + 3.0 * 0.044715 * gate * gate)
        )
        hidden = (gelu * up).astype(HALF)
        y_stage[j, :, 2 * FF_PAD :] = hidden
        d_both = jnp.concatenate([d_hidden * up * slope, d_hidden * gelu], axis=1).astype(HALF)
        y_stage[j, :, 0 : 2 * FF_PAD] = d_both
        stash(j).start()
        share(j).start()
        out_acc[...] += dot_nt(hidden, ff_weight(slot, 2 * FF_PAD, FF_PAD))
        in_acc[...] += dot_nt(d_both, ff_weight(slot, 0, 2 * FF_PAD))

    pl.loop(0, 2)(one_block)
    pl.loop(2, 4)(one_block)
    pl.loop(4, 6)(one_block)
    flow_w.far(2)
    pl.loop(6, 8)(one_block)
    mixed_ref[...] = out_acc[...].astype(HALF)
    d_inner = norm_backward(g2_ref[...], gain_ref[2:3, :], in_acc[...])
    g_two = cot_ref[...].astype(FLOAT) + d_inner
    g2_ref[...] = g_two
    h3[...] = g_two.astype(HALF)
    spread(h3, lambda j: weights(j, 384, 128), send_do)
    do_trade.start_all()
    do_ref[rows_at(me, rows), :] = send_do[me]
    flow_w.done(2)
    for copy in copies:
        copy.wait_recv()
    join_columns(xtc_ref, xrc)
    join_columns(xt3_ref, xr3)
    do_trade.arrived()
    flow_w.arrived()
    for trade in (kv_trade, o1_trade, q2_trade, o2_trade, do_trade):
        trade.finish()
    for flow in (flow_b, flow_c, flow_f, flow_g, flow_w, row_sends, column_sends, pairs):
        flow.finish()
    keep.wait()
    for copy in stores:
        copy.wait()

    @pl.loop(0, 8)
    def settle(j):
        stash(j).wait()
        share(j).wait()


def forward(vectors, scalars):
    tokens, memory = vectors[13:15]
    rows, mem_rows = tokens.shape[0], memory.shape[0]
    group, keys = rows * 8, mem_rows * 8
    tiles, key_tiles = group // TILE, keys // TILE
    vmem = pl.BlockSpec(memory_space=pltpu.VMEM)
    smem = pl.BlockSpec(memory_space=pltpu.SMEM)
    anywhere = pl.BlockSpec(memory_space=pl.ANY)
    shape = jax.ShapeDtypeStruct
    places = (4, 2, 4, 2, 2)
    turned = (4, 2, SHARD, rows)
    big = (
        shape((8, rows, 1024), HALF),
        shape((rows, 1024), HALF),
        shape((group, 256), HALF),
        shape((keys, 128), HALF),
        shape((group, 128), HALF),
        shape((8, rows, 128), HALF),
        shape((rows, 1024), FLOAT),
        shape((group, 128), HALF),
        shape((group, 128), HALF),
        shape((8, rows, 128), HALF),
    )
    return pl.pallas_call(
        forward_kernel,
        out_shape=(
            shape(places + (SHARD, 1152), HALF),
            shape(places + (SHARD, 512), HALF),
            shape(places + (SHARD, 256), HALF),
            shape((8, 2 * rows, 3 * FF_PAD), HALF),
        )
        + big
        + (
            shape((8, 1024), FLOAT),
            shape((16, PAIR), FLOAT),
            shape((8, PAIR), FLOAT),
            shape((8, PAIR), FLOAT),
            shape((rows, 1024), HALF),
            shape((rows, 1024), FLOAT),
            shape((group, 128), HALF),
            shape((4, 2, SHARD, 2 * rows), HALF),
            shape((4, 2, SHARD, 2 * rows), HALF),
        ),
        in_specs=[vmem] * 17 + [smem] * 3,
        out_specs=(anywhere,) * 14 + (vmem,) * 9,
        scratch_shapes=[pltpu.VMEM(one.shape, one.dtype) for one in big]
        + [
            pltpu.VMEM(places + (SHARD, 512), HALF),
            pltpu.VMEM((SHARD, 1152), HALF),
            pltpu.VMEM((4, 2, 2, SHARD, 256), HALF),
            pltpu.VMEM((4, 2, 2, 16, 128), HALF),
            pltpu.VMEM((4, 2, rows, 1024), HALF),
            pltpu.VMEM((8, mem_rows, 128), HALF),
            pltpu.VMEM((8, rows, 128), HALF),
            pltpu.VMEM((tiles, TILE, HDIM), HALF),
            pltpu.VMEM((tiles, HDIM, TILE), HALF),
            pltpu.VMEM((tiles, TILE, PAIR), FLOAT),
            pltpu.VMEM((key_tiles, TILE, HDIM), HALF),
            pltpu.VMEM((key_tiles, HDIM, TILE), HALF),
            pltpu.VMEM((SEGMENTS, HDIM, PAIR), FLOAT),
            pltpu.SMEM((SEGMENTS, 8), jnp.int32),
            pltpu.VMEM((rows, 1024), HALF),
            pltpu.VMEM((8, rows, 3 * FF_PAD), HALF),
        ]
        + [pltpu.VMEM(turned, HALF)] * 4
        + [
            pltpu.VMEM((2, 4, 2, 2, SHARD, 1152), HALF),
            pltpu.VMEM((8, rows, 128), HALF),
            pltpu.VMEM((rows, 1024), FLOAT),
            pltpu.VMEM((rows, 1024), FLOAT),
            pltpu.SemaphoreType.DMA((2,)),
            pltpu.SemaphoreType.DMA((2,)),
            pltpu.SemaphoreType.DMA((3, 8)),
            pltpu.SemaphoreType.DMA((10,)),
        ]
        + flow_sems(3, 2) + flow_sems(3, 2)
        + [pltpu.SemaphoreType.DMA((13,))] * 2 + [pltpu.SemaphoreType.DMA((20,))] * 2
        + trade_sems() * 5
        + [pltpu.SemaphoreType.DMA((2,))] * 2 + flow_sems(2, 2)
        + flow_sems(1, 2) + flow_sems(3, 2),
        compiler_params=pltpu.CompilerParams(
            collective_id=0, has_side_effects=True, vmem_limit_bytes=62 * 2**20
        ),
    )(*vectors, *scalars)


class Drain:
    def __init__(self, torus, acc, out_ref, cuts, orders, halves, buffers, sems):
        self.torus, self.acc, self.out_ref = torus, acc, out_ref
        self.cuts, self.orders, self.halves = cuts, orders, halves
        self.buffers, self.sems = buffers, sems
        self.rows = (0, acc.shape[4])
        self.sends, self.last = [], {}

    def plan(self, stage):
        for part, cut in enumerate(self.cuts):
            first = (stage * len(self.cuts) + part) * 2
            got, final = self.buffers[first : first + 2]
            yield part, cut, self.orders[part][stage], self.orders[part][:stage], got, final

    def view(self, place, whole, rows, cut):
        return self.acc.at[block_index(place, whole) + (pl.ds(*rows), pl.ds(*cut))]

    def send(self, axis, hops, step, whole, rows, cut, buffer, slot):
        copy = Remote(
            lambda: self.view(self.torus.moved(axis, hops), whole, rows, cut),
            lambda: buffer.at[slot],
            self.sems, len(self.sends),
            lambda: self.torus.neighbour(axis, step),
        )
        copy.start()
        self.sends.append(copy)
        return copy

    def add(self, place, whole, rows, cut, sources):
        dims = whole_dims(whole)
        count = 1
        for dim in dims:
            count *= dim

        def one(step):
            index, rest_of = [], step
            for dim in reversed(dims):
                index.append(lax.rem(rest_of, dim))
                rest_of = rest_of // dim
            index = index[::-1]
            left = iter(index)
            at = tuple(
                next(left) if isinstance(entry, slice) else entry
                for entry in block_index(place, whole)
            )
            where = at + (pl.ds(*rows), pl.ds(*cut))
            total = self.acc[where].astype(FLOAT)
            for buffer, slot in sources:
                total = total + buffer[(slot,) + tuple(index)].astype(FLOAT)
            self.acc[where] = total.astype(self.acc.dtype)

        if count == 1:
            one(jnp.int32(0))
        else:
            pl.loop(0, count)(one)

    def begin(self, stage):
        for part, cut, axis, whole, got, _ in self.plan(stage):
            self.last[part] = [
                self.send(axis, 2, 1 - 2 * slot, whole, rows, cut, got, slot)
                for slot, rows in enumerate(self.halves)
            ]

    def turn(self, stage):
        torus = self.torus
        for part, cut, axis, whole, got, final in self.plan(stage):
            copies = []
            for slot, step in enumerate((1, -1)):
                place = torus.moved(axis, step)
                if slot < len(self.halves):
                    self.last[part][slot].wait_recv()
                    self.add(place, whole, self.halves[slot], cut, [(got, slot)])
                copies.append(self.send(axis, step, step, whole, self.rows, cut, final, slot))
            self.last[part] = copies

    def settle(self, stage):
        for part, cut, axis, whole, _, final in self.plan(stage):
            for copy in self.last[part]:
                copy.wait_recv()
            if stage > 0:
                self.add(self.torus.pos, whole, self.rows, cut, [(final, 0), (final, 1)])
            else:
                mine = self.acc[block_index(self.torus.pos, "") + (slice(None), pl.ds(*cut))]
                self.out_ref[:, pl.ds(*cut)] = (
                    mine.astype(FLOAT) + final[0].astype(FLOAT) + final[1].astype(FLOAT)
                )

    def finish(self):
        for copy in self.sends:
            copy.wait_send()


def drain_scratch(cuts, orders, halves, rows, dtype):
    width = sum(cut[1] for cut in cuts)
    scratch = [pltpu.VMEM((4, 2, 4, 2, rows, width), dtype)]
    for stage in range(3):
        for part, cut in enumerate(cuts):
            dims = whole_dims(orders[part][:stage])
            scratch.append(pltpu.VMEM((len(halves),) + dims + (halves[0][1], cut[1]), dtype))
            scratch.append(pltpu.VMEM((2,) + dims + (rows, cut[1]), dtype))
    count = len(cuts) * 3 * (2 + len(halves))
    return scratch + [pltpu.SemaphoreType.DMA((count,))] * 2


def split_columns(torus, value, mine_ref, other_ref):
    size = value.shape[0]
    turned = value.T.astype(HALF).reshape(4, 2, 2, SHARD, size)
    first = torus.core == 0
    mine_ref[:, :, :, 0:size] = jnp.where(first, turned[:, :, 0], turned[:, :, 1])
    other_ref[...] = jnp.where(first, turned[:, :, 1], turned[:, :, 0])


def join_columns(turned, arrived):
    size = arrived.shape[-1]
    turned[...] = jnp.concatenate([turned[:, :, :, 0:size], arrived[...]], axis=-1)


def fill_product(acc, first, width, turned, right, unroll):
    @pl.loop(0, 8, unroll=unroll)
    def one_j(j):
        left = turned[...].reshape(8 * SHARD, turned.shape[-1])
        value = dot(left, right(j)).astype(HALF)
        acc[j // 2, lax.rem(j, 2), :, :, :, first : first + width] = value.reshape(
            4, 2, SHARD, width
        )


def spread(left_ref, weights, send_ref):
    width = send_ref.shape[-1]
    group = max(1, 256 // width)
    for first in range(0, 8, group):
        right = [weights(first + at) for at in range(group)]
        right = right[0] if group == 1 else jnp.concatenate(right, axis=1)
        value = dot(left_ref[...], right).astype(HALF)
        for at in range(group):
            send_ref[first + at] = value[:, at * width : (at + 1) * width]


def backward_kernel(
    lse2_ref, g2_ref, mem_ref, h2_ref, gain_ref, xt3_ref, xtc_ref, win_ref, lse_ref, bucket_ref,
    wq_ref, wk_ref, wv_ref, cq_ref, wg_ref, wu_ref,
    norm_ref, len_ref, slot_ref, enc_ref,
    q2_in, kv2_in, do2_in, o2_in, x1_in, tok_in, qkv_in, o1_in, h1_ref, o1r_ref, o2r_ref, wa_ref, wqkv_ref, yff_ref,
    dtok_ref, gu_out, down_out, mix_out, early_out, qkv_out, last_out, dnorm_ref, dmem_ref,
    *rest,
):
    rest = list(rest)

    def take(count):
        taken = rest[:count]
        del rest[:count]
        return taken

    q2_ref, kv2_ref, do2_ref, o2_ref, x1_ref, tok_ref, qkv_ref, o1_ref = take(8)
    y_o1, y_o2, y_q2, y_kv2, y_qkv, h1_turned = take(6)
    xt_h2, xt_mem, xt_g1, xt_g2 = take(4)
    xs_h2, xs_mem, xs_g1, xs_g2 = take(4)
    xr_h2, xr_mem, xr_g1, xr_g2 = take(4)
    g1_half, send_do, do_ref, dqkv_ref, dq2_ref, dkv2_ref, seg = take(7)
    t_acc, t_send, t_recv, tx_send, tx_recv, ty_send, ty_recv = take(7)
    s_all, s_acc, s_recv, sx_send, sx_recv, sy_send, sy_recv = take(7)
    n_send, n_recv = take(2)
    gu_scratch, down_scratch, mix_scratch, early_scratch = take(19), take(19), take(13), take(7)
    local_sem = rest.pop(0)
    sems = rest
    gu_sems, down_sems, mix_sems, early_sems = sems[0:2], sems[2:4], sems[4:6], sems[6:8]
    pair_sems, trade_sem = sems[8:10], sems[10:20]

    torus = Torus()
    me = lax.axis_index("hid")
    y, xhi = torus.pos["y"], torus.pos["x"] // 2
    rows, mem_rows = tok_ref.shape[0], mem_ref.shape[0]
    tiles = qkv_ref.shape[0] // TILE
    barrier, count = greet(
        hid_peers() + torus_peers(torus) + [torus.beyond(), torus.neighbour("y", 2)]
    )
    owns = [
        pltpu.make_async_copy(o1r_ref, y_o1.at[:, pl.ds(0, rows)], local_sem.at[0]),
        pltpu.make_async_copy(o2r_ref, y_o2.at[:, pl.ds(0, rows)], local_sem.at[1]),
    ]
    for own in owns:
        own.start()
    sources = (q2_in, kv2_in, do2_in, o2_in, x1_in, tok_in, qkv_in, o1_in)
    targets = (q2_ref, kv2_ref, do2_ref, o2_ref, x1_ref, tok_ref, qkv_ref, o1_ref)
    late = [
        pltpu.make_async_copy(src, dst, local_sem.at[4 + at])
        for at, (src, dst) in enumerate(zip(sources, targets))
    ]
    for copy in late:
        copy.start()
    dq2_trade = Trade(
        lambda j: dq2_ref.at[rows_at(j, rows)], lambda j: y_q2.at[j, pl.ds(0, rows)],
        trade_sem[0:2],
    )
    dkv2_trade = Trade(
        lambda j: dkv2_ref.at[rows_at(j, mem_rows)], lambda j: y_kv2.at[j, pl.ds(0, mem_rows)],
        trade_sem[2:4],
    )
    do_trade = Trade(
        lambda j: send_do.at[j], lambda j: do_ref.at[rows_at(j, rows)], trade_sem[4:6]
    )
    dqkv_trade = Trade(
        lambda j: dqkv_ref.at[rows_at(j, rows)], lambda j: y_qkv.at[j], trade_sem[6:8]
    )
    norm_trade = Trade(lambda j: n_send, lambda j: n_recv.at[j], trade_sem[8:10])
    pairs = Pairs(torus, pair_sems)

    def share(buffer, size):
        return pairs.send(
            lambda: buffer.at[:, pl.ds(0, size)], lambda: buffer.at[:, pl.ds(size, size)]
        )

    drain_gu = Drain(
        torus, gu_scratch[0], gu_out, GATE_UP_CUTS, ORDERS, HALVES, gu_scratch[1:], gu_sems
    )
    drain_down = Drain(
        torus, down_scratch[0], down_out, DOWN_CUTS, ORDERS, HALVES, down_scratch[1:], down_sems
    )
    drain_mix = Drain(
        torus, mix_scratch[0], mix_out, MIX_CUTS, ORDERS, HALVES, mix_scratch[1:], mix_sems,
    )
    drain_early = Drain(
        torus, early_scratch[0], early_out, EARLY_CUTS, (ORDERS[2],), HALVES, early_scratch[1:],
        early_sems,
    )

    build_segments(seg, len_ref, slot_ref, enc_ref, tiles)

    def load_ff(yff, h1):
        load = pltpu.make_async_copy(yff_ref, yff, local_sem.at[2])
        load.start()
        load_h1 = pltpu.make_async_copy(h1_ref, h1, local_sem.at[3])
        load_h1.start()
        split_columns(torus, g2_ref[...], xt_g2, xs_g2)
        split_columns(torus, h2_ref[...].astype(FLOAT), xt_h2, xs_h2)
        split_columns(torus, mem_ref[...].astype(FLOAT), xt_mem, xs_mem)
        load.wait()
        fill_product(gu_scratch[0], 0, 768, xt3_ref, lambda j: yff[j, :, 0:768], 4)
        fill_product(down_scratch[0], 0, 384, xtc_ref, lambda j: yff[j, :, 768:1152], 4)
        load_h1.wait()
        for pair in range(4):
            block = h1[2 * pair : 2 * pair + 2].reshape(2 * rows, 1024)
            h1_turned[:, 2 * rows * pair : 2 * rows * (pair + 1)] = (
                block.astype(FLOAT).T.astype(HALF)
            )

    pl.run_scoped(
        load_ff, pltpu.VMEM((8, 2 * rows, 1152), HALF), pltpu.VMEM((8, rows, 1024), HALF)
    )

    pl.semaphore_wait(barrier, count)
    drain_gu.begin(2)
    drain_down.begin(2)
    pair_g2 = pairs.send(lambda: xs_g2, lambda: xr_g2)
    pair_h2 = pairs.send(lambda: xs_h2, lambda: xr_h2)
    pair_mem = pairs.send(lambda: xs_mem, lambda: xr_mem)
    for own in owns + late:
        own.wait()
    pair_y = [share(y, size) for y, size in ((y_o1, rows), (y_o2, rows))]

    def cross_attention(keys, values, keys_t, queries, grads, deltas, dq, dkv):
        for tile in range(kv2_ref.shape[0] // TILE):
            block = kv2_ref[tile * TILE : (tile + 1) * TILE, :]
            keys[tile] = block[:, :HDIM]
            values[tile] = block[:, HDIM:]
            keys_t[tile] = block[:, :HDIM].astype(FLOAT).T.astype(HALF)
        row_prepare(tiles, lambda at: q2_ref[at, :], do2_ref, o2_ref, queries, grads, deltas)
        dkv[...] = jnp.zeros_like(dkv)

        def segment(at):
            tile, slot, valid = seg[at, 2], seg[at, 3], seg[at, 4]
            query = of_tile(at, tile, tiles, lambda place: queries[place])
            grad = of_tile(at, tile, tiles, lambda place: grads[place])
            delta = of_tile(at, tile, tiles, lambda place: deltas[place])

            def whole(ref, axis):
                parts = [of_slot(slot, other, lambda place: ref[place]) for other in range(4)]
                return jnp.concatenate(parts, axis=axis)

            scores = masked_keys(dot_nt(whole(keys, 0), query), 0, valid)
            weights = jnp.exp(scores - lse2_ref[pl.ds(at, 1), :])
            d_weights = dot_nt(whole(values, 0), grad)
            d_half = (weights * (d_weights - delta)).astype(HALF)
            dq[at] = dot(whole(keys_t, 1), d_half)
            both = jnp.concatenate(
                [dot(d_half, query), dot(weights.astype(HALF), grad)], axis=1
            )
            for memory in range(3):
                dkv[memory] += jnp.where(slot == memory, both, 0.0)

        done = 0
        for first, last in ((0, 2), (2, 4), (4, 6), (6, SEGMENTS)):
            pl.loop(first, last)(segment)
            for tile in range(done, last - 2):
                total = jnp.zeros((HDIM, PAIR), FLOAT)
                for at in range(tile, tile + 3):
                    total = total + jnp.where(seg[at, 2] == tile, dq[at], 0.0)
                dq2_ref[tile * TILE : (tile + 1) * TILE, :] = unstack_heads(total).astype(HALF)
            dq2_trade.start_to(complete(last - 2, rows, done))
            done = last - 2
            if last == 4:
                drain_gu.turn(2)
        for memory in range(3):
            dkv2_ref[memory * ENC : (memory + 1) * ENC, :] = dkv[memory].astype(HALF)
        dkv2_trade.start_all()
        y_q2[me, 0:rows] = dq2_ref[rows_at(me, rows), :]
        y_kv2[me, 0:mem_rows] = dkv2_ref[rows_at(me, mem_rows), :]

    key_tiles = kv2_ref.shape[0] // TILE
    pl.run_scoped(
        cross_attention,
        pltpu.VMEM((key_tiles, TILE, HDIM), HALF),
        pltpu.VMEM((key_tiles, TILE, HDIM), HALF),
        pltpu.VMEM((key_tiles, HDIM, TILE), HALF),
        pltpu.VMEM((tiles, PAIR, HDIM), HALF),
        pltpu.VMEM((tiles, PAIR, HDIM), HALF),
        pltpu.VMEM((tiles, 1, PAIR), FLOAT),
        pltpu.VMEM((SEGMENTS, HDIM, PAIR), FLOAT),
        pltpu.VMEM((3, ENC, 2 * HDIM), FLOAT),
    )

    def inner(w_in, w_out, dmem):
        loads = [
            pltpu.make_async_copy(wa_ref.at[:, :, pl.ds(128, 256)], w_in, local_sem.at[2]),
            pltpu.make_async_copy(wa_ref.at[:, :, pl.ds(0, 128)], w_out, local_sem.at[3]),
        ]
        for load in loads:
            load.start()
        for load in loads:
            load.wait()
        dq2_trade.arrived()
        drain_gu.settle(2)
        pair_q2 = share(y_q2, rows)
        total = jnp.zeros((rows, 1024), FLOAT)
        for pair in range(4):
            left = [y_q2[2 * pair + side, 0:rows] for side in range(2)]
            right = [w_in[2 * pair + side, :, 0:128] for side in range(2)]
            total = total + dot_nt(
                jnp.concatenate(left, axis=1), jnp.concatenate(right, axis=1)
            )
        d_inner = norm_backward(x1_ref[...], gain_ref[1:2, :], total)
        g_one = g2_ref[...] + d_inner
        dtok_ref[...] = g_one
        g1_half[...] = g_one.astype(HALF)

        spread(g1_half, lambda j: w_out[j], send_do)
        do_trade.start_all()
        do_ref[rows_at(me, rows), :] = send_do[me]
        drain_gu.begin(1)
        drain_down.turn(2)
        split_columns(torus, dtok_ref[...], xt_g1, xs_g1)
        pair_g1 = pairs.send(lambda: xs_g1, lambda: xr_g1)
        dkv2_trade.arrived()
        pair_kv2 = share(y_kv2, mem_rows)
        for pair in range(4):
            left = [y_kv2[2 * pair + side, 0:mem_rows] for side in range(2)]
            right = [w_in[2 * pair + side, :, 128:256] for side in range(2)]
            value = dot_nt(jnp.concatenate(left, axis=1), jnp.concatenate(right, axis=1))
            dmem[...] = value if pair == 0 else dmem[...] + value
        store = pltpu.make_async_copy(dmem, dmem_ref, local_sem.at[2])
        store.start()
        for copy in [pair_g2, pair_mem, pair_kv2, pair_y[1]]:
            copy.wait_recv()
        join_columns(xt_mem, xr_mem)
        join_columns(xt_g2, xr_g2)
        fill_product(early_scratch[0], 0, 128, xt_mem, lambda j: y_kv2[j], 4)
        fill_product(early_scratch[0], 128, 128, xt_g2, lambda j: y_o2[j], 8)
        drain_early.begin(2)
        for copy in [pair_h2, pair_q2, pair_g1, pair_y[0]]:
            copy.wait_recv()
        join_columns(xt_g1, xr_g1)
        join_columns(xt_h2, xr_h2)
        fill_product(mix_scratch[0], 128, 128, xt_h2, lambda j: y_q2[j], 8)
        fill_product(mix_scratch[0], 0, 128, xt_g1, lambda j: y_o1[j], 8)
        drain_mix.begin(2)
        store.wait()

    pl.run_scoped(
        inner,
        pltpu.VMEM((8, 1024, 256), HALF),
        pltpu.VMEM((8, 1024, 128), HALF),
        pltpu.VMEM((mem_rows, 1024), FLOAT),
    )

    core_copies = []

    def self_attention(keys, values, keys_t, queries, grads, deltas, bias, bias_grad, dq):
        build_bias(win_ref, bias, tiles)
        for tile in range(tiles):
            block = qkv_ref[tile * TILE : (tile + 1) * TILE, 128:256]
            keys[tile] = block[:, :HDIM]
            values[tile] = block[:, HDIM:]
            keys_t[tile] = block[:, :HDIM].astype(FLOAT).T.astype(HALF)
        bias_grad[...] = jnp.zeros_like(bias_grad)
        dq[...] = jnp.zeros_like(dq)
        ends = doc_ends(len_ref)
        drain_gu.turn(1)
        do_trade.arrived()
        row_prepare(
            tiles, lambda at: qkv_ref[at, 0:128], do_ref, o1_ref, queries, grads, deltas
        )

        def key_tile(other):
            key_pos = other * TILE + lax.broadcasted_iota(jnp.int32, (TILE, 1), 0)
            dk, dv = jnp.zeros((TILE, HDIM), FLOAT), jnp.zeros((TILE, HDIM), FLOAT)
            for tile in range(other, min(tiles, other + LONG // TILE + 1)):
                row_start = start_of(lane_positions(tile * TILE), ends)
                scores = dot_nt(keys[other], queries[tile]) + bias[tile - other]
                scores = jnp.where(key_pos >= row_start, scores, NEG)
                weights = jnp.exp(scores - lse_ref[tile : tile + 1, :])
                d_weights = dot_nt(values[other], grads[tile])
                d_scores = weights * (d_weights - deltas[tile])
                bias_grad[tile - other] += d_scores
                d_half = d_scores.astype(HALF)
                dv = dv + dot(weights.astype(HALF), grads[tile])
                dk = dk + dot(d_half, queries[tile])
                dq[tile] += dot(keys_t[other], d_half)
            at = slice(other * TILE, (other + 1) * TILE)
            dqkv_ref[at, 128:256] = jnp.concatenate([dk, dv], axis=1).astype(HALF)

        for other in range(tiles):
            key_tile(other)
            at = slice(other * TILE, (other + 1) * TILE)
            dqkv_ref[at, 0:128] = unstack_heads(dq[other]).astype(HALF)
            dqkv_trade.start_to(complete(other + 1, rows, other))
            if other == 1:
                drain_mix.turn(2)
                drain_early.turn(2)
        y_qkv[me] = dqkv_ref[rows_at(me, rows), :]
        drain_gu.settle(1)
        drain_down.settle(2)
        drain_down.begin(1)
        drain_mix.settle(2)
        value = dot(h1_turned[...], dqkv_ref[...]).reshape(4, 2, 2, SHARD, 256)
        first = torus.core == 0
        t_acc[...] = jnp.where(first, value[:, :, 0], value[:, :, 1])
        t_send[...] = jnp.where(first, value[:, :, 1], value[:, :, 0]).astype(HALF)
        core_copies.append(pairs.send(lambda: t_send, lambda: t_recv))
        drain_mix.begin(1)
        sums = []
        for head in range(2):
            parts = []
            for tile in range(tiles):
                part = bias_grad[tile, :, head * TILE : (head + 1) * TILE]
                part = jnp.concatenate([part, jnp.zeros_like(part)], axis=1)
                parts.append(fold_diagonals(part))
            parts.append(jnp.zeros((8 - tiles, PAIR), FLOAT))
            sums.append(jnp.concatenate(parts, axis=0))
        buckets = bucket_windows(bucket_ref)
        s_all[...] = jnp.zeros_like(s_all)
        for bucket in range(32):
            mask = buckets == bucket
            shard, part = bucket // 2, bucket % 2
            for head in range(2):
                picked = jnp.where(mask, sums[head], 0.0)
                value = jnp.sum(jnp.sum(picked, axis=0, keepdims=True), axis=1, keepdims=True)
                at = 3 + part * 2 + head
                place = (shard % 2, shard // 4, shard // 2 % 2)
                s_all[place + (slice(at, at + 1), slice(None))] = jnp.broadcast_to(
                    value, (1, 128)
                )
        core_copies.append(pairs.send(lambda: s_all.at[1 - torus.core], lambda: s_recv))
        drain_early.settle(2)
        drain_early.begin(1)

    pl.run_scoped(
        self_attention,
        pltpu.VMEM((tiles, TILE, HDIM), HALF),
        pltpu.VMEM((tiles, TILE, HDIM), HALF),
        pltpu.VMEM((tiles, HDIM, TILE), HALF),
        pltpu.VMEM((tiles, PAIR, HDIM), HALF),
        pltpu.VMEM((tiles, PAIR, HDIM), HALF),
        pltpu.VMEM((tiles, 1, PAIR), FLOAT),
        pltpu.VMEM((tiles, TILE, PAIR), FLOAT),
        pltpu.VMEM((tiles, TILE, PAIR), FLOAT),
        pltpu.VMEM((tiles, HDIM, PAIR), FLOAT),
    )

    x_copies = []

    def first_inputs(w_in):
        load = pltpu.make_async_copy(wqkv_ref, w_in, local_sem.at[2])
        load.start()
        core_copies[0].wait_recv()
        t_acc[...] += t_recv[...].astype(FLOAT)
        tx_send[...] = t_acc[:, 1 - xhi].astype(HALF)
        x_copies.append(pairs.send(lambda: tx_send, lambda: tx_recv, torus.beyond))
        core_copies[1].wait_recv()
        s_acc[...] = s_all[torus.core] + s_recv[...]
        sx_send[...] = s_acc[:, 1 - xhi]
        x_copies.append(pairs.send(lambda: sx_send, lambda: sx_recv, torus.beyond))
        drain_gu.begin(0)
        drain_down.turn(1)
        drain_mix.turn(1)
        drain_early.turn(1)
        load.wait()
        dqkv_trade.arrived()
        total = jnp.zeros((rows, 1024), FLOAT)
        for j in range(8):
            total = total + dot_nt(y_qkv[j], w_in[j])
        residual = tok_ref[...].astype(FLOAT)
        dtok_ref[...] += norm_backward(residual, gain_ref[0:1, :], total)
        drain_gu.turn(0)
        drain_down.settle(1)
        drain_down.begin(0)
        drain_mix.settle(1)
        drain_mix.begin(0)
        drain_early.settle(1)
        drain_early.begin(0)

    pl.run_scoped(first_inputs, pltpu.VMEM((8, 1024, 256), HALF))
    for copy in x_copies:
        copy.wait_recv()
    t_acc[:, xhi] += tx_recv[...].astype(FLOAT)
    s_acc[:, xhi] += sx_recv[...]
    y_copies = []
    for at, step in enumerate((1, -1, 2)):
        place = torus.moved("y", step)["y"]
        ty_send[at] = t_acc[place, xhi].astype(HALF)
        sy_send[at] = s_acc[place, xhi]
        for src, dst in ((ty_send, ty_recv), (sy_send, sy_recv)):
            y_copies.append(
                pairs.send(
                    functools.partial(src.at.__getitem__, at),
                    functools.partial(dst.at.__getitem__, at),
                    functools.partial(torus.neighbour, "y", step),
                )
            )
    drain_gu.settle(0)
    drain_down.turn(0)
    drain_mix.turn(0)
    drain_early.turn(0)
    for copy in y_copies:
        copy.wait_recv()
    total, last = t_acc[y, xhi], s_acc[y, xhi]
    for at in range(3):
        total = total + ty_recv[at].astype(FLOAT)
        last = last + sy_recv[at]
    qkv_out[...] = total
    last_out[...] = last
    drain_down.settle(0)
    drain_mix.settle(0)
    drain_early.settle(0)

    def dotted(value, weight):
        return jnp.sum(value * weight.astype(FLOAT), axis=1, keepdims=True)

    width = wg_ref.shape[1]
    sums = [
        dotted(qkv_out[:, 0:128], wq_ref[...])
        + dotted(qkv_out[:, 128:192], wk_ref[...])
        + dotted(qkv_out[:, 192:256], wv_ref[...]),
        dotted(mix_out[:, 128:256], cq_ref[...]),
        dotted(gu_out[:, 0:width], wg_ref[...])
        + dotted(gu_out[:, FF_PAD : FF_PAD + width], wu_ref[...]),
    ]
    lane = lax.broadcasted_iota(jnp.int32, (SHARD, 128), 1)
    block = jnp.zeros((SHARD, 128), FLOAT)
    for at, value in enumerate(sums):
        block = jnp.where(lane == at, value, block)
    n_send[...] = block.T[0:8]
    norm_trade.start_all()
    n_recv[me] = n_send[...]
    norm_trade.arrived()
    value = n_recv[0]
    for j in range(1, 8):
        value = value + n_recv[j]
    dnorm_ref[...] = value
    dnorm_ref[0:3, :] = value[0:3] / norm_ref[...].astype(FLOAT)
    for drain in (drain_gu, drain_down, drain_mix, drain_early):
        drain.finish()
    for trade in (dq2_trade, dkv2_trade, do_trade, dqkv_trade, norm_trade):
        trade.finish()
    pairs.finish()


def backward(vectors, scalars, arrays):
    memory, tokens = vectors[2], arrays[5]
    rows, mem_rows = tokens.shape[0], memory.shape[0]
    group = rows * 8
    vmem = pl.BlockSpec(memory_space=pltpu.VMEM)
    smem = pl.BlockSpec(memory_space=pltpu.SMEM)
    anywhere = pl.BlockSpec(memory_space=pl.ANY)
    shape = jax.ShapeDtypeStruct
    drains = [
        drain_scratch(GATE_UP_CUTS, ORDERS, HALVES, SHARD, HALF),
        drain_scratch(DOWN_CUTS, ORDERS, HALVES, SHARD, HALF),
        drain_scratch(MIX_CUTS, ORDERS, HALVES, SHARD, HALF),
        drain_scratch(EARLY_CUTS, (ORDERS[2],), HALVES, SHARD, HALF),
    ]
    counts = (rows, mem_rows, rows, rows)
    scratch = [pltpu.VMEM(one.shape, one.dtype) for one in arrays[:8]]
    scratch += [pltpu.VMEM((8, 2 * rows, 128), HALF)] * 3
    scratch += [pltpu.VMEM((8, 2 * mem_rows, 128), HALF), pltpu.VMEM((8, rows, 256), HALF)]
    scratch += [pltpu.VMEM((1024, group), HALF)]
    scratch += [pltpu.VMEM((4, 2, SHARD, 2 * size), HALF) for size in counts]
    scratch += [pltpu.VMEM((4, 2, SHARD, size), HALF) for size in counts + counts]
    scratch += [
        pltpu.VMEM((rows, 1024), HALF),
        pltpu.VMEM((8, rows, 128), HALF),
        pltpu.VMEM((group, 128), HALF),
        pltpu.VMEM((group, 256), HALF),
        pltpu.VMEM((group, 128), HALF),
        pltpu.VMEM((mem_rows * 8, 128), HALF),
        pltpu.SMEM((SEGMENTS, 8), jnp.int32),
        pltpu.VMEM((4, 2, SHARD, 256), FLOAT),
        pltpu.VMEM((4, 2, SHARD, 256), HALF),
        pltpu.VMEM((4, 2, SHARD, 256), HALF),
        pltpu.VMEM((4, SHARD, 256), HALF),
        pltpu.VMEM((4, SHARD, 256), HALF),
        pltpu.VMEM((3, SHARD, 256), HALF),
        pltpu.VMEM((3, SHARD, 256), HALF),
        pltpu.VMEM((2, 4, 2, 16, 128), FLOAT),
        pltpu.VMEM((4, 2, 16, 128), FLOAT),
        pltpu.VMEM((4, 2, 16, 128), FLOAT),
        pltpu.VMEM((4, 16, 128), FLOAT),
        pltpu.VMEM((4, 16, 128), FLOAT),
        pltpu.VMEM((3, 16, 128), FLOAT),
        pltpu.VMEM((3, 16, 128), FLOAT),
        pltpu.VMEM((8, SHARD), FLOAT),
        pltpu.VMEM((8, 8, SHARD), FLOAT),
    ]
    for drain in drains:
        scratch += drain[:-2]
    scratch.append(pltpu.SemaphoreType.DMA((12,)))
    for drain in drains:
        scratch += drain[-2:]
    scratch += [pltpu.SemaphoreType.DMA((18,))] * 2 + trade_sems() * 5
    return pl.pallas_call(
        backward_kernel,
        out_shape=(
            shape((rows, 1024), FLOAT),
            shape((SHARD, 2 * FF_PAD), FLOAT),
            shape((SHARD, FF_PAD), FLOAT),
            shape((SHARD, 256), FLOAT),
            shape((SHARD, 256), FLOAT),
            shape((SHARD, 256), FLOAT),
            shape((16, 128), FLOAT),
            shape((8, SHARD), FLOAT),
            shape((mem_rows, 1024), FLOAT),
        ),
        in_specs=[vmem] * 17 + [smem] * 3 + [anywhere] * 14,
        out_specs=(vmem,) * 8 + (anywhere,),
        scratch_shapes=scratch,
        compiler_params=pltpu.CompilerParams(
            collective_id=1, has_side_effects=True, vmem_limit_bytes=64 * 2**20
        ),
    )(*vectors, *scalars, *arrays)


def finish_kernel(
    mixed_ref, dtok_ref, dmem_ref, gu_ref, down_ref, mix_ref, early_ref, qkv_ref, last_ref, dnorm_ref,
    mixed_out, dtok_out, dmem_out, n1_out, wq_out, wk_out, wv_out, wo_out, rel_out, n2_out,
    cq_out, ck_out, cv_out, co_out, n3_out, wg_out, wu_out, wd_out,
):
    mixed_out[...] = mixed_ref[...]
    dtok_out[...] = dtok_ref[...]
    dmem_out[...] = dmem_ref[...]
    for at, out in enumerate((n1_out, n2_out, n3_out)):
        out[...] = dnorm_ref[at : at + 1, :]
    rel_out[0:1, 0:1] = last_ref[3:4, 0:1]
    rel_out[0:1, 1:2] = last_ref[4:5, 0:1]
    rel_out[1:2, 0:1] = last_ref[5:6, 0:1]
    rel_out[1:2, 1:2] = last_ref[6:7, 0:1]
    wq_out[...] = qkv_ref[:, 0:128]
    wk_out[...] = qkv_ref[:, 128:192]
    wv_out[...] = qkv_ref[:, 192:256]
    wo_out[...] = mix_ref[:, 0:128]
    cq_out[...] = mix_ref[:, 128:256]
    ck_out[...] = early_ref[:, 0:64]
    cv_out[...] = early_ref[:, 64:128]
    co_out[...] = early_ref[:, 128:256]
    width = wg_out.shape[1]
    wg_out[...] = gu_ref[:, 0:width]
    wu_out[...] = gu_ref[:, FF_PAD : FF_PAD + width]
    wd_out[...] = down_ref[:, 0:width]


def finish_outputs(mixed, d_tokens, d_memory, grads, ff_width):
    vmem = pl.BlockSpec(memory_space=pltpu.VMEM)

    def shape(*dims):
        return jax.ShapeDtypeStruct(dims, FLOAT)

    return pl.pallas_call(
        finish_kernel,
        out_shape=(
            jax.ShapeDtypeStruct(mixed.shape, HALF),
            shape(*d_tokens.shape),
            shape(*d_memory.shape),
            shape(1, SHARD), shape(SHARD, 128), shape(SHARD, HDIM), shape(SHARD, HDIM),
            shape(SHARD, 128), shape(2, 2), shape(1, SHARD),
            shape(SHARD, 128), shape(SHARD, HDIM), shape(SHARD, HDIM), shape(SHARD, 128),
            shape(1, SHARD), shape(SHARD, ff_width), shape(SHARD, ff_width),
            shape(SHARD, ff_width),
        ),
        in_specs=[vmem] * 10,
        out_specs=(vmem,) * 18,
    )(mixed, d_tokens, d_memory, *grads)


def local(
    tokens, memory, cotangent, norm1, w_query, w_key, w_value, w_out, rel_bias, norm2,
    cross_query, cross_key, cross_value, cross_out, norm3, w_gate, w_up, w_down,
    doc_lengths, memory_slot, enc_lengths, rel_bucket,
):
    norms = jnp.stack([norm1, norm2, norm3])
    buckets = rel_bucket.reshape(-1, TILE)
    (
        _, wa, w_qkv, y_ff, h_one, h_two, qkv, kv_two, o_one, o_one_rows, x_one, q_two, o_two,
        o_two_rows, gains, windows, lse_one, lse_two, mixed, g_two, d_out, xt_three, xt_cot,
    ) = forward(
        (
            w_query, w_key, w_value, w_out.T, cross_query, cross_key, cross_value, cross_out.T,
            w_gate, w_up, w_down.T, norms, rel_bias, tokens, memory, buckets, cotangent,
        ),
        (doc_lengths, memory_slot, enc_lengths),
    )
    d_tokens, *grads, d_memory = backward(
        (
            lse_two, g_two, memory, h_two, gains, xt_three, xt_cot, windows, lse_one, buckets,
            w_query, w_key, w_value, cross_query, w_gate, w_up, norms,
        ),
        (doc_lengths, memory_slot, enc_lengths),
        (
            q_two, kv_two, d_out, o_two, x_one, tokens, qkv, o_one,
            h_one, o_one_rows, o_two_rows, wa.reshape(8, 16 * SHARD, 512),
            w_qkv.reshape(8, 16 * SHARD, 256), y_ff,
        ),
    )
    outs = list(finish_outputs(mixed, d_tokens, d_memory, grads, w_gate.shape[1]))
    for at in (3, 9, 14):
        outs[at] = outs[at][0]
    for at in (7, 13, 17):
        outs[at] = outs[at].T
    return tuple(outs)


def solution(mesh):
    return jax.shard_map(
        local,
        mesh=mesh,
        in_specs=(
            P(("tok", "hid"), None),
            P(("tok", "hid"), None),
            P(("tok", "hid"), None),
            P("tok"),
            P("tok", "hid"),
            P("tok", "hid"),
            P("tok", "hid"),
            P("hid", "tok"),
            P("tok", "hid"),
            P("tok"),
            P("tok", "hid"),
            P("tok", "hid"),
            P("tok", "hid"),
            P("hid", "tok"),
            P("tok"),
            P("tok", "hid"),
            P("tok", "hid"),
            P("hid", "tok"),
            P("tok", None),
            P("tok", None),
            P("tok", None),
            P(),
        ),
        out_specs=(
            P(("tok", "hid"), None),
            P(("tok", "hid"), None),
            P(("tok", "hid"), None),
            P("tok"),
            P("tok", "hid"),
            P("tok", "hid"),
            P("tok", "hid"),
            P("hid", "tok"),
            P("tok", "hid"),
            P("tok"),
            P("tok", "hid"),
            P("tok", "hid"),
            P("tok", "hid"),
            P("hid", "tok"),
            P("tok"),
            P("tok", "hid"),
            P("tok", "hid"),
            P("hid", "tok"),
        ),
        check_vma=False,
    )
```

```python
import functools

import jax
import jax.numpy as jnp
from jax import lax
from jax.experimental import pallas as pl
from jax.experimental.pallas import tpu as pltpu
from jax.sharding import PartitionSpec as P

EPS = 1e-06
MESH = pl.DeviceIdType.MESH

HDIM = 64
ENC = 1024
LONG = 1024
FLOAT = jnp.float32
HALF = jnp.bfloat16
TILE = 256
PAIR = 2 * TILE
NEG = -1e30
NT_DIMS = (((1,), (1,)), ((), ()))


def dot(first, second):
    return jnp.dot(first, second, preferred_element_type=FLOAT)


def dot_nt(first, second):
    return lax.dot_general(first, second, NT_DIMS, preferred_element_type=FLOAT)


def stack_heads(block):
    return jnp.concatenate([block[:, :HDIM], block[:, HDIM:]], axis=0)


def unstack_heads(columns):
    return jnp.concatenate(
        [columns[:, :TILE].T, columns[:, TILE:].T], axis=1
    )


def tile_rows(tile):
    return pl.ds(pl.multiple_of(tile * TILE, TILE), TILE)


def lane_positions(first):
    lane = lax.broadcasted_iota(jnp.int32, (1, PAIR), 1)
    return first + jnp.where(lane >= TILE, lane - TILE, lane)


def doc_ends(len_ref):
    first_end = len_ref[0, 0]
    return first_end, first_end + len_ref[0, 1]


def start_of(position, ends):
    return jnp.where(position >= ends[1], ends[1], jnp.where(position >= ends[0], ends[0], 0))


def build_bias(win_ref, bias, tiles):
    for diag in range(tiles):
        for head in range(2):
            row = win_ref[pl.ds(head * 8 + diag, 1), :]
            spread = jnp.broadcast_to(row, (TILE, PAIR))
            rolled = pltpu.roll(spread, 0, 1, stride=1, stride_axis=0)
            bias[diag, :, pl.ds(head * TILE, TILE)] = rolled[:, :TILE]


def soft_sum(scores, values_t):
    peak = jnp.max(scores[0], axis=0, keepdims=True)
    for tile in scores[1:]:
        peak = jnp.maximum(peak, jnp.max(tile, axis=0, keepdims=True))
    total, acc = None, None
    for at, tile in enumerate(scores):
        weights = jnp.exp(tile - peak)
        part = jnp.sum(weights, axis=0, keepdims=True)
        value = dot(values_t(at), weights.astype(HALF))
        total = part if at == 0 else total + part
        acc = value if at == 0 else acc + value
    return acc / total, peak + jnp.log(total)


def bucket_windows(bucket_ref):
    tiles = bucket_ref[...]
    count = tiles.shape[0]
    before = jnp.concatenate([tiles[0:1], tiles[0 : count - 1]], axis=0)
    windows = jnp.concatenate([tiles, before], axis=1)
    return jnp.concatenate([windows, jnp.zeros((8 - count, PAIR), jnp.int32)], axis=0)


def row_prepare(tiles, q_of, do_ref, o_ref, queries, grads, deltas):
    for tile in range(tiles):
        rows = slice(tile * TILE, (tile + 1) * TILE)
        queries[tile] = stack_heads(q_of(rows))
        block = do_ref[rows, :]
        grads[tile] = stack_heads(block)
        product = (block.astype(FLOAT) * o_ref[rows, :].astype(FLOAT)).T
        deltas[tile] = jnp.concatenate(
            [
                jnp.sum(product[:HDIM], axis=0, keepdims=True),
                jnp.sum(product[HDIM:], axis=0, keepdims=True),
            ],
            axis=1,
        )


def fold_diagonals(block):
    half = TILE // 2
    while half >= 8:
        block = block[:half] + pltpu.roll(block[half:], PAIR - half, 1)
        half //= 2
    total = block[0:1]
    for row in range(1, 8):
        total = total + pltpu.roll(block[row : row + 1], PAIR - row, 1)
    return total


SEGMENTS = 8


def build_segments(seg_ref, len_ref, slot_ref, enc_ref, tiles):
    ends = doc_ends(len_ref)
    starts = [(ends[0], (ends[0] + TILE - 1) // TILE), (ends[1], (ends[1] + TILE - 1) // TILE + 1)]
    for tile in range(tiles):
        first = tile * TILE
        before = (ends[0] <= first).astype(jnp.int32) + (ends[1] <= first).astype(jnp.int32)
        starts.append((first, tile + before))
    points = []
    for at in range(SEGMENTS):
        point = 0
        for value, order in starts:
            point = point + jnp.where(order == at, value, 0)
        points.append(point)
    points.append(tiles * TILE)
    for at in range(SEGMENTS):
        start = points[at]
        slot = jnp.where(
            start >= ends[1], slot_ref[0, 2],
            jnp.where(start >= ends[0], slot_ref[0, 1], slot_ref[0, 0]),
        )
        tile = 0
        for first in range(1, tiles):
            tile = tile + (start >= first * TILE).astype(jnp.int32)
        seg_ref[at, 0] = start
        seg_ref[at, 1] = points[at + 1]
        seg_ref[at, 2] = tile
        seg_ref[at, 3] = slot
        seg_ref[at, 4] = jnp.where(
            slot == 2, enc_ref[0, 2], jnp.where(slot == 1, enc_ref[0, 1], enc_ref[0, 0])
        )


def of_tile(at, tile, tiles, load):
    picked = load(jnp.minimum(at, tiles - 1))
    for back in (1, 2):
        other = jnp.maximum(jnp.minimum(at - back, tiles - 1), 0)
        picked = jnp.where(tile == at - back, load(other), picked)
    return picked


def of_slot(slot, other, load):
    picked = load(other)
    for memory in (1, 2):
        picked = jnp.where(slot == memory, load(memory * (ENC // TILE) + other), picked)
    return picked


def masked_keys(scores, tile, valid):
    key_pos = tile * TILE + lax.broadcasted_iota(jnp.int32, (scores.shape[0], 1), 0)
    return jnp.where(key_pos < valid, scores, NEG)


def cross_segment(at, seg_ref, q_ref, keys, values_t, out, lse_ref):
    tiles = q_ref.shape[0] // TILE
    tile, slot, valid = seg_ref[at, 2], seg_ref[at, 3], seg_ref[at, 4]
    queries = stack_heads(of_tile(at, tile, tiles, lambda place: q_ref[tile_rows(place), :]))
    row_pos = lane_positions(tile * TILE)

    scores = []
    for other in range(ENC // TILE):
        tile_scores = dot_nt(of_slot(slot, other, lambda place: keys[place]), queries)
        scores.append(masked_keys(tile_scores, other, valid))
    value, log_total = soft_sum(
        scores, lambda other: of_slot(slot, other, lambda place: values_t[place])
    )
    mine = (row_pos >= seg_ref[at, 0]) & (row_pos < seg_ref[at, 1])
    out[at] = value
    lse_ref[pl.ds(at, 1), :] = jnp.where(mine, log_total, -NEG)


def join_segments(seg_ref, out, out_ref, tiles):
    for tile in tiles:
        row_pos = lane_positions(tile * TILE)
        total = jnp.zeros((HDIM, PAIR), FLOAT)
        for at in range(SEGMENTS):
            mine = (row_pos >= seg_ref[at, 0]) & (row_pos < seg_ref[at, 1])
            total = jnp.where(mine, out[at], total)
        out_ref[tile * TILE : (tile + 1) * TILE, :] = unstack_heads(total).astype(HALF)


SHARD = 64
FF_PAD = 384
ORDERS = ("zyx", "yxz", "xzy")
Y_LAST = ("xzy", "zxy")


class Torus:
    def __init__(self):
        tok, hid = lax.axis_index("tok"), lax.axis_index("hid")
        self.core = lax.rem(tok, 2)
        self.pos = {
            "x": lax.rem(tok // 2, 2) * 2 + lax.rem(hid, 2),
            "y": tok // 4,
            "z": hid // 2,
        }

    def moved(self, axis, step):
        place = dict(self.pos)
        place[axis] = lax.rem(place[axis] + step + 4, 4)
        return place

    def device(self, place, core=None):
        core = self.core if core is None else core
        return (
            (place["y"] * 2 + place["x"] // 2) * 2 + core,
            place["z"] * 2 + lax.rem(place["x"], 2),
        )

    def neighbour(self, axis, step):
        return self.device(self.moved(axis, step))

    def sibling(self):
        return self.device(self.pos, 1 - self.core)

    def beyond(self):
        return self.neighbour("x", 2)


def block_index(place, whole):
    return (
        slice(None) if "z" in whole else place["z"],
        slice(None) if "x" in whole else lax.rem(place["x"], 2),
        slice(None) if "y" in whole else place["y"],
        slice(None) if "x" in whole else place["x"] // 2,
    )


def whole_dims(whole):
    dims = (4,) if "z" in whole else ()
    dims += (2,) if "x" in whole else ()
    dims += (4,) if "y" in whole else ()
    return dims + ((2,) if "x" in whole else ())


class Flow:
    def __init__(self, torus, out_ref, cuts, orders, sems, own_ref=None):
        self.torus, self.out_ref, self.cuts, self.orders = torus, out_ref, cuts, orders
        self.sems, self.own_ref = sems, own_ref
        self.rows = out_ref.shape[5]
        self.sends, self.siblings = [], []
        self.last = {}

    def view(self, place, whole, cut, rows=None):
        rows = (0, self.rows) if rows is None else rows
        return self.out_ref.at[
            block_index(place, whole) + (self.torus.core, pl.ds(*rows), pl.ds(*cut))
        ]

    def copy(self, ref, target, first, log, src=None):
        at = len(log)
        copy = pltpu.make_async_remote_copy(
            src_ref=ref if src is None else src, dst_ref=ref,
            send_sem=self.sems[first].at[at], recv_sem=self.sems[first + 1].at[at],
            device_id=target, device_id_type=MESH,
        )
        copy.start()
        log.append(copy)
        return copy

    def to_sibling(self, place, whole, cut):
        self.copy(self.view(place, whole, cut), self.torus.sibling(), 2, self.siblings)

    def plan(self, stage):
        for part, cut in enumerate(self.cuts):
            yield part, cut, self.orders[part][stage], self.orders[part][:stage]

    def near(self, stage):
        torus = self.torus
        for part, cut, axis, whole in self.plan(stage):
            src = None
            if stage == 0:
                src = None if self.own_ref is None else self.own_ref.at[:, pl.ds(*cut)]
            ref = self.view(torus.pos, whole, cut)
            self.last[part] = [
                self.copy(ref, torus.neighbour(axis, step), 0, self.sends, src)
                for step in (1, -1)
            ]
            if stage == 2:
                self.to_sibling(torus.pos, whole, cut)

    def far(self, stage):
        torus, half = self.torus, self.rows // 2
        for part, cut, axis, whole in self.plan(stage):
            copies = []
            for copy, step, first in zip(self.last[part], (1, -1), (0, half)):
                origin = torus.moved(axis, -step)
                copy.wait_recv()
                if half >= 16:
                    ref = self.view(origin, whole, cut, (first, half))
                    copies.append(self.copy(ref, torus.neighbour(axis, step), 0, self.sends))
                elif step == 1:
                    ref = self.view(origin, whole, cut)
                    copies.append(self.copy(ref, torus.neighbour(axis, step), 0, self.sends))
                if stage == 2:
                    self.to_sibling(origin, whole, cut)
            self.last[part] = copies

    def done(self, stage):
        for part, cut, axis, whole in self.plan(stage):
            for copy in self.last[part]:
                copy.wait_recv()
            if stage == 2:
                self.to_sibling(self.torus.moved(axis, 2), whole, cut)

    def arrived(self):
        for copy in self.siblings:
            copy.wait_recv()

    def finish(self):
        for copy in self.sends + self.siblings:
            copy.wait_send()


def flow_sems(parts, split):
    sends = parts * 3 * (2 + split)
    return [pltpu.SemaphoreType.DMA((sends,))] * 2 + [pltpu.SemaphoreType.DMA((parts * 4,))] * 2


class Trade:
    def __init__(self, src, land, sems):
        self.src, self.land, self.sems = src, land, sems
        self.me = lax.axis_index("hid")
        self.tok = lax.axis_index("tok")

    def copy(self, step):
        target = lax.rem(self.me + step, 8)
        return pltpu.make_async_remote_copy(
            src_ref=self.src(target), dst_ref=self.land(self.me),
            send_sem=self.sems[0].at[step - 1], recv_sem=self.sems[1].at[step - 1],
            device_id=(self.tok, target), device_id_type=MESH,
        )

    def start_all(self):
        for step in range(1, 8):
            self.copy(step).start()

    def start_to(self, targets):
        for target in targets:
            step = lax.rem(target - self.me + 8, 8)

            @pl.when(step > 0)
            def _():
                self.copy(step).start()

    def arrived(self):
        for step in range(1, 8):
            self.copy(step).wait_recv()

    def finish(self):
        for step in range(1, 8):
            self.copy(step).wait_send()


def complete(tiles, rows, before):
    return range(before * TILE // rows, tiles * TILE // rows)


def trade_sems():
    return [pltpu.SemaphoreType.DMA((7,))] * 2


def greet(peers):
    barrier = pltpu.get_barrier_semaphore()
    for peer in peers:
        pl.semaphore_signal(barrier, inc=1, device_id=peer, device_id_type=MESH)
    return barrier, len(peers)


def hid_peers():
    tok, me = lax.axis_index("tok"), lax.axis_index("hid")
    return [(tok, lax.rem(me + step, 8)) for step in range(1, 8)]


def torus_peers(torus):
    outside = 2 * lax.rem(lax.axis_index("hid"), 2) - 1
    return [
        torus.neighbour("y", 1), torus.neighbour("y", -1), torus.neighbour("x", outside),
        torus.sibling(),
    ]


def rows_at(index, rows):
    return pl.ds(pl.multiple_of(index * rows, 64), rows)


def scale_of(row_vals):
    return lax.rsqrt(jnp.mean(row_vals * row_vals, axis=-1, keepdims=True) + EPS)


def norm_backward(row_vals, gain, gradient):
    scale = scale_of(row_vals)
    normal = row_vals * scale
    weighted = gradient * gain
    inner = jnp.mean(weighted * normal, axis=-1, keepdims=True)
    return scale * (weighted - normal * inner)


class Remote:
    def __init__(self, src, dst, sems, at, target):
        self.src, self.dst, self.sems, self.at, self.target = src, dst, sems, at, target

    def copy(self):
        return pltpu.make_async_remote_copy(
            src_ref=self.src(), dst_ref=self.dst(),
            send_sem=self.sems[0].at[self.at], recv_sem=self.sems[1].at[self.at],
            device_id=self.target(), device_id_type=MESH,
        )

    def start(self):
        self.copy().start()

    def wait_recv(self):
        self.copy().wait_recv()

    def wait_send(self):
        self.copy().wait_send()


class Pairs:
    def __init__(self, torus, sems):
        self.torus, self.sems, self.log = torus, sems, []

    def send(self, src, dst, target=None):
        target = self.torus.sibling if target is None else target
        copy = Remote(src, dst, self.sems, len(self.log), target)
        copy.start()
        self.log.append(copy)
        return copy

    def finish(self):
        for copy in self.log:
            copy.wait_send()


class Columns:
    def __init__(self, torus, buffer, sends):
        self.torus, self.buffer, self.sends = torus, buffer, sends
        self.siblings = []

    def send(self, step, half, target):
        torus = self.torus

        def ref():
            y = torus.moved("y", step)["y"]
            xhi = torus.pos["x"] // 2
            at = (slice(None), xhi, 1 - xhi)[0 if half is None else half + 1]
            return self.buffer.at[y, at, torus.core]

        return self.sends.send(ref, ref, target)

    def up(self):
        return self.torus.neighbour("y", 1)

    def down(self):
        return self.torus.neighbour("y", -1)

    def start(self):
        self.first = self.send(0, 0, self.torus.beyond)
        self.siblings.append(self.send(0, 0, None))

    def near(self):
        self.first.wait_recv()
        self.last = [self.send(0, None, self.up), self.send(0, None, self.down)]
        self.siblings.append(self.send(0, 1, None))

    def far(self):
        self.last[0].wait_recv()
        one = self.send(-1, 0, self.up)
        self.siblings.append(self.send(-1, None, None))
        self.last[1].wait_recv()
        two = self.send(1, 1, self.down)
        self.siblings.append(self.send(1, None, None))
        self.last = [one, two]

    def done(self):
        for copy in self.last:
            copy.wait_recv()
        self.siblings.append(self.send(2, None, None))

    def arrived(self):
        for copy in self.siblings:
            copy.wait_recv()


class Rows:
    def __init__(self, torus, buffer, sends):
        self.torus, self.buffer, self.sends = torus, buffer, sends
        self.half = buffer.shape[2] // 2

    def send(self, step, whole, rows, target):
        torus = self.torus

        def ref():
            z = torus.moved("z", step)["z"]
            xlo = slice(None) if whole else lax.rem(torus.pos["x"], 2)
            return self.buffer.at[z, xlo, pl.ds(*rows)]

        return self.sends.send(ref, ref, target)

    def partner(self):
        me = lax.axis_index("hid")
        return lax.axis_index("tok"), me + 1 - 2 * lax.rem(me, 2)

    def up(self):
        return self.torus.neighbour("z", 1)

    def down(self):
        return self.torus.neighbour("z", -1)

    def start(self):
        half = self.half
        self.one = [self.send(0, False, (0, half), to) for to in (self.up, self.down)]
        self.across = self.send(0, False, (half, half), self.partner)
        self.others = [self.send(0, False, (0, half), self.partner)]

    def near(self):
        half = self.half
        self.across.wait_recv()
        self.two = [self.send(0, True, (half, half), to) for to in (self.up, self.down)]

    def far(self, first):
        half, part = self.half, self.half // 2
        near, base, whole = (self.one, 0, False) if first else (self.two, half, True)
        near[0].wait_recv()
        copies = [self.send(-1, whole, (base, part), self.up)]
        if first:
            self.others.append(self.send(-1, False, (0, half), self.partner))
        near[1].wait_recv()
        copies.append(self.send(1, whole, (base + part, part), self.down))
        if first:
            self.others.append(self.send(1, False, (0, half), self.partner))
            self.one = copies
        else:
            self.two = copies

    def done(self, first):
        for copy in self.one if first else self.two:
            copy.wait_recv()
        if first:
            self.others.append(self.send(2, False, (0, self.half), self.partner))
        else:
            for copy in self.others:
                copy.wait_recv()


GATE_UP_CUTS = ((0, 256), (256, 256), (512, 256))
DOWN_CUTS = ((0, 128), (128, 128), (256, 128))
MIX_CUTS = ((0, 128), (128, 128))
EARLY_CUTS = ((0, 256),)
HALVES = ((0, 32), (32, 32))
QKV_CUTS = ((0, 128), (128, 128))
GATHER_MIX = ((0, 128), (128, 128), (256, 128))
GATHER_LAST = ((384, 128),)
GATHER_ONE = ((0, 128), (128, 256), (384, 256))
GATHER_TWO = ((640, 128), (768, 128), (896, 256))
TWO_ORDERS = ORDERS[:2] + Y_LAST[1:]

def forward_kernel(
    wq_ref, wk_ref, wv_ref, wo_ref, cq_ref, ck_ref, cv_ref, co_ref, wg_ref, wu_ref, wd_ref,
    norm_ref, rel_ref, tok_ref, mem_ref, bucket_ref, cot_ref, len_ref, slot_ref, enc_ref,
    wf_ref, wa_ref, wqkv_ref, yff_ref,
    h1_out, h2_out, qkv_out, kv_out, o1_out, o1r_out, x1_out, q2_out, o2_out, o2r_out,
    gain_ref, win_ref, lse_ref, lse2_ref, mixed_ref, g2_ref, do_ref, xt3_ref, xtc_ref,
    h1_ref, h2_ref, qkv_ref, kv_ref, o1_ref, o1r_ref, x1_ref, q2_ref, o2_ref, o2r_ref,
    wa, pack, w_first, small, token_rows, send_kv, send_q2, keys, values_t, bias,
    cross_keys, cross_values_t, cross_out, seg,
    h3, y_stage, xs3, xsc, xr3, xrc, w_ff, send_do, out_acc, in_acc,
    own_sem, ff_sem, y_sem, store_sem, *sems,
):
    torus = Torus()
    me = lax.axis_index("hid")
    rows, mem_rows = tok_ref.shape[0], mem_ref.shape[0]
    tiles = qkv_ref.shape[0] // TILE
    barrier, count = greet(hid_peers() + torus_peers(torus) + [torus.beyond()])
    stores = []

    def store(*pairs_of_refs):
        for src, dst in pairs_of_refs:
            copy = pltpu.make_async_copy(src, dst, store_sem.at[len(stores)])
            copy.start()
            stores.append(copy)

    here = block_index(torus.pos, "") + (torus.core,)
    z, xlo = torus.pos["z"], lax.rem(me, 2)
    y, xhi = torus.pos["y"], torus.pos["x"] // 2
    token_rows[z, xlo] = tok_ref[...]
    norms = norm_ref[...].astype(FLOAT)
    blank = jnp.zeros_like(norms)
    first = jnp.concatenate([norms, blank], axis=1)
    second = jnp.concatenate([blank, norms], axis=1)
    lines = [jnp.where(torus.core == 0, first, second)]
    table = rel_ref[...].astype(FLOAT)
    for part in range(2):
        for head in range(2):
            value = table[part : part + 1, head : head + 1]
            lines.append(jnp.broadcast_to(value, (1, 128)))
    lines.append(jnp.zeros((9, 128), FLOAT))
    small[y, xhi, torus.core] = jnp.concatenate(lines, axis=0).astype(HALF)
    w_first[y, xhi, torus.core] = jnp.concatenate(
        [wq_ref[...], wk_ref[...], wv_ref[...]], axis=1
    )
    wa[here] = jnp.concatenate(
        [wo_ref[...], cq_ref[...], ck_ref[...], cv_ref[...], co_ref[...]], axis=1
    )
    blank = jnp.zeros((SHARD, FF_PAD - wg_ref.shape[1]), HALF)
    pack[...] = jnp.concatenate(
        [wg_ref[...], blank, wu_ref[...], blank, wd_ref[...], blank], axis=1
    )
    own = pltpu.make_async_copy(pack, wf_ref.at[here], own_sem.at[0])
    own.start()
    flow_b = Flow(torus, wa, GATHER_MIX, ORDERS, sems[0:4])
    flow_c = Flow(torus, wa, GATHER_LAST, ORDERS[2:], sems[28:32])
    flow_f = Flow(torus, wf_ref, GATHER_ONE, ORDERS, sems[4:8], pack)
    flow_g = Flow(torus, wf_ref, GATHER_TWO, TWO_ORDERS, sems[32:36], pack)
    row_sends, column_sends = Pairs(torus, sems[8:10]), Pairs(torus, sems[10:12])
    gather_rows = Rows(torus, token_rows, row_sends)
    columns = [Columns(torus, w_first, column_sends), Columns(torus, small, column_sends)]
    kv_trade = Trade(
        lambda j: send_kv.at[j], lambda j: kv_ref.at[rows_at(j, mem_rows)], sems[12:14]
    )
    o1_trade = Trade(
        lambda j: o1_ref.at[rows_at(j, rows)], lambda j: o1r_ref.at[j], sems[14:16]
    )
    q2_trade = Trade(
        lambda j: send_q2.at[j], lambda j: q2_ref.at[rows_at(j, rows)], sems[16:18]
    )
    o2_trade = Trade(
        lambda j: o2_ref.at[rows_at(j, rows)], lambda j: o2r_ref.at[j], sems[18:20]
    )
    do_trade = Trade(
        lambda j: send_do.at[j], lambda j: do_ref.at[rows_at(j, rows)], sems[20:22]
    )
    pairs = Pairs(torus, sems[22:24])
    flow_w = Flow(
        torus, wqkv_ref, QKV_CUTS, Y_LAST, sems[24:28], w_first.at[y, xhi, torus.core]
    )
    own_first = pltpu.make_async_copy(
        w_first.at[y, xhi, torus.core], wqkv_ref.at[here], own_sem.at[1]
    )
    own_first.start()
    build_segments(seg, len_ref, slot_ref, enc_ref, tiles)
    split_columns(torus, cot_ref[...].astype(FLOAT), xtc_ref, xsc)
    pl.semaphore_wait(barrier, count)
    flow_w.near(0)
    flow_b.near(0)
    flow_g.near(0)
    gather_rows.start()
    for column in columns:
        column.start()
    flow_f.near(0)
    flow_w.far(0)
    flow_b.far(0)
    flow_c.near(0)
    flow_g.far(0)
    for column in columns:
        column.near()
    gather_rows.near()
    for column in columns:
        column.far()
    own.wait()
    own_first.wait()
    flow_f.far(0)
    gather_rows.far(True)
    flow_b.done(0)
    flow_g.done(0)
    for column in columns:
        column.done()
    flow_b.near(1)
    flow_c.far(0)
    gather_rows.far(False)
    flow_f.done(0)
    for column in columns:
        column.arrived()
    gain_parts = []
    heads = [jnp.zeros((8, PAIR), FLOAT), jnp.zeros((8, PAIR), FLOAT)]
    buckets = bucket_windows(bucket_ref)
    for pair in range(8):
        blocks = [small[pair // 2, pair % 2, core].astype(FLOAT) for core in range(2)]
        gain_parts.append((blocks[0] + blocks[1])[0:8])
        for core in range(2):
            for part in range(2):
                bucket = (pair * 2 + core) * 2 + part
                for head in range(2):
                    at = 3 + part * 2 + head
                    value = blocks[core][at : at + 1]
                    value = jnp.concatenate([value] * 4, axis=1)
                    heads[head] = jnp.where(buckets == bucket, value, heads[head])
    gain_ref[...] = jnp.concatenate(gain_parts, axis=1)
    after = lax.broadcasted_iota(jnp.int32, (8, PAIR), 0) * PAIR + lax.broadcasted_iota(
        jnp.int32, (8, PAIR), 1
    )
    after = (after >= TILE) & (after < PAIR)
    win_ref[0:8] = jnp.where(after, NEG, heads[0])
    win_ref[8:16] = jnp.where(after, NEG, heads[1])
    build_bias(win_ref, bias, tiles)
    flow_f.near(1)
    flow_b.far(1)
    flow_c.done(0)
    flow_c.near(1)
    gather_rows.done(True)
    flow_f.far(1)
    flow_b.done(1)
    flow_b.near(2)
    flow_c.far(1)
    gather_rows.done(False)
    for j in range(8):
        block = token_rows[j // 2, j % 2].astype(FLOAT)
        h1 = (block * scale_of(block) * gain_ref[0:1, :]).astype(HALF)
        h1_ref[j] = h1
        qkv = dot(h1, w_first[...].reshape(16 * SHARD, 256))
        qkv_ref[j * rows : (j + 1) * rows, :] = qkv.astype(HALF)
    store((h1_ref, h1_out), (qkv_ref, qkv_out))
    flow_f.done(1)
    flow_f.near(2)
    flow_b.far(2)
    flow_c.done(1)
    flow_g.near(1)

    def weights(j, first, width):
        block = wa[j // 2, j % 2, :, :, :, :, first : first + width]
        return block.reshape(16 * SHARD, width)

    def spread_trade(trade, left_ref, first, send_ref, land_ref):
        width = send_ref.shape[-1]
        spread(left_ref, lambda j: weights(j, first, width), send_ref)
        trade.start_all()
        land_ref[rows_at(me, left_ref.shape[0]), :] = send_ref[me]

    for tile in range(tiles):
        block = qkv_ref[tile * TILE : (tile + 1) * TILE, 128:256]
        keys[tile] = block[:, :HDIM]
        values_t[tile] = block[:, HDIM:].astype(FLOAT).T.astype(HALF)
    ends = doc_ends(len_ref)

    def row_tile(tile):
        at = slice(tile * TILE, (tile + 1) * TILE)
        queries = stack_heads(qkv_ref[at, 0:128])
        row_start = start_of(lane_positions(tile * TILE), ends)
        first = max(0, tile - LONG // TILE)
        scores = []
        for other in range(first, tile + 1):
            tile_scores = dot_nt(keys[other], queries) + bias[tile - other]
            key_pos = other * TILE + lax.broadcasted_iota(jnp.int32, (TILE, 1), 0)
            scores.append(jnp.where(key_pos >= row_start, tile_scores, NEG))
        value, log_total = soft_sum(scores, lambda other: values_t[first + other])
        o1_ref[at, :] = unstack_heads(value).astype(HALF)
        lse_ref[tile : tile + 1, :] = log_total

    for tile in range(tiles):
        row_tile(tile)
        o1_trade.start_to(complete(tile + 1, rows, tile))
        if tile == 3:
            flow_w.done(0)
            flow_c.near(2)
    o1r_ref[me] = o1_ref[rows_at(me, rows), :]
    flow_w.near(1)
    flow_b.done(2)
    flow_g.far(1)
    flow_b.arrived()
    spread_trade(kv_trade, mem_ref, 256, send_kv, kv_ref)
    store((o1_ref, o1_out))
    flow_w.far(1)
    copies = [pairs.send(lambda: xsc, lambda: xrc)]
    o1_trade.arrived()
    flow_c.far(2)
    flow_g.done(1)
    total = tok_ref[...].astype(FLOAT)
    for pair in range(4):
        left = jnp.concatenate([o1r_ref[2 * pair], o1r_ref[2 * pair + 1]], axis=1)
        right = jnp.concatenate(
            [weights(2 * pair, 0, 128), weights(2 * pair + 1, 0, 128)], axis=1
        )
        total = total + dot_nt(left, right)
    x1_ref[...] = total
    h2_ref[...] = (total * scale_of(total) * gain_ref[1:2, :]).astype(HALF)
    spread_trade(q2_trade, h2_ref, 128, send_q2, q2_ref)
    store((o1r_ref, o1r_out), (x1_ref, x1_out), (h2_ref, h2_out))
    flow_g.near(2)
    q2_trade.arrived()
    flow_f.far(2)
    kv_trade.arrived()
    store((q2_ref, q2_out), (kv_ref, kv_out))
    flow_w.done(1)
    for tile in range(kv_ref.shape[0] // TILE):
        block = kv_ref[tile * TILE : (tile + 1) * TILE, :]
        cross_keys[tile] = block[:, :HDIM]
        cross_values_t[tile] = block[:, HDIM:].astype(FLOAT).T.astype(HALF)

    def segment(at):
        cross_segment(at, seg, q2_ref, cross_keys, cross_values_t, cross_out, lse2_ref)

    done = 0
    for first, last in ((0, 2), (2, 4), (4, 6), (6, SEGMENTS)):
        pl.loop(first, last)(segment)
        join_segments(seg, cross_out, o2_ref, range(done, last - 2))
        o2_trade.start_to(complete(last - 2, rows, done))
        done = last - 2
        if last == 4:
            flow_c.done(2)
            flow_g.far(2)
        if last == 6:
            flow_w.near(2)
    flow_f.done(2)
    flow_g.done(2)
    o2r_ref[me] = o2_ref[rows_at(me, rows), :]
    flow_c.arrived()
    keep = pltpu.make_async_copy(wa, wa_ref, own_sem.at[0])
    keep.start()
    flow_f.arrived()
    flow_g.arrived()

    def fetch(j):
        slot = lax.rem(j, 2)
        return pltpu.make_async_copy(
            wf_ref.at[j // 2, lax.rem(j, 2)], w_ff.at[slot], ff_sem.at[slot]
        )

    fetch(0).start()
    o2_trade.arrived()
    store((o2_ref, o2_out), (o2r_ref, o2r_out))
    x_two = x1_ref[...]
    for pair in range(4):
        left = jnp.concatenate([o2r_ref[2 * pair], o2r_ref[2 * pair + 1]], axis=1)
        right = jnp.concatenate(
            [weights(2 * pair, 384, 128), weights(2 * pair + 1, 384, 128)], axis=1
        )
        x_two = x_two + dot_nt(left, right)
    out_acc[...] = x_two
    g2_ref[...] = x_two
    in_acc[...] = jnp.zeros_like(in_acc)
    h3[...] = (x_two * scale_of(x_two) * gain_ref[2:3, :]).astype(HALF)
    split_columns(torus, h3[...].astype(FLOAT), xt3_ref, xs3)
    copies.append(pairs.send(lambda: xs3, lambda: xr3))

    def stash(j):
        return pltpu.make_async_copy(
            y_stage.at[j], yff_ref.at[j, pl.ds(0, rows)], y_sem.at[0, j]
        )

    def share(j):
        return pltpu.make_async_remote_copy(
            src_ref=y_stage.at[j], dst_ref=yff_ref.at[j, pl.ds(rows, rows)],
            send_sem=y_sem.at[1, j], recv_sem=y_sem.at[2, j],
            device_id=torus.sibling(), device_id_type=MESH,
        )

    def ff_weight(slot, first, width):
        return w_ff[slot, :, :, :, :, first : first + width].reshape(16 * SHARD, width)

    def one_block(j):
        @pl.when(j < 7)
        def _():
            fetch(j + 1).start()

        fetch(j).wait()
        slot = lax.rem(j, 2)
        gate_up = dot(h3[...], ff_weight(slot, 0, 2 * FF_PAD))
        gate, up = gate_up[:, :FF_PAD], gate_up[:, FF_PAD:]
        d_hidden = dot(cot_ref[...], ff_weight(slot, 2 * FF_PAD, FF_PAD))
        curve = 0.7978845608028654 * (gate + 0.044715 * gate * gate * gate)
        bend = jnp.tanh(curve)
        gelu = 0.5 * gate * (1.0 + bend)
        slope = 0.5 * (1.0 + bend) + 0.5 * gate * (1.0 - bend * bend) * (
            0.7978845608028654 * (1.0 + 3.0 * 0.044715 * gate * gate)
        )
        hidden = (gelu * up).astype(HALF)
        y_stage[j, :, 2 * FF_PAD :] = hidden
        d_both = jnp.concatenate([d_hidden * up * slope, d_hidden * gelu], axis=1).astype(HALF)
        y_stage[j, :, 0 : 2 * FF_PAD] = d_both
        stash(j).start()
        share(j).start()
        out_acc[...] += dot_nt(hidden, ff_weight(slot, 2 * FF_PAD, FF_PAD))
        in_acc[...] += dot_nt(d_both, ff_weight(slot, 0, 2 * FF_PAD))

    pl.loop(0, 6, unroll=2)(one_block)
    flow_w.far(2)
    pl.loop(6, 8, unroll=2)(one_block)
    mixed_ref[...] = out_acc[...].astype(HALF)
    d_inner = norm_backward(g2_ref[...], gain_ref[2:3, :], in_acc[...])
    g_two = cot_ref[...].astype(FLOAT) + d_inner
    g2_ref[...] = g_two
    h3[...] = g_two.astype(HALF)
    spread(h3, lambda j: weights(j, 384, 128), send_do)
    do_trade.start_all()
    do_ref[rows_at(me, rows), :] = send_do[me]
    flow_w.done(2)
    for copy in copies:
        copy.wait_recv()
    join_columns(xtc_ref, xrc)
    join_columns(xt3_ref, xr3)
    do_trade.arrived()
    flow_w.arrived()
    for trade in (kv_trade, o1_trade, q2_trade, o2_trade, do_trade):
        trade.finish()
    for flow in (flow_b, flow_c, flow_f, flow_g, flow_w, row_sends, column_sends, pairs):
        flow.finish()
    keep.wait()
    for copy in stores:
        copy.wait()

    @pl.loop(0, 8)
    def settle(j):
        stash(j).wait()
        share(j).wait()


def forward(vectors, scalars):
    tokens, memory = vectors[13:15]
    rows, mem_rows = tokens.shape[0], memory.shape[0]
    group, keys = rows * 8, mem_rows * 8
    tiles, key_tiles = group // TILE, keys // TILE
    vmem = pl.BlockSpec(memory_space=pltpu.VMEM)
    smem = pl.BlockSpec(memory_space=pltpu.SMEM)
    anywhere = pl.BlockSpec(memory_space=pl.ANY)
    shape = jax.ShapeDtypeStruct
    places = (4, 2, 4, 2, 2)
    turned = (4, 2, SHARD, rows)
    big = (
        shape((8, rows, 1024), HALF),
        shape((rows, 1024), HALF),
        shape((group, 256), HALF),
        shape((keys, 128), HALF),
        shape((group, 128), HALF),
        shape((8, rows, 128), HALF),
        shape((rows, 1024), FLOAT),
        shape((group, 128), HALF),
        shape((group, 128), HALF),
        shape((8, rows, 128), HALF),
    )
    return pl.pallas_call(
        forward_kernel,
        out_shape=(
            shape(places + (SHARD, 1152), HALF),
            shape(places + (SHARD, 512), HALF),
            shape(places + (SHARD, 256), HALF),
            shape((8, 2 * rows, 3 * FF_PAD), HALF),
        )
        + big
        + (
            shape((8, 1024), FLOAT),
            shape((16, PAIR), FLOAT),
            shape((8, PAIR), FLOAT),
            shape((8, PAIR), FLOAT),
            shape((rows, 1024), HALF),
            shape((rows, 1024), FLOAT),
            shape((group, 128), HALF),
            shape((4, 2, SHARD, 2 * rows), HALF),
            shape((4, 2, SHARD, 2 * rows), HALF),
        ),
        in_specs=[vmem] * 17 + [smem] * 3,
        out_specs=(anywhere,) * 14 + (vmem,) * 9,
        scratch_shapes=[pltpu.VMEM(one.shape, one.dtype) for one in big]
        + [
            pltpu.VMEM(places + (SHARD, 512), HALF),
            pltpu.VMEM((SHARD, 1152), HALF),
            pltpu.VMEM((4, 2, 2, SHARD, 256), HALF),
            pltpu.VMEM((4, 2, 2, 16, 128), HALF),
            pltpu.VMEM((4, 2, rows, 1024), HALF),
            pltpu.VMEM((8, mem_rows, 128), HALF),
            pltpu.VMEM((8, rows, 128), HALF),
            pltpu.VMEM((tiles, TILE, HDIM), HALF),
            pltpu.VMEM((tiles, HDIM, TILE), HALF),
            pltpu.VMEM((tiles, TILE, PAIR), FLOAT),
            pltpu.VMEM((key_tiles, TILE, HDIM), HALF),
            pltpu.VMEM((key_tiles, HDIM, TILE), HALF),
            pltpu.VMEM((SEGMENTS, HDIM, PAIR), FLOAT),
            pltpu.SMEM((SEGMENTS, 8), jnp.int32),
            pltpu.VMEM((rows, 1024), HALF),
            pltpu.VMEM((8, rows, 3 * FF_PAD), HALF),
        ]
        + [pltpu.VMEM(turned, HALF)] * 4
        + [
            pltpu.VMEM((2, 4, 2, 2, SHARD, 1152), HALF),
            pltpu.VMEM((8, rows, 128), HALF),
            pltpu.VMEM((rows, 1024), FLOAT),
            pltpu.VMEM((rows, 1024), FLOAT),
            pltpu.SemaphoreType.DMA((2,)),
            pltpu.SemaphoreType.DMA((2,)),
            pltpu.SemaphoreType.DMA((3, 8)),
            pltpu.SemaphoreType.DMA((10,)),
        ]
        + flow_sems(3, 2) + flow_sems(3, 2)
        + [pltpu.SemaphoreType.DMA((13,))] * 2 + [pltpu.SemaphoreType.DMA((20,))] * 2
        + trade_sems() * 5
        + [pltpu.SemaphoreType.DMA((2,))] * 2 + flow_sems(2, 2)
        + flow_sems(1, 2) + flow_sems(3, 2),
        compiler_params=pltpu.CompilerParams(
            collective_id=0, has_side_effects=True, vmem_limit_bytes=62 * 2**20
        ),
    )(*vectors, *scalars)


class Drain:
    def __init__(self, torus, acc, out_ref, cuts, orders, halves, buffers, sems):
        self.torus, self.acc, self.out_ref = torus, acc, out_ref
        self.cuts, self.orders, self.halves = cuts, orders, halves
        self.buffers, self.sems = buffers, sems
        self.rows = (0, acc.shape[4])
        self.sends, self.last = [], {}

    def plan(self, stage):
        for part, cut in enumerate(self.cuts):
            first = (stage * len(self.cuts) + part) * 2
            got, final = self.buffers[first : first + 2]
            yield part, cut, self.orders[part][stage], self.orders[part][:stage], got, final

    def view(self, place, whole, rows, cut):
        return self.acc.at[block_index(place, whole) + (pl.ds(*rows), pl.ds(*cut))]

    def send(self, axis, hops, step, whole, rows, cut, buffer, slot):
        copy = Remote(
            lambda: self.view(self.torus.moved(axis, hops), whole, rows, cut),
            lambda: buffer.at[slot],
            self.sems, len(self.sends),
            lambda: self.torus.neighbour(axis, step),
        )
        copy.start()
        self.sends.append(copy)
        return copy

    def add(self, place, whole, rows, cut, sources):
        dims = whole_dims(whole)
        count = 1
        for dim in dims:
            count *= dim

        def one(step):
            index, rest_of = [], step
            for dim in reversed(dims):
                index.append(lax.rem(rest_of, dim))
                rest_of = rest_of // dim
            index = index[::-1]
            left = iter(index)
            at = tuple(
                next(left) if isinstance(entry, slice) else entry
                for entry in block_index(place, whole)
            )
            where = at + (pl.ds(*rows), pl.ds(*cut))
            total = self.acc[where].astype(FLOAT)
            for buffer, slot in sources:
                total = total + buffer[(slot,) + tuple(index)].astype(FLOAT)
            self.acc[where] = total.astype(self.acc.dtype)

        if count == 1:
            one(jnp.int32(0))
        else:
            pl.loop(0, count)(one)

    def begin(self, stage):
        for part, cut, axis, whole, got, _ in self.plan(stage):
            self.last[part] = [
                self.send(axis, 2, 1 - 2 * slot, whole, rows, cut, got, slot)
                for slot, rows in enumerate(self.halves)
            ]

    def turn(self, stage):
        torus = self.torus
        for part, cut, axis, whole, got, final in self.plan(stage):
            copies = []
            for slot, step in enumerate((1, -1)):
                place = torus.moved(axis, step)
                if slot < len(self.halves):
                    self.last[part][slot].wait_recv()
                    self.add(place, whole, self.halves[slot], cut, [(got, slot)])
                copies.append(self.send(axis, step, step, whole, self.rows, cut, final, slot))
            self.last[part] = copies

    def settle(self, stage):
        for part, cut, axis, whole, _, final in self.plan(stage):
            for copy in self.last[part]:
                copy.wait_recv()
            if stage > 0:
                self.add(self.torus.pos, whole, self.rows, cut, [(final, 0), (final, 1)])
            else:
                mine = self.acc[block_index(self.torus.pos, "") + (slice(None), pl.ds(*cut))]
                self.out_ref[:, pl.ds(*cut)] = (
                    mine.astype(FLOAT) + final[0].astype(FLOAT) + final[1].astype(FLOAT)
                )

    def finish(self):
        for copy in self.sends:
            copy.wait_send()


def drain_scratch(cuts, orders, halves, rows, dtype):
    width = sum(cut[1] for cut in cuts)
    scratch = [pltpu.VMEM((4, 2, 4, 2, rows, width), dtype)]
    for stage in range(3):
        for part, cut in enumerate(cuts):
            dims = whole_dims(orders[part][:stage])
            scratch.append(pltpu.VMEM((len(halves),) + dims + (halves[0][1], cut[1]), dtype))
            scratch.append(pltpu.VMEM((2,) + dims + (rows, cut[1]), dtype))
    count = len(cuts) * 3 * (2 + len(halves))
    return scratch + [pltpu.SemaphoreType.DMA((count,))] * 2


def split_columns(torus, value, mine_ref, other_ref):
    size = value.shape[0]
    turned = value.T.astype(HALF).reshape(4, 2, 2, SHARD, size)
    first = torus.core == 0
    mine_ref[:, :, :, 0:size] = jnp.where(first, turned[:, :, 0], turned[:, :, 1])
    other_ref[...] = jnp.where(first, turned[:, :, 1], turned[:, :, 0])


def join_columns(turned, arrived):
    size = arrived.shape[-1]
    turned[...] = jnp.concatenate([turned[:, :, :, 0:size], arrived[...]], axis=-1)


def fill_product(acc, first, width, turned, right, unroll):
    @pl.loop(0, 8, unroll=unroll)
    def one_j(j):
        left = turned[...].reshape(8 * SHARD, turned.shape[-1])
        value = dot(left, right(j)).astype(HALF)
        acc[j // 2, lax.rem(j, 2), :, :, :, first : first + width] = value.reshape(
            4, 2, SHARD, width
        )


def spread(left_ref, weights, send_ref):
    width = send_ref.shape[-1]
    group = max(1, 256 // width)
    for first in range(0, 8, group):
        right = [weights(first + at) for at in range(group)]
        right = right[0] if group == 1 else jnp.concatenate(right, axis=1)
        value = dot(left_ref[...], right).astype(HALF)
        for at in range(group):
            send_ref[first + at] = value[:, at * width : (at + 1) * width]


def backward_kernel(
    lse2_ref, g2_ref, mem_ref, h2_ref, gain_ref, xt3_ref, xtc_ref, win_ref, lse_ref, bucket_ref,
    wq_ref, wk_ref, wv_ref, cq_ref, wg_ref, wu_ref,
    norm_ref, len_ref, slot_ref, enc_ref,
    q2_in, kv2_in, do2_in, o2_in, x1_in, tok_in, qkv_in, o1_in, h1_ref, o1r_ref, o2r_ref, wa_ref, wqkv_ref, yff_ref,
    dtok_ref, gu_out, down_out, mix_out, early_out, qkv_out, last_out, dnorm_ref, dmem_ref,
    *rest,
):
    rest = list(rest)

    def take(count):
        taken = rest[:count]
        del rest[:count]
        return taken

    q2_ref, kv2_ref, do2_ref, o2_ref, x1_ref, tok_ref, qkv_ref, o1_ref = take(8)
    y_o1, y_o2, y_q2, y_kv2, y_qkv, h1_turned = take(6)
    xt_h2, xt_mem, xt_g1, xt_g2 = take(4)
    xs_h2, xs_mem, xs_g1, xs_g2 = take(4)
    xr_h2, xr_mem, xr_g1, xr_g2 = take(4)
    g1_half, send_do, do_ref, dqkv_ref, dq2_ref, dkv2_ref, seg = take(7)
    t_acc, t_send, t_recv, tx_send, tx_recv, ty_send, ty_recv = take(7)
    s_all, s_acc, s_recv, sx_send, sx_recv, sy_send, sy_recv = take(7)
    n_send, n_recv = take(2)
    gu_scratch, down_scratch, mix_scratch, early_scratch = take(19), take(19), take(13), take(7)
    local_sem = rest.pop(0)
    sems = rest
    gu_sems, down_sems, mix_sems, early_sems = sems[0:2], sems[2:4], sems[4:6], sems[6:8]
    pair_sems, trade_sem = sems[8:10], sems[10:20]

    torus = Torus()
    me = lax.axis_index("hid")
    y, xhi = torus.pos["y"], torus.pos["x"] // 2
    rows, mem_rows = tok_ref.shape[0], mem_ref.shape[0]
    tiles = qkv_ref.shape[0] // TILE
    barrier, count = greet(
        hid_peers() + torus_peers(torus) + [torus.beyond(), torus.neighbour("y", 2)]
    )
    owns = [
        pltpu.make_async_copy(o1r_ref, y_o1.at[:, pl.ds(0, rows)], local_sem.at[0]),
        pltpu.make_async_copy(o2r_ref, y_o2.at[:, pl.ds(0, rows)], local_sem.at[1]),
    ]
    for own in owns:
        own.start()
    sources = (q2_in, kv2_in, do2_in, o2_in, x1_in, tok_in, qkv_in, o1_in)
    targets = (q2_ref, kv2_ref, do2_ref, o2_ref, x1_ref, tok_ref, qkv_ref, o1_ref)
    late = [
        pltpu.make_async_copy(src, dst, local_sem.at[4 + at])
        for at, (src, dst) in enumerate(zip(sources, targets))
    ]
    for copy in late:
        copy.start()
    dq2_trade = Trade(
        lambda j: dq2_ref.at[rows_at(j, rows)], lambda j: y_q2.at[j, pl.ds(0, rows)],
        trade_sem[0:2],
    )
    dkv2_trade = Trade(
        lambda j: dkv2_ref.at[rows_at(j, mem_rows)], lambda j: y_kv2.at[j, pl.ds(0, mem_rows)],
        trade_sem[2:4],
    )
    do_trade = Trade(
        lambda j: send_do.at[j], lambda j: do_ref.at[rows_at(j, rows)], trade_sem[4:6]
    )
    dqkv_trade = Trade(
        lambda j: dqkv_ref.at[rows_at(j, rows)], lambda j: y_qkv.at[j], trade_sem[6:8]
    )
    norm_trade = Trade(lambda j: n_send, lambda j: n_recv.at[j], trade_sem[8:10])
    pairs = Pairs(torus, pair_sems)

    def share(buffer, size):
        return pairs.send(
            lambda: buffer.at[:, pl.ds(0, size)], lambda: buffer.at[:, pl.ds(size, size)]
        )

    drain_gu = Drain(
        torus, gu_scratch[0], gu_out, GATE_UP_CUTS, ORDERS, HALVES, gu_scratch[1:], gu_sems
    )
    drain_down = Drain(
        torus, down_scratch[0], down_out, DOWN_CUTS, ORDERS, HALVES, down_scratch[1:], down_sems
    )
    drain_mix = Drain(
        torus, mix_scratch[0], mix_out, MIX_CUTS, ORDERS, HALVES, mix_scratch[1:], mix_sems,
    )
    drain_early = Drain(
        torus, early_scratch[0], early_out, EARLY_CUTS, (ORDERS[2],), HALVES, early_scratch[1:],
        early_sems,
    )

    build_segments(seg, len_ref, slot_ref, enc_ref, tiles)

    def load_ff(yff):
        load = pltpu.make_async_copy(yff_ref, yff, local_sem.at[2])
        load.start()
        split_columns(torus, g2_ref[...], xt_g2, xs_g2)
        split_columns(torus, h2_ref[...].astype(FLOAT), xt_h2, xs_h2)
        split_columns(torus, mem_ref[...].astype(FLOAT), xt_mem, xs_mem)
        load.wait()
        fill_product(gu_scratch[0], 0, 768, xt3_ref, lambda j: yff[j, :, 0:768], 4)
        fill_product(down_scratch[0], 0, 384, xtc_ref, lambda j: yff[j, :, 768:1152], 4)

    pl.run_scoped(load_ff, pltpu.VMEM((8, 2 * rows, 1152), HALF))

    pl.semaphore_wait(barrier, count)
    drain_gu.begin(2)
    drain_down.begin(2)
    pair_g2 = pairs.send(lambda: xs_g2, lambda: xr_g2)
    pair_h2 = pairs.send(lambda: xs_h2, lambda: xr_h2)
    pair_mem = pairs.send(lambda: xs_mem, lambda: xr_mem)
    for own in owns + late:
        own.wait()
    pair_y = [share(y, size) for y, size in ((y_o1, rows), (y_o2, rows))]

    def cross_attention(keys, values, keys_t, queries, grads, deltas, dq, dkv):
        for tile in range(kv2_ref.shape[0] // TILE):
            block = kv2_ref[tile * TILE : (tile + 1) * TILE, :]
            keys[tile] = block[:, :HDIM]
            values[tile] = block[:, HDIM:]
            keys_t[tile] = block[:, :HDIM].astype(FLOAT).T.astype(HALF)
        row_prepare(tiles, lambda at: q2_ref[at, :], do2_ref, o2_ref, queries, grads, deltas)
        dkv[...] = jnp.zeros_like(dkv)

        def segment(at):
            tile, slot, valid = seg[at, 2], seg[at, 3], seg[at, 4]
            query = of_tile(at, tile, tiles, lambda place: queries[place])
            grad = of_tile(at, tile, tiles, lambda place: grads[place])
            delta = of_tile(at, tile, tiles, lambda place: deltas[place])

            def whole(ref, axis):
                parts = [of_slot(slot, other, lambda place: ref[place]) for other in range(4)]
                return jnp.concatenate(parts, axis=axis)

            scores = masked_keys(dot_nt(whole(keys, 0), query), 0, valid)
            weights = jnp.exp(scores - lse2_ref[pl.ds(at, 1), :])
            d_weights = dot_nt(whole(values, 0), grad)
            d_half = (weights * (d_weights - delta)).astype(HALF)
            dq[at] = dot(whole(keys_t, 1), d_half)
            both = jnp.concatenate(
                [dot(d_half, query), dot(weights.astype(HALF), grad)], axis=1
            )
            for memory in range(3):
                dkv[memory] += jnp.where(slot == memory, both, 0.0)

        done = 0
        for first, last in ((0, 2), (2, 4), (4, 6), (6, SEGMENTS)):
            pl.loop(first, last)(segment)
            for tile in range(done, last - 2):
                total = jnp.zeros((HDIM, PAIR), FLOAT)
                for at in range(tile, tile + 3):
                    total = total + jnp.where(seg[at, 2] == tile, dq[at], 0.0)
                dq2_ref[tile * TILE : (tile + 1) * TILE, :] = unstack_heads(total).astype(HALF)
            dq2_trade.start_to(complete(last - 2, rows, done))
            done = last - 2
            if last == 4:
                drain_gu.turn(2)
        for memory in range(3):
            dkv2_ref[memory * ENC : (memory + 1) * ENC, :] = dkv[memory].astype(HALF)
        drain_gu.settle(2)
        dkv2_trade.start_all()
        y_q2[me, 0:rows] = dq2_ref[rows_at(me, rows), :]
        y_kv2[me, 0:mem_rows] = dkv2_ref[rows_at(me, mem_rows), :]

    key_tiles = kv2_ref.shape[0] // TILE
    pl.run_scoped(
        cross_attention,
        pltpu.VMEM((key_tiles, TILE, HDIM), HALF),
        pltpu.VMEM((key_tiles, TILE, HDIM), HALF),
        pltpu.VMEM((key_tiles, HDIM, TILE), HALF),
        pltpu.VMEM((tiles, PAIR, HDIM), HALF),
        pltpu.VMEM((tiles, PAIR, HDIM), HALF),
        pltpu.VMEM((tiles, 1, PAIR), FLOAT),
        pltpu.VMEM((SEGMENTS, HDIM, PAIR), FLOAT),
        pltpu.VMEM((3, ENC, 2 * HDIM), FLOAT),
    )

    def inner(w_in, w_out, dmem, h1):
        loads = [
            pltpu.make_async_copy(wa_ref.at[:, :, pl.ds(128, 256)], w_in, local_sem.at[2]),
            pltpu.make_async_copy(wa_ref.at[:, :, pl.ds(0, 128)], w_out, local_sem.at[3]),
        ]
        load_h1 = pltpu.make_async_copy(h1_ref, h1, local_sem.at[0])
        for load in loads + [load_h1]:
            load.start()
        load_h1.wait()
        for pair in range(4):
            block = h1[2 * pair : 2 * pair + 2].reshape(2 * rows, 1024)
            h1_turned[:, 2 * rows * pair : 2 * rows * (pair + 1)] = (
                block.astype(FLOAT).T.astype(HALF)
            )
        for load in loads:
            load.wait()
        dq2_trade.arrived()
        pair_q2 = share(y_q2, rows)
        total = jnp.zeros((rows, 1024), FLOAT)
        for pair in range(4):
            left = [y_q2[2 * pair + side, 0:rows] for side in range(2)]
            right = [w_in[2 * pair + side, :, 0:128] for side in range(2)]
            total = total + dot_nt(
                jnp.concatenate(left, axis=1), jnp.concatenate(right, axis=1)
            )
        d_inner = norm_backward(x1_ref[...], gain_ref[1:2, :], total)
        g_one = g2_ref[...] + d_inner
        dtok_ref[...] = g_one
        g1_half[...] = g_one.astype(HALF)

        spread(g1_half, lambda j: w_out[j], send_do)
        do_trade.start_all()
        do_ref[rows_at(me, rows), :] = send_do[me]
        drain_gu.begin(1)
        drain_down.turn(2)
        split_columns(torus, dtok_ref[...], xt_g1, xs_g1)
        pair_g1 = pairs.send(lambda: xs_g1, lambda: xr_g1)
        dkv2_trade.arrived()
        pair_kv2 = share(y_kv2, mem_rows)
        for pair in range(4):
            left = [y_kv2[2 * pair + side, 0:mem_rows] for side in range(2)]
            right = [w_in[2 * pair + side, :, 128:256] for side in range(2)]
            value = dot_nt(jnp.concatenate(left, axis=1), jnp.concatenate(right, axis=1))
            dmem[...] = value if pair == 0 else dmem[...] + value
        store = pltpu.make_async_copy(dmem, dmem_ref, local_sem.at[2])
        store.start()
        for copy in [pair_g2, pair_mem, pair_kv2, pair_y[1]]:
            copy.wait_recv()
        join_columns(xt_mem, xr_mem)
        join_columns(xt_g2, xr_g2)
        fill_product(early_scratch[0], 0, 128, xt_mem, lambda j: y_kv2[j], 4)
        fill_product(early_scratch[0], 128, 128, xt_g2, lambda j: y_o2[j], 8)
        drain_early.begin(2)
        for copy in [pair_h2, pair_q2, pair_g1, pair_y[0]]:
            copy.wait_recv()
        join_columns(xt_g1, xr_g1)
        join_columns(xt_h2, xr_h2)
        fill_product(mix_scratch[0], 128, 128, xt_h2, lambda j: y_q2[j], 8)
        fill_product(mix_scratch[0], 0, 128, xt_g1, lambda j: y_o1[j], 8)
        drain_mix.begin(2)
        store.wait()

    pl.run_scoped(
        inner,
        pltpu.VMEM((8, 1024, 256), HALF),
        pltpu.VMEM((8, 1024, 128), HALF),
        pltpu.VMEM((mem_rows, 1024), FLOAT),
        pltpu.VMEM((8, rows, 1024), HALF),
    )

    core_copies = []

    def self_attention(keys, values, keys_t, queries, grads, deltas, bias, bias_grad, dq):
        build_bias(win_ref, bias, tiles)
        for tile in range(tiles):
            block = qkv_ref[tile * TILE : (tile + 1) * TILE, 128:256]
            keys[tile] = block[:, :HDIM]
            values[tile] = block[:, HDIM:]
            keys_t[tile] = block[:, :HDIM].astype(FLOAT).T.astype(HALF)
        bias_grad[...] = jnp.zeros_like(bias_grad)
        dq[...] = jnp.zeros_like(dq)
        ends = doc_ends(len_ref)
        drain_gu.turn(1)
        do_trade.arrived()
        row_prepare(
            tiles, lambda at: qkv_ref[at, 0:128], do_ref, o1_ref, queries, grads, deltas
        )

        def key_tile(other):
            key_pos = other * TILE + lax.broadcasted_iota(jnp.int32, (TILE, 1), 0)
            dk, dv = jnp.zeros((TILE, HDIM), FLOAT), jnp.zeros((TILE, HDIM), FLOAT)
            for tile in range(other, min(tiles, other + LONG // TILE + 1)):
                row_start = start_of(lane_positions(tile * TILE), ends)
                scores = dot_nt(keys[other], queries[tile]) + bias[tile - other]
                scores = jnp.where(key_pos >= row_start, scores, NEG)
                weights = jnp.exp(scores - lse_ref[tile : tile + 1, :])
                d_weights = dot_nt(values[other], grads[tile])
                d_scores = weights * (d_weights - deltas[tile])
                bias_grad[tile - other] += d_scores
                d_half = d_scores.astype(HALF)
                dv = dv + dot(weights.astype(HALF), grads[tile])
                dk = dk + dot(d_half, queries[tile])
                dq[tile] += dot(keys_t[other], d_half)
            at = slice(other * TILE, (other + 1) * TILE)
            dqkv_ref[at, 128:256] = jnp.concatenate([dk, dv], axis=1).astype(HALF)

        for other in range(tiles):
            key_tile(other)
            at = slice(other * TILE, (other + 1) * TILE)
            dqkv_ref[at, 0:128] = unstack_heads(dq[other]).astype(HALF)
            dqkv_trade.start_to(complete(other + 1, rows, other))
            if other == 1:
                drain_mix.turn(2)
                drain_early.turn(2)
        y_qkv[me] = dqkv_ref[rows_at(me, rows), :]
        drain_gu.settle(1)
        drain_down.settle(2)
        drain_down.begin(1)
        drain_mix.settle(2)
        value = dot(h1_turned[...], dqkv_ref[...]).reshape(4, 2, 2, SHARD, 256)
        first = torus.core == 0
        t_acc[...] = jnp.where(first, value[:, :, 0], value[:, :, 1])
        t_send[...] = jnp.where(first, value[:, :, 1], value[:, :, 0]).astype(HALF)
        core_copies.append(pairs.send(lambda: t_send, lambda: t_recv))
        drain_mix.begin(1)
        sums = []
        reach = min(tiles, LONG // TILE + 1)
        for head in range(2):
            parts = []
            for tile in range(reach):
                part = bias_grad[tile, :, head * TILE : (head + 1) * TILE]
                part = jnp.concatenate([part, jnp.zeros_like(part)], axis=1)
                parts.append(fold_diagonals(part))
            parts.append(jnp.zeros((8 - reach, PAIR), FLOAT))
            sums.append(jnp.concatenate(parts, axis=0))
        buckets = bucket_windows(bucket_ref)
        s_all[...] = jnp.zeros_like(s_all)
        for bucket in range(32):
            mask = buckets == bucket
            shard, part = bucket // 2, bucket % 2
            for head in range(2):
                picked = jnp.where(mask, sums[head], 0.0)
                value = jnp.sum(jnp.sum(picked, axis=0, keepdims=True), axis=1, keepdims=True)
                at = 3 + part * 2 + head
                place = (shard % 2, shard // 4, shard // 2 % 2)
                s_all[place + (slice(at, at + 1), slice(None))] = jnp.broadcast_to(
                    value, (1, 128)
                )
        core_copies.append(pairs.send(lambda: s_all.at[1 - torus.core], lambda: s_recv))
        drain_early.settle(2)
        drain_early.begin(1)

    pl.run_scoped(
        self_attention,
        pltpu.VMEM((tiles, TILE, HDIM), HALF),
        pltpu.VMEM((tiles, TILE, HDIM), HALF),
        pltpu.VMEM((tiles, HDIM, TILE), HALF),
        pltpu.VMEM((tiles, PAIR, HDIM), HALF),
        pltpu.VMEM((tiles, PAIR, HDIM), HALF),
        pltpu.VMEM((tiles, 1, PAIR), FLOAT),
        pltpu.VMEM((tiles, TILE, PAIR), FLOAT),
        pltpu.VMEM((tiles, TILE, PAIR), FLOAT),
        pltpu.VMEM((tiles, HDIM, PAIR), FLOAT),
    )

    x_copies = []

    def first_inputs(w_in):
        load = pltpu.make_async_copy(wqkv_ref, w_in, local_sem.at[2])
        load.start()
        core_copies[0].wait_recv()
        t_acc[...] += t_recv[...].astype(FLOAT)
        tx_send[...] = t_acc[:, 1 - xhi].astype(HALF)
        x_copies.append(pairs.send(lambda: tx_send, lambda: tx_recv, torus.beyond))
        core_copies[1].wait_recv()
        s_acc[...] = s_all[torus.core] + s_recv[...]
        sx_send[...] = s_acc[:, 1 - xhi]
        x_copies.append(pairs.send(lambda: sx_send, lambda: sx_recv, torus.beyond))
        drain_gu.begin(0)
        drain_down.turn(1)
        drain_mix.turn(1)
        drain_early.turn(1)
        load.wait()
        dqkv_trade.arrived()
        total = jnp.zeros((rows, 1024), FLOAT)
        for j in range(8):
            total = total + dot_nt(y_qkv[j], w_in[j])
        residual = tok_ref[...].astype(FLOAT)
        dtok_ref[...] += norm_backward(residual, gain_ref[0:1, :], total)
        drain_gu.turn(0)
        drain_down.settle(1)
        drain_down.begin(0)
        drain_mix.settle(1)
        drain_mix.begin(0)
        drain_early.settle(1)
        drain_early.begin(0)

    pl.run_scoped(first_inputs, pltpu.VMEM((8, 1024, 256), HALF))
    for copy in x_copies:
        copy.wait_recv()
    t_acc[:, xhi] += tx_recv[...].astype(FLOAT)
    s_acc[:, xhi] += sx_recv[...]
    y_copies = []
    for at, step in enumerate((1, -1, 2)):
        place = torus.moved("y", step)["y"]
        ty_send[at] = t_acc[place, xhi].astype(HALF)
        sy_send[at] = s_acc[place, xhi]
        for src, dst in ((ty_send, ty_recv), (sy_send, sy_recv)):
            y_copies.append(
                pairs.send(
                    functools.partial(src.at.__getitem__, at),
                    functools.partial(dst.at.__getitem__, at),
                    functools.partial(torus.neighbour, "y", step),
                )
            )
    drain_gu.settle(0)
    drain_down.turn(0)
    drain_mix.turn(0)
    drain_early.turn(0)
    for copy in y_copies:
        copy.wait_recv()
    total, last = t_acc[y, xhi], s_acc[y, xhi]
    for at in range(3):
        total = total + ty_recv[at].astype(FLOAT)
        last = last + sy_recv[at]
    qkv_out[...] = total
    last_out[...] = last
    drain_down.settle(0)
    drain_mix.settle(0)
    drain_early.settle(0)

    def dotted(value, weight):
        return jnp.sum(value * weight.astype(FLOAT), axis=1, keepdims=True)

    width = wg_ref.shape[1]
    sums = [
        dotted(qkv_out[:, 0:128], wq_ref[...])
        + dotted(qkv_out[:, 128:192], wk_ref[...])
        + dotted(qkv_out[:, 192:256], wv_ref[...]),
        dotted(mix_out[:, 128:256], cq_ref[...]),
        dotted(gu_out[:, 0:width], wg_ref[...])
        + dotted(gu_out[:, FF_PAD : FF_PAD + width], wu_ref[...]),
    ]
    lane = lax.broadcasted_iota(jnp.int32, (SHARD, 128), 1)
    block = jnp.zeros((SHARD, 128), FLOAT)
    for at, value in enumerate(sums):
        block = jnp.where(lane == at, value, block)
    n_send[...] = block.T[0:8]
    norm_trade.start_all()
    n_recv[me] = n_send[...]
    norm_trade.arrived()
    value = n_recv[0]
    for j in range(1, 8):
        value = value + n_recv[j]
    dnorm_ref[...] = value
    dnorm_ref[0:3, :] = value[0:3] / norm_ref[...].astype(FLOAT)
    for drain in (drain_gu, drain_down, drain_mix, drain_early):
        drain.finish()
    for trade in (dq2_trade, dkv2_trade, do_trade, dqkv_trade, norm_trade):
        trade.finish()
    pairs.finish()


def backward(vectors, scalars, arrays):
    memory, tokens = vectors[2], arrays[5]
    rows, mem_rows = tokens.shape[0], memory.shape[0]
    group = rows * 8
    vmem = pl.BlockSpec(memory_space=pltpu.VMEM)
    smem = pl.BlockSpec(memory_space=pltpu.SMEM)
    anywhere = pl.BlockSpec(memory_space=pl.ANY)
    shape = jax.ShapeDtypeStruct
    drains = [
        drain_scratch(GATE_UP_CUTS, ORDERS, HALVES, SHARD, HALF),
        drain_scratch(DOWN_CUTS, ORDERS, HALVES, SHARD, HALF),
        drain_scratch(MIX_CUTS, ORDERS, HALVES, SHARD, HALF),
        drain_scratch(EARLY_CUTS, (ORDERS[2],), HALVES, SHARD, HALF),
    ]
    counts = (rows, mem_rows, rows, rows)
    scratch = [pltpu.VMEM(one.shape, one.dtype) for one in arrays[:8]]
    scratch += [pltpu.VMEM((8, 2 * rows, 128), HALF)] * 3
    scratch += [pltpu.VMEM((8, 2 * mem_rows, 128), HALF), pltpu.VMEM((8, rows, 256), HALF)]
    scratch += [pltpu.VMEM((1024, group), HALF)]
    scratch += [pltpu.VMEM((4, 2, SHARD, 2 * size), HALF) for size in counts]
    scratch += [pltpu.VMEM((4, 2, SHARD, size), HALF) for size in counts + counts]
    scratch += [
        pltpu.VMEM((rows, 1024), HALF),
        pltpu.VMEM((8, rows, 128), HALF),
        pltpu.VMEM((group, 128), HALF),
        pltpu.VMEM((group, 256), HALF),
        pltpu.VMEM((group, 128), HALF),
        pltpu.VMEM((mem_rows * 8, 128), HALF),
        pltpu.SMEM((SEGMENTS, 8), jnp.int32),
        pltpu.VMEM((4, 2, SHARD, 256), FLOAT),
        pltpu.VMEM((4, 2, SHARD, 256), HALF),
        pltpu.VMEM((4, 2, SHARD, 256), HALF),
        pltpu.VMEM((4, SHARD, 256), HALF),
        pltpu.VMEM((4, SHARD, 256), HALF),
        pltpu.VMEM((3, SHARD, 256), HALF),
        pltpu.VMEM((3, SHARD, 256), HALF),
        pltpu.VMEM((2, 4, 2, 16, 128), FLOAT),
        pltpu.VMEM((4, 2, 16, 128), FLOAT),
        pltpu.VMEM((4, 2, 16, 128), FLOAT),
        pltpu.VMEM((4, 16, 128), FLOAT),
        pltpu.VMEM((4, 16, 128), FLOAT),
        pltpu.VMEM((3, 16, 128), FLOAT),
        pltpu.VMEM((3, 16, 128), FLOAT),
        pltpu.VMEM((8, SHARD), FLOAT),
        pltpu.VMEM((8, 8, SHARD), FLOAT),
    ]
    for drain in drains:
        scratch += drain[:-2]
    scratch.append(pltpu.SemaphoreType.DMA((12,)))
    for drain in drains:
        scratch += drain[-2:]
    scratch += [pltpu.SemaphoreType.DMA((18,))] * 2 + trade_sems() * 5
    return pl.pallas_call(
        backward_kernel,
        out_shape=(
            shape((rows, 1024), FLOAT),
            shape((SHARD, 2 * FF_PAD), FLOAT),
            shape((SHARD, FF_PAD), FLOAT),
            shape((SHARD, 256), FLOAT),
            shape((SHARD, 256), FLOAT),
            shape((SHARD, 256), FLOAT),
            shape((16, 128), FLOAT),
            shape((8, SHARD), FLOAT),
            shape((mem_rows, 1024), FLOAT),
        ),
        in_specs=[vmem] * 17 + [smem] * 3 + [anywhere] * 14,
        out_specs=(vmem,) * 8 + (anywhere,),
        scratch_shapes=scratch,
        compiler_params=pltpu.CompilerParams(
            collective_id=1, has_side_effects=True, vmem_limit_bytes=64 * 2**20
        ),
    )(*vectors, *scalars, *arrays)


def finish_kernel(
    mixed_ref, dtok_ref, dmem_ref, gu_ref, down_ref, mix_ref, early_ref, qkv_ref, last_ref, dnorm_ref,
    mixed_out, dtok_out, dmem_out, n1_out, wq_out, wk_out, wv_out, wo_out, rel_out, n2_out,
    cq_out, ck_out, cv_out, co_out, n3_out, wg_out, wu_out, wd_out,
):
    mixed_out[...] = mixed_ref[...]
    dtok_out[...] = dtok_ref[...]
    dmem_out[...] = dmem_ref[...]
    for at, out in enumerate((n1_out, n2_out, n3_out)):
        out[...] = dnorm_ref[at : at + 1, :]
    rel_out[0:1, 0:1] = last_ref[3:4, 0:1]
    rel_out[0:1, 1:2] = last_ref[4:5, 0:1]
    rel_out[1:2, 0:1] = last_ref[5:6, 0:1]
    rel_out[1:2, 1:2] = last_ref[6:7, 0:1]
    wq_out[...] = qkv_ref[:, 0:128]
    wk_out[...] = qkv_ref[:, 128:192]
    wv_out[...] = qkv_ref[:, 192:256]
    wo_out[...] = mix_ref[:, 0:128]
    cq_out[...] = mix_ref[:, 128:256]
    ck_out[...] = early_ref[:, 0:64]
    cv_out[...] = early_ref[:, 64:128]
    co_out[...] = early_ref[:, 128:256]
    width = wg_out.shape[1]
    wg_out[...] = gu_ref[:, 0:width]
    wu_out[...] = gu_ref[:, FF_PAD : FF_PAD + width]
    wd_out[...] = down_ref[:, 0:width]


def finish_outputs(mixed, d_tokens, d_memory, grads, ff_width):
    def shape(*dims):
        return jax.ShapeDtypeStruct(dims, FLOAT)

    outs = (
        jax.ShapeDtypeStruct(mixed.shape, HALF),
        shape(*d_tokens.shape),
        shape(*d_memory.shape),
        shape(1, SHARD), shape(SHARD, 128), shape(SHARD, HDIM), shape(SHARD, HDIM),
        shape(SHARD, 128), shape(2, 2), shape(1, SHARD),
        shape(SHARD, 128), shape(SHARD, HDIM), shape(SHARD, HDIM), shape(SHARD, 128),
        shape(1, SHARD), shape(SHARD, ff_width), shape(SHARD, ff_width),
        shape(SHARD, ff_width),
    )

    vmem = pl.BlockSpec(memory_space=pltpu.VMEM)
    return pl.pallas_call(
        finish_kernel,
        out_shape=outs,
        in_specs=[vmem] * (3 + len(grads)),
        out_specs=(vmem,) * len(outs),
    )(mixed, d_tokens, d_memory, *grads)


def local(
    tokens, memory, cotangent, norm1, w_query, w_key, w_value, w_out, rel_bias, norm2,
    cross_query, cross_key, cross_value, cross_out, norm3, w_gate, w_up, w_down,
    doc_lengths, memory_slot, enc_lengths, rel_bucket,
):
    norms = jnp.stack([norm1, norm2, norm3])
    buckets = rel_bucket.reshape(-1, TILE)
    (
        _, wa, w_qkv, y_ff, h_one, h_two, qkv, kv_two, o_one, o_one_rows, x_one, q_two, o_two,
        o_two_rows, gains, windows, lse_one, lse_two, mixed, g_two, d_out, xt_three, xt_cot,
    ) = forward(
        (
            w_query, w_key, w_value, w_out.T, cross_query, cross_key, cross_value, cross_out.T,
            w_gate, w_up, w_down.T, norms, rel_bias, tokens, memory, buckets, cotangent,
        ),
        (doc_lengths, memory_slot, enc_lengths),
    )
    d_tokens, *grads, d_memory = backward(
        (
            lse_two, g_two, memory, h_two, gains, xt_three, xt_cot, windows, lse_one, buckets,
            w_query, w_key, w_value, cross_query, w_gate, w_up, norms,
        ),
        (doc_lengths, memory_slot, enc_lengths),
        (
            q_two, kv_two, d_out, o_two, x_one, tokens, qkv, o_one,
            h_one, o_one_rows, o_two_rows, wa.reshape(8, 16 * SHARD, 512),
            w_qkv.reshape(8, 16 * SHARD, 256), y_ff,
        ),
    )
    outs = list(finish_outputs(mixed, d_tokens, d_memory, grads, w_gate.shape[1]))
    for at in (3, 9, 14):
        outs[at] = outs[at][0]
    for at in (7, 13, 17):
        outs[at] = outs[at].T
    return tuple(outs)


def solution(mesh):
    return jax.shard_map(
        local,
        mesh=mesh,
        in_specs=(
            P(("tok", "hid"), None),
            P(("tok", "hid"), None),
            P(("tok", "hid"), None),
            P("tok"),
            P("tok", "hid"),
            P("tok", "hid"),
            P("tok", "hid"),
            P("hid", "tok"),
            P("tok", "hid"),
            P("tok"),
            P("tok", "hid"),
            P("tok", "hid"),
            P("tok", "hid"),
            P("hid", "tok"),
            P("tok"),
            P("tok", "hid"),
            P("tok", "hid"),
            P("hid", "tok"),
            P("tok", None),
            P("tok", None),
            P("tok", None),
            P(),
        ),
        out_specs=(
            P(("tok", "hid"), None),
            P(("tok", "hid"), None),
            P(("tok", "hid"), None),
            P("tok"),
            P("tok", "hid"),
            P("tok", "hid"),
            P("tok", "hid"),
            P("hid", "tok"),
            P("tok", "hid"),
            P("tok"),
            P("tok", "hid"),
            P("tok", "hid"),
            P("tok", "hid"),
            P("hid", "tok"),
            P("tok"),
            P("tok", "hid"),
            P("tok", "hid"),
            P("hid", "tok"),
        ),
        check_vma=False,
    )
```
